32 devices in a mesh: dp: 16 (over z, x, core), tensor: 2 (over y).
Axes of the slice: x: 2, y: 2, z: 4, core: 2. Of those that a mesh axis runs over, the one named last changes fastest.
Arguments:
- hidden_in: bfloat16 [32768, 1024], P(('dp', 'tensor')), may hold values from -6 to 6
- lengths: int32 [16, 4], P('dp'), may hold values from 1 to 1536, 2048 in all within a row
- cotangent: bfloat16 [32768, 1024], P(('dp', 'tensor')), may hold values from -6 to 6
- query_weight: bfloat16 [1024, 512], P('dp', 'tensor'), may hold values from -0.1875 to 0.1875
- key_weight: bfloat16 [1024, 512], P('dp', 'tensor'), may hold values from -0.1875 to 0.1875
- value_weight: bfloat16 [1024, 1024], P('dp', 'tensor'), may hold values from -0.1875 to 0.1875
- outgate_weight: bfloat16 [1024, 1024], P('dp', 'tensor'), may hold values from -0.1875 to 0.1875
- output_weight: bfloat16 [1024, 1024], P('tensor', 'dp'), may hold values from -0.375 to 0.375
- gate_weight: bfloat16 [1024, 2816], P('dp', 'tensor'), may hold values from -0.1875 to 0.1875
- up_weight: bfloat16 [1024, 2816], P('dp', 'tensor'), may hold values from -0.1875 to 0.1875
- down_weight: bfloat16 [2816, 1024], P('tensor', 'dp'), may hold values from -0.109375 to 0.109375
- mixer_gain: float32 [1024], replicated, may hold values from 0.5 to 1.5
- feed_gain: float32 [1024], replicated, may hold values from 0.5 to 1.5
- low_first: float32 [1024, 16], replicated, may hold values from -0.1875 to 0.1875
- low_second: float32 [16, 512], replicated, may hold values from -1.5 to 1.5
- decay_bias: float32 [512], replicated, may hold values from 0 to 7
- head_gain: float32 [256], replicated, may hold values from 0.5 to 1.5
Outputs:
- block_out: bfloat16 [32768, 1024], P(('dp', 'tensor'))
- input_grad: bfloat16 [32768, 1024], P(('dp', 'tensor'))
- query_grad: float32 [1024, 512], P('dp', 'tensor')
- key_grad: float32 [1024, 512], P('dp', 'tensor')
- value_grad: float32 [1024, 1024], P('dp', 'tensor')
- outgate_grad: float32 [1024, 1024], P('dp', 'tensor')
- output_grad: float32 [1024, 1024], P('tensor', 'dp')
- gate_grad: float32 [1024, 2816], P('dp', 'tensor')
- up_grad: float32 [1024, 2816], P('dp', 'tensor')
- down_grad: float32 [2816, 1024], P('tensor', 'dp')
- mixer_gain_grad: float32 [1024], replicated
- feed_gain_grad: float32 [1024], replicated
- low_first_grad: float32 [1024, 16], replicated
- low_second_grad: float32 [16, 512], replicated
- decay_bias_grad: float32 [512], replicated
- head_gain_grad: float32 [256], replicated
The draws below stay inside these ranges and needn't reach their ends.
Inputs may be any that keep to these rules, and one draw needn't show every extreme that they name: `lengths`: each row sums to 2048, and its largest entry is exactly 1536.
All inputs are finite; a program needn't handle non-finite values.
Results may differ from the reference program's by a relative error of at most 0.02.
Values may be sent and summed in bfloat16 or wider, within the bound.
No kernel may reach another device: no remote copies, remote signals or barrier semaphores. Data moves between devices by JAX's collectives and lax.ppermute only.
A program may use at most 320 MiB of HBM per device.

```python
import math
import jax
import jax.numpy as jnp
import numpy as np
from jax import lax

D = 1024
HEADS = 4
KEY = 128
VAL = 256
FF = 2816
LOWRANK = 16
SPAN = 64
SEQS = 4
SEQ_TOK = 2048
MOST = 1536
TOKENS = 32768
N_DP = 16


def block_scale(rng, extent, cuts, smallest, largest):
    gain = 1.0
    for position, shards_of in cuts:
        heights = jax.random.uniform(jax.random.fold_in(jax.random.fold_in(rng, 6), position), (shards_of,), jnp.float32, smallest / len(cuts), largest / len(cuts))
        gain = gain * jnp.repeat(jnp.exp(heights), extent[position] // shards_of).reshape((-1,) + (1,) * (len(extent) - 1 - position))
    return gain


def profile(number_of, total, bound, lean):
    weights = [(1 << 20) // math.isqrt(grade ** lean) + 1 for grade in range(2, number_of + 1)]
    surplus, given = total - bound - (number_of - 1), [1] * (number_of - 1)
    while surplus > 0:
        candidates = [i for i in range(number_of - 1) if given[i] < bound]
        whole, remaining = sum([weights[i] for i in candidates]), surplus
        for i in candidates:
            extra = min(bound - given[i], max(1, remaining * weights[i] // whole), surplus)
            given[i] = given[i] + extra
            surplus = surplus - extra
    return np.array([bound] + given)


def ragged(stream_key, count, total, most, slope):
    if count == 2:
        one = jax.random.randint(stream_key, (), max(1, total - most), min(most, total - 1) + 1)
        return jnp.stack([one, total - one])
    sizes = jnp.asarray(profile(count, total, most, slope), jnp.int32)
    twos = (count - 1) // 2
    source_of, sink = sizes[1:1 + 2 * twos:2], sizes[2:2 + 2 * twos:2]
    room = jnp.minimum(source_of - 1, most - sink)
    shifted = jax.random.randint(jax.random.fold_in(stream_key, 1), (twos,), 0, 1 << 20) % (room + 1)
    sizes = sizes.at[1:1 + 2 * twos:2].set(source_of - shifted).at[2:2 + 2 * twos:2].set(sink + shifted)
    return sizes[jax.random.permutation(jax.random.fold_in(stream_key, 2), count)]


def bell_draw(stream_key, dims, scale, reach, shards=(), kind=jnp.bfloat16):
    level = block_scale(stream_key, dims, shards, -0.22, 0.18) if shards else 1.0
    values = jax.random.normal(stream_key, dims, jnp.float32) * scale * level
    return jnp.minimum(jnp.maximum(values, -reach), reach).astype(kind)


def setup_inputs(seed: int = 0) -> dict:
    arg_keys = jax.random.split(jax.random.key(seed), 18)
    hidden_in = bell_draw(arg_keys[0], (TOKENS, D), 1.0, 6.0, ((0, 32),))
    lengths = jax.vmap(lambda own: ragged(own, SEQS, SEQ_TOK, MOST, 2))(jax.random.split(arg_keys[1], N_DP)).reshape((N_DP, SEQS)).astype(jnp.int32)
    cotangent = bell_draw(arg_keys[2], (TOKENS, D), 1.0, 6.0, ((0, 32),))
    query_weight = bell_draw(arg_keys[3], (D, HEADS * KEY), D ** -0.5, 0.1875, ((0, 16), (1, 2)))
    key_weight = bell_draw(arg_keys[4], (D, HEADS * KEY), D ** -0.5, 0.1875, ((0, 16), (1, 2)))
    value_weight = bell_draw(arg_keys[5], (D, HEADS * VAL), D ** -0.5, 0.1875, ((0, 16), (1, 2)))
    outgate_weight = bell_draw(arg_keys[6], (D, HEADS * VAL), D ** -0.5, 0.1875, ((0, 16), (1, 2)))
    output_weight = bell_draw(arg_keys[7], (HEADS * VAL, D), (HEADS * VAL // 4) ** -0.5, 0.375, ((0, 2), (1, 16)))
    gate_weight = bell_draw(arg_keys[8], (D, FF), D ** -0.5, 0.1875, ((0, 16), (1, 2)))
    up_weight = bell_draw(arg_keys[9], (D, FF), D ** -0.5, 0.1875, ((0, 16), (1, 2)))
    down_weight = bell_draw(arg_keys[10], (FF, D), FF ** -0.5, 0.109375, ((0, 2), (1, 16)))
    mixer_gain = jnp.clip(1.0 + 0.1 * jax.random.normal(arg_keys[11], (D,), jnp.float32), 0.5, 1.5)
    feed_gain = jnp.clip(1.0 + 0.1 * jax.random.normal(arg_keys[12], (D,), jnp.float32), 0.5, 1.5)
    low_first = bell_draw(arg_keys[13], (D, LOWRANK), D ** -0.5, 0.1875, (), jnp.float32)
    low_second = bell_draw(arg_keys[14], (LOWRANK, HEADS * KEY), LOWRANK ** -0.5, 1.5, (), jnp.float32)
    decay_bias = jnp.clip(jax.random.uniform(arg_keys[15], (HEADS * KEY,), jnp.float32, 0.0, 7.0), 0.0, 7.0)
    head_gain = jnp.clip(1.0 + 0.1 * jax.random.normal(arg_keys[16], (VAL,), jnp.float32), 0.5, 1.5)
    return {"hidden_in": hidden_in, "lengths": lengths, "cotangent": cotangent, "query_weight": query_weight, "key_weight": key_weight, "value_weight": value_weight, "outgate_weight": outgate_weight, "output_weight": output_weight, "gate_weight": gate_weight, "up_weight": up_weight, "down_weight": down_weight, "mixer_gain": mixer_gain, "feed_gain": feed_gain, "low_first": low_first, "low_second": low_second, "decay_bias": decay_bias, "head_gain": head_gain}


@jax.custom_vjp
def low(v):
    return lax.optimization_barrier(v.astype(jnp.bfloat16)).astype(jnp.float32)

@jax.custom_vjp
def low_back(v):
    return v

def low_keep(v):
    return (low(v), None)

def low_pass(kept, grad):
    return (grad,)

def back_keep(v):
    return (v, None)

def back_low(kept, grad):
    return (low(grad),)
low.defvjp(low_keep, low_pass)
low_back.defvjp(back_keep, back_low)
HIGH_ACCURACY = lax.Precision.HIGHEST

def matmul(left, right):
    return jnp.dot(left, right, precision=HIGH_ACCURACY, preferred_element_type=jnp.float32)

def rms_scale(values, gains, eps):
    return values * lax.rsqrt(lax.optimization_barrier(jnp.mean(values * values, axis=-1, keepdims=True)) + eps) * gains

def segment_ids(lengths_row, total):
    starts = jnp.cumsum(lengths_row) - lengths_row
    places = jnp.arange(total, dtype=jnp.int32)
    return lax.optimization_barrier(jnp.sum((places[:, None] >= starts[None, 1:]).astype(jnp.int32), axis=1)).astype(jnp.int32)

def linear_core(queries, keys, values, decays, segment):
    total = queries.shape[0]
    heads = queries.shape[1] // KEY
    blocks = total // SPAN

    def split(array, width):
        return array.reshape(blocks, SPAN, heads, width).transpose(0, 2, 1, 3)
    lower = jnp.arange(SPAN)[:, None] >= jnp.arange(SPAN)[None, :]

    def advance(carry, item):
        state_matrix, before = carry
        query_block, key_block, block_values, decay_block, seg_block = item
        cumul = jnp.cumsum(decay_block, axis=1)
        final_state = cumul[:, -1:, :]
        query_decayed = query_block * jnp.exp(cumul)
        key_dec = key_block * jnp.exp(-cumul)
        mask = (lower & (seg_block[:, None] == seg_block[None, :])).astype(jnp.float32)
        scores = jnp.einsum('hik,hjk->hij', query_decayed, key_dec, precision=HIGH_ACCURACY) * mask[None]
        running_state = (seg_block == before).astype(jnp.float32)[None, :, None]
        cross_block_term = jnp.einsum('wcb,wba->wca', query_decayed, state_matrix, precision=HIGH_ACCURACY) * running_state
        outputs = cross_block_term + jnp.einsum('hij,hjv->hiv', scores, block_values, precision=HIGH_ACCURACY)
        tail = (seg_block == seg_block[-1]).astype(jnp.float32)[None, :, None]
        key_tail_decay = key_block * jnp.exp(final_state - cumul) * tail
        retain_factor = (seg_block[-1] == before).astype(jnp.float32)
        state_matrix = state_matrix * (jnp.exp(final_state)[:, 0, :, None] * retain_factor) + jnp.einsum('zco,zcr->zor', key_tail_decay, block_values, precision=HIGH_ACCURACY)
        return ((state_matrix, seg_block[-1]), outputs)
    start = (jnp.zeros((heads, KEY, VAL), jnp.float32), jnp.array(-1, dtype=jnp.int32))
    items = (split(queries, KEY), split(keys, KEY), split(values, VAL), split(decays, KEY), segment.reshape(blocks, SPAN))
    unused, outs = lax.scan(advance, start, items)
    return outs.transpose(0, 2, 1, 3).reshape(total, heads * VAL)

def post_gate(core, gains, outgate):
    shaped = core.reshape(core.shape[0], -1, VAL)
    normed = rms_scale(shaped, gains, 1.0).reshape(core.shape)
    return normed * jax.nn.silu(outgate)

def reference(hidden_in, lengths, cotangent, query_weight, key_weight, value_weight, outgate_weight, output_weight, gate_weight, up_weight, down_weight, mixer_gain, feed_gain, low_first, low_second, decay_bias, head_gain):
    segment = jax.vmap(lambda row: segment_ids(row, SEQ_TOK))(lengths)
    scale = KEY ** (-0.5)

    def run_core(item):
        return linear_core(item[0], item[1], item[2], item[3], item[4])

    def forward(resid, w_query, w_key, w_value, w_outgate, w_output, w_gate, w_up, w_down, gain_one, gain_two, first_low, second_low, bias_decay, gain_head):
        normed_a = low(rms_scale(resid, gain_one, 1e-06))
        queries = low_back(low(matmul(normed_a, w_query) * scale))
        keys = low_back(low(matmul(normed_a, w_key)))
        values = low_back(low(matmul(normed_a, w_value)))
        outgate = low_back(matmul(normed_a, w_outgate))
        decays = jax.nn.log_sigmoid(matmul(matmul(normed_a, first_low), second_low) + bias_decay) / 16.0

        def shaped(array):
            return array.reshape(N_DP, SEQ_TOK, array.shape[-1])
        core = lax.map(jax.checkpoint(run_core), (shaped(queries), shaped(keys), shaped(values), shaped(decays), segment))
        core = core.reshape(TOKENS, HEADS * VAL)
        mixed_in = low(post_gate(core, gain_head, outgate))
        middle = resid + low_back(matmul(mixed_in, w_output))
        normed_b = low(rms_scale(middle, gain_two, 1e-06))
        gate_pre = low_back(matmul(normed_b, w_gate))
        up_pre = low_back(matmul(normed_b, w_up))
        activ = low(jax.nn.silu(gate_pre) * up_pre)
        return middle + low_back(matmul(activ, w_down))
    floats = (hidden_in.astype(jnp.float32), query_weight.astype(jnp.float32), key_weight.astype(jnp.float32), value_weight.astype(jnp.float32), outgate_weight.astype(jnp.float32), output_weight.astype(jnp.float32), gate_weight.astype(jnp.float32), up_weight.astype(jnp.float32), down_weight.astype(jnp.float32), mixer_gain, feed_gain, low_first, low_second, decay_bias, head_gain)
    result, pull = jax.vjp(forward, *floats)
    grads = pull(cotangent.astype(jnp.float32))
    return (result.astype(jnp.bfloat16), grads[0].astype(jnp.bfloat16), grads[1], grads[2], grads[3], grads[4], grads[5], grads[6], grads[7], grads[8], grads[9], grads[10], grads[11], grads[12], grads[13], grads[14])
```

```python
import jax
import jax.numpy as jnp
from jax import lax
from jax.experimental import pallas as pl
from jax.experimental.pallas import tpu as pltpu
from jax.sharding import PartitionSpec as P

HEADS = 4
KEY = 128
VAL = 256
CHUNK = 128
SCALE = KEY ** (-0.5)
F32 = jnp.float32
BF16 = jnp.bfloat16
HIGHEST = lax.Precision.HIGHEST
ALL = ("tensor", "dp")
VMEM_BYTES = 48 * 1024 * 1024


def nn(a, b):
    return lax.dot_general(a, b, (((1,), (0,)), ((), ())), preferred_element_type=F32)


def nt(a, b):
    return lax.dot_general(a, b, (((1,), (1,)), ((), ())), preferred_element_type=F32)


def tn(a, b):
    return lax.dot_general(a, b, (((0,), (0,)), ((), ())), preferred_element_type=F32)


def triangle(lower):
    rows = lax.broadcasted_iota(jnp.int32, (CHUNK, CHUNK), 0)
    cols = lax.broadcasted_iota(jnp.int32, (CHUNK, CHUNK), 1)
    return rows >= cols if lower else rows <= cols


def split_sum(tri, x, terms):
    total = None
    for _ in range(terms):
        part = x.astype(BF16)
        x = x - part.astype(F32)
        term = nn(tri, part)
        total = term if total is None else total + term
    return total


def head_cols(h, width):
    return h // 2, slice((h % 2) * width, (h % 2 + 1) * width)


def gate_kernel(info, low_ref, second_ref, bias_ref, k_ref, v_ref, seg_ref, cum_ref, sig_ref, state_ref):
    c = pl.program_id(0)

    @pl.when(c == 0)
    def _():
        state_ref[...] = jnp.zeros_like(state_ref)

    logit = (
        jnp.dot(low_ref[...], second_ref[...], precision=HIGHEST, preferred_element_type=F32)
        + bias_ref[...]
    )
    e = jnp.exp(-jnp.abs(logit))
    decays = (jnp.minimum(logit, 0.0) - jnp.log1p(e)) * (1.0 / 16.0)
    sig_ref[...] = (jnp.where(logit >= 0, e, 1.0) / (1.0 + e)).astype(BF16)
    tri = triangle(True).astype(F32).astype(BF16)
    cum = split_sum(tri, decays, 3)
    cum_ref[...] = cum
    final = cum[CHUNK - 1 :, :]
    tail = (seg_ref[...] == info[1, c]).astype(F32)
    retain = (info[1, c] == info[0, c]).astype(F32)
    tail_decay = jnp.exp(final - cum) * tail
    keep = jnp.exp(final) * retain
    for h in range(HEADS):
        p, kc = head_cols(h, KEY)
        _, vc = head_cols(h, VAL)
        hk = slice(h * KEY, (h + 1) * KEY)
        kt = (k_ref[p, :, kc].astype(F32) * tail_decay[:, hk]).astype(BF16)
        state_ref[h] = state_ref[h] * keep[:, hk].reshape(KEY, 1) + tn(kt, v_ref[p, :, vc])


def core_kernel(
    info, q_ref, k_ref, v_ref, og_ref, cum_ref, seg_ref, row_ref, first_ref, gain_ref,
    mixed_ref, core_ref, states_ref, state,
):
    c = pl.program_id(0)

    @pl.when(c == 0)
    def _():
        state[...] = first_ref[...].astype(F32)

    before, last = info[0, c], info[1, c]
    seg = seg_ref[...]
    mask = triangle(True) & (seg == row_ref[0])
    running = (seg == before).astype(F32)
    tail = (seg == last).astype(F32)
    retain = (last == before).astype(F32)
    cum = cum_ref[...]
    final = cum[CHUNK - 1 :, :]
    mid = cum[CHUNK // 2 - 1 : CHUNK // 2, :]
    up, down = jnp.exp(cum - mid), jnp.exp(mid - cum)
    whole = jnp.exp(cum) * running
    rest = jnp.exp(final - cum) * tail
    keep = jnp.exp(final) * retain
    for h in range(HEADS):
        p, kc = head_cols(h, KEY)
        _, vc = head_cols(h, VAL)
        hk = slice(h * KEY, (h + 1) * KEY)
        q = q_ref[p, :, kc].astype(F32) * SCALE
        k = k_ref[p, :, kc].astype(F32)
        v = v_ref[p, :, vc]
        s = state[h]
        s_low = s.astype(BF16)
        states_ref[0, h] = s_low
        scores = nt((q * up[:, hk]).astype(BF16), (k * down[:, hk]).astype(BF16))
        scores = jnp.where(mask, scores, 0.0).astype(BF16)
        core = nn((q * whole[:, hk]).astype(BF16), s_low) + nn(scores, v)
        state[h] = s * keep[:, hk].reshape(KEY, 1) + tn((k * rest[:, hk]).astype(BF16), v)
        normed = core * lax.rsqrt(jnp.mean(core * core, axis=-1, keepdims=True) + 1.0)
        og = og_ref[p, :, vc].astype(F32)
        hv = slice(h * VAL, (h + 1) * VAL)
        mixed_ref[:, hv] = (normed * gain_ref[...] * (og * jax.nn.sigmoid(og))).astype(BF16)
        core_ref[:, hv] = core.astype(BF16)


def post_kernel(
    info, dm_ref, core_ref, og_ref, q_ref, cum_ref, seg_ref, gain_ref,
    dcore_ref, dog_ref, dgain_ref, dstate_ref, prefix,
):
    c = pl.program_id(0)

    @pl.when(c == 0)
    def _():
        prefix[...] = jnp.zeros_like(prefix)
        dgain_ref[...] = jnp.zeros_like(dgain_ref)
        dstate_ref[...] = jnp.zeros_like(dstate_ref)

    running = (seg_ref[...] == info[0, 0]).astype(F32)
    cum = cum_ref[...]
    decay = jnp.exp(cum + prefix[...]) * running * SCALE
    prefix[...] += cum[CHUNK - 1 :, :]
    gain = gain_ref[...]
    total = jnp.zeros((1, VAL), F32)
    for h in range(HEADS):
        p, kc = head_cols(h, KEY)
        _, vc = head_cols(h, VAL)
        hk = slice(h * KEY, (h + 1) * KEY)
        hv = slice(h * VAL, (h + 1) * VAL)
        core = core_ref[:, hv].astype(F32)
        scale = lax.rsqrt(jnp.mean(core * core, axis=-1, keepdims=True) + 1.0)
        normed = core * scale
        og = og_ref[p, :, vc].astype(F32)
        sig = jax.nn.sigmoid(og)
        silu = og * sig
        dm = dm_ref[:, hv].astype(F32)
        both = dm * normed
        total += jnp.sum(both * silu, axis=0, keepdims=True)
        dog_ref[p, :, vc] = (both * gain * (sig * (1.0 + og * (1.0 - sig)))).astype(BF16)
        dn = dm * gain * silu
        dcore = scale * (dn - normed * jnp.mean(dn * normed, axis=-1, keepdims=True))
        dcore = dcore.astype(BF16)
        dcore_ref[:, hv] = dcore
        qa = (q_ref[p, :, kc].astype(F32) * decay[:, hk]).astype(BF16)
        dstate_ref[h] += tn(qa, dcore)
    dgain_ref[...] += total


def back_kernel(
    info, q_ref, k_ref, v_ref, cum_ref, sig_ref, states_ref, dcore_ref, seg_ref, row_ref,
    first_ref, second_ref, low_ref, dqkv_ref, drank_ref, dsecond_ref, dbias_ref, dstate,
):
    i = pl.program_id(0)
    c = pl.num_programs(0) - 1 - i

    @pl.when(i == 0)
    def _():
        dstate[...] = first_ref[...].astype(F32)
        dsecond_ref[...] = jnp.zeros_like(dsecond_ref)
        dbias_ref[...] = jnp.zeros_like(dbias_ref)

    before, last = info[0, c], info[1, c]
    seg = seg_ref[...]
    mask = triangle(True) & (seg == row_ref[0])
    upper = triangle(False).astype(F32).astype(BF16)
    running = (seg == before).astype(F32)
    tail = (seg == last).astype(F32)
    retain = (last == before).astype(F32)
    cum = cum_ref[...]
    final = cum[CHUNK - 1 :, :]
    mid = cum[CHUNK // 2 - 1 : CHUNK // 2, :]
    up, down = jnp.exp(cum - mid), jnp.exp(mid - cum)
    whole = jnp.exp(cum) * running
    rest = jnp.exp(final - cum) * tail
    keep = jnp.exp(final) * retain
    logits = []
    for h in range(HEADS):
        p, kc = head_cols(h, KEY)
        _, vc = head_cols(h, VAL)
        hk = slice(h * KEY, (h + 1) * KEY)
        hv = slice(h * VAL, (h + 1) * VAL)
        q = q_ref[p, :, kc].astype(F32) * SCALE
        k = k_ref[p, :, kc].astype(F32)
        v = v_ref[p, :, vc]
        do = dcore_ref[:, hv]
        s = states_ref[0, h]
        ds = dstate[h]
        ds_low = ds.astype(BF16)
        q_up = (q * up[:, hk]).astype(BF16)
        k_down = (k * down[:, hk]).astype(BF16)
        q_whole = (q * whole[:, hk]).astype(BF16)
        k_rest = (k * rest[:, hk]).astype(BF16)
        scores = jnp.where(mask, nt(q_up, k_down), 0.0).astype(BF16)
        dscores = jnp.where(mask, nt(do, v), 0.0).astype(BF16)
        dq_up = nn(dscores, k_down)
        dk_down = tn(dscores, q_up)
        dq_whole = nt(do, s)
        dk_rest = nt(v, ds_low)
        dv = tn(scores, do) + nn(k_rest, ds_low)
        dq = dq_up * up[:, hk] + dq_whole * whole[:, hk]
        dk = dk_down * down[:, hk] + dk_rest * rest[:, hk]
        from_rest = k_rest.astype(F32) * dk_rest
        dcum = (
            q_up.astype(F32) * dq_up
            - k_down.astype(F32) * dk_down
            + q_whole.astype(F32) * dq_whole
            - from_rest
        )
        kept = keep[:, hk].reshape(KEY, 1)
        through = jnp.sum(s.astype(F32) * ds, axis=1, keepdims=True) * kept
        dfinal = through.reshape(1, KEY) + jnp.sum(from_rest, axis=0, keepdims=True)
        ddecay = split_sum(upper, dcum, 2) + dfinal
        dstate[h] = ds * kept + tn(q_whole, do)
        logits.append(ddecay * (sig_ref[:, hk].astype(F32) * (1.0 / 16.0)))
        dqkv_ref[p, :, kc] = (dq * SCALE).astype(BF16)
        dqkv_ref[p, :, slice(256 + kc.start, 256 + kc.stop)] = dk.astype(BF16)
        dqkv_ref[p, :, slice(512 + vc.start, 512 + vc.stop)] = dv.astype(BF16)
    dlogit = jnp.concatenate(logits, axis=1)
    dbias_ref[...] += jnp.sum(dlogit, axis=0, keepdims=True)
    low = dlogit.astype(BF16)
    dsecond_ref[...] += tn(low_ref[...].astype(BF16), low)
    drank_ref[...] = nt(low, second_ref[...].astype(BF16))


def shape(dims, dtype):
    return jax.ShapeDtypeStruct(dims, dtype)


def call(kernel, blocks, in_specs, out_specs, out_shape, scratch, cost):
    return pl.pallas_call(
        kernel,
        grid_spec=pltpu.PrefetchScalarGridSpec(
            num_scalar_prefetch=1,
            grid=(blocks,),
            in_specs=in_specs,
            out_specs=out_specs,
            scratch_shapes=scratch,
        ),
        out_shape=out_shape,
        compiler_params=pltpu.CompilerParams(
            dimension_semantics=("arbitrary",), vmem_limit_bytes=VMEM_BYTES
        ),
        cost_estimate=pl.CostEstimate(flops=cost, bytes_accessed=16 << 20, transcendentals=1 << 20),
    )


def specs(blocks, backward=False):
    def at(c):
        return blocks - 1 - c if backward else c

    def proj(width, place):
        return pl.BlockSpec((2, CHUNK, width), lambda c, _: (0, at(c), place))

    def rows(width):
        return pl.BlockSpec((CHUNK, width), lambda c, _: (at(c), 0))

    def full(*dims):
        return pl.BlockSpec(dims, lambda c, _: (0,) * len(dims))

    row = pl.BlockSpec((1, 1, CHUNK), lambda c, _: (at(c), 0, 0))
    states = pl.BlockSpec((1, HEADS, KEY, VAL), lambda c, _: (at(c), 0, 0, 0))
    return proj, rows, full, row, states


def rms(x, eps):
    return x * lax.rsqrt(jnp.mean(x * x, axis=-1, keepdims=True) + eps)


def rms_back(x, gain, eps, grad):
    scale = lax.rsqrt(jnp.mean(x * x, axis=-1, keepdims=True) + eps)
    normed = x * scale
    dn = grad * gain
    back = scale * (dn - normed * jnp.mean(dn * normed, axis=-1, keepdims=True))
    return back, jnp.sum(grad * normed, axis=0)


def gather(shard):
    return lax.all_gather(shard, ALL, axis=0, tiled=True).reshape(2, -1, shard.shape[1])


def scatter(grad):
    flat = grad.reshape(-1, grad.shape[-1])
    return lax.psum_scatter(flat, ALL, scatter_dimension=0, tiled=True).astype(F32)


def total_sum(x):
    x = x + lax.ppermute(x, "tensor", [(0, 1), (1, 0)])
    n = lax.axis_size("dp")
    stride = 1
    while stride < n:
        x = x + lax.ppermute(x, "dp", [(i, i ^ stride) for i in range(n)])
        stride *= 2
    return x


def local(
    hidden_in, lengths, cotangent, query_weight, key_weight, value_weight, outgate_weight,
    output_weight, gate_weight, up_weight, down_weight, mixer_gain, feed_gain, low_first,
    low_second, decay_bias, head_gain,
):
    rows, width = hidden_in.shape
    blocks = rows // CHUNK
    place = lax.axis_index("tensor")
    half = gate_weight.shape[1]

    starts = jnp.cumsum(lengths[0]) - lengths[0]
    spots = place * rows + jnp.arange(-1, rows, dtype=jnp.int32)
    segments = jnp.sum((spots[:, None] >= starts[None, 1:]).astype(jnp.int32), axis=1)
    segments = jnp.where(spots < 0, -1, segments)
    seg = segments[1:].reshape(rows, 1)
    seg_row = segments[1:].reshape(blocks, 1, CHUNK)
    info = jnp.stack([segments[:-1].reshape(blocks, CHUNK)[:, 0], seg_row[:, 0, -1]])

    w_in = gather(jnp.concatenate([query_weight, key_weight, value_weight, outgate_weight], axis=1))
    w_out = gather(output_weight.T)
    w_gu = gather(jnp.concatenate([gate_weight, up_weight], axis=1))
    w_down = gather(down_weight.T)

    resid = hidden_in.astype(F32)
    normed_a = (rms(resid, 1e-6) * mixer_gain).astype(BF16)
    proj = jnp.einsum("td,pdc->ptc", normed_a, w_in, preferred_element_type=F32).astype(BF16)
    lowrank = jnp.dot(normed_a.astype(F32), low_first, precision=HIGHEST)
    gain = head_gain.reshape(1, VAL)
    p_spec, r_spec, f_spec, row_spec, s_spec = specs(blocks)
    state_f32 = shape((HEADS, KEY, VAL), F32)
    cum, sig, final_state = call(
        gate_kernel,
        blocks,
        [r_spec(16), f_spec(16, 512), f_spec(1, 512), p_spec(256, 1), p_spec(512, 1), r_spec(1)],
        [r_spec(512), r_spec(512), f_spec(HEADS, KEY, VAL)],
        [shape((rows, 512), F32), shape((rows, 512), BF16), state_f32],
        [],
        1 << 29,
    )(info, lowrank, low_second, decay_bias.reshape(1, 512), proj, proj, seg)
    state_in = lax.ppermute(final_state.astype(BF16), "tensor", [(0, 1)])
    mixed, core, states = call(
        core_kernel,
        blocks,
        [p_spec(256, 0), p_spec(256, 1), p_spec(512, 1), p_spec(512, 2), r_spec(512), r_spec(1),
         row_spec, f_spec(HEADS, KEY, VAL), f_spec(1, VAL)],
        [r_spec(1024), r_spec(1024), s_spec],
        [shape((rows, 1024), BF16), shape((rows, 1024), BF16),
         shape((blocks, HEADS, KEY, VAL), BF16)],
        [pltpu.VMEM((HEADS, KEY, VAL), F32)],
        1 << 30,
    )(info, proj, proj, proj, proj, cum, seg, seg_row, state_in, gain)
    middle = resid + nt(mixed[:, :512], w_out[0]) + nt(mixed[:, 512:], w_out[1])

    normed_b = (rms(middle, 1e-6) * feed_gain).astype(BF16)
    pre = jnp.einsum("td,pdc->ptc", normed_b, w_gu, preferred_element_type=F32).astype(BF16)
    gate_pre, up_pre = pre[..., :half].astype(F32), pre[..., half:].astype(F32)
    sig_gate = jax.nn.sigmoid(gate_pre)
    silu = gate_pre * sig_gate
    activ = (silu * up_pre).astype(BF16)
    feed_out = nt(activ[0], w_down[0]) + nt(activ[1], w_down[1])
    block_out = (middle + feed_out).astype(BF16)

    down_grad = jnp.einsum("to,ptc->poc", cotangent, activ, preferred_element_type=F32).astype(BF16)
    own_down = scatter(down_grad)
    d_activ = jnp.einsum("to,poc->ptc", cotangent, w_down, preferred_element_type=F32)
    d_gate = (d_activ * up_pre * (sig_gate * (1.0 + gate_pre * (1.0 - sig_gate)))).astype(BF16)
    d_up = (d_activ * silu).astype(BF16)
    d_pre = jnp.concatenate([d_gate, d_up], axis=-1)
    gu_grad = jnp.einsum("td,ptc->pdc", normed_b, d_pre, preferred_element_type=F32).astype(BF16)
    own_gu = scatter(gu_grad)
    d_normed_b = nt(d_pre[0], w_gu[0]) + nt(d_pre[1], w_gu[1])
    back, feed_gain_grad = rms_back(middle, feed_gain, 1e-6, d_normed_b)
    d_middle = cotangent.astype(F32) + back
    d_mix = d_middle.astype(BF16)

    out_grad = jnp.einsum(
        "to,tpc->poc", d_mix, mixed.reshape(rows, 2, 512), preferred_element_type=F32
    ).astype(BF16)
    d_mixed = jnp.concatenate([nn(d_mix, w_out[0]), nn(d_mix, w_out[1])], axis=1).astype(BF16)
    d_core, d_og, head_gain_grad, d_state = call(
        post_kernel,
        blocks,
        [r_spec(1024), r_spec(1024), p_spec(512, 2), p_spec(256, 0), r_spec(512), r_spec(1),
         f_spec(1, VAL)],
        [r_spec(1024), p_spec(512, 0), f_spec(1, VAL), f_spec(HEADS, KEY, VAL)],
        [shape((rows, 1024), BF16), shape((2, rows, 512), BF16), shape((1, VAL), F32), state_f32],
        [pltpu.VMEM((1, 512), F32)],
        1 << 29,
    )(info, d_mixed, core, proj, proj, cum, seg, gain)
    d_state_in = lax.ppermute(d_state.astype(BF16), "tensor", [(1, 0)])
    p_spec, r_spec, f_spec, row_spec, s_spec = specs(blocks, True)
    d_qkv, d_rank, low_second_grad, bias_grad = call(
        back_kernel,
        blocks,
        [p_spec(256, 0), p_spec(256, 1), p_spec(512, 1), r_spec(512), r_spec(512), s_spec,
         r_spec(1024), r_spec(1), row_spec, f_spec(HEADS, KEY, VAL), f_spec(16, 512), r_spec(16)],
        [p_spec(1024, 0), r_spec(16), f_spec(16, 512), f_spec(1, 512)],
        [shape((2, rows, 1024), BF16), shape((rows, 16), F32), shape((16, 512), F32),
         shape((1, 512), F32)],
        [pltpu.VMEM((HEADS, KEY, VAL), F32)],
        3 << 30,
    )(info, proj, proj, proj, cum, sig, states, d_core, seg, seg_row, d_state_in, low_second, lowrank)
    d_proj = jnp.concatenate([d_qkv, d_og], axis=-1)
    in_grad = jnp.einsum("td,ptc->pdc", normed_a, d_proj, preferred_element_type=F32).astype(BF16)
    own_mix = scatter(jnp.concatenate([in_grad, out_grad], axis=-1))
    low_first_grad = tn(normed_a, d_rank.astype(BF16))
    d_normed_a = (
        nt(d_proj[0], w_in[0])
        + nt(d_proj[1], w_in[1])
        + nt(d_rank.astype(BF16), low_first.astype(BF16))
    )
    back, mixer_gain_grad = rms_back(resid, mixer_gain, 1e-6, d_normed_a)
    input_grad = (d_middle + back).astype(BF16)

    parts = (mixer_gain_grad, feed_gain_grad, low_first_grad, low_second_grad, bias_grad, head_gain_grad)
    flat = total_sum(jnp.concatenate([part.reshape(-1, 128) for part in parts]))
    small, spot = [], 0
    for part, dims in zip(
        parts, ((width,), (width,), low_first.shape, low_second.shape, (512,), (VAL,))
    ):
        size = part.size // 128
        small.append(flat[spot : spot + size].reshape(dims))
        spot += size
    return (
        block_out,
        input_grad,
        own_mix[:, :256],
        own_mix[:, 256:512],
        own_mix[:, 512:1024],
        own_mix[:, 1024:1536],
        own_mix[:, 1536:].T,
        own_gu[:, :half],
        own_gu[:, half:],
        own_down.T,
        *small,
    )


def solution(mesh):
    tokens = P(("dp", "tensor"), None)
    split_in = P("dp", "tensor")
    split_out = P("tensor", "dp")
    weights = (split_in,) * 4 + (split_out,) + (split_in,) * 2 + (split_out,)
    in_specs = (tokens, P("dp", None), tokens) + weights + (P(),) * 6
    out_specs = (tokens, tokens) + weights + (P(),) * 6
    return jax.shard_map(local, mesh=mesh, in_specs=in_specs, out_specs=out_specs, check_vma=False)
```

```python
import jax
import jax.numpy as jnp
from jax import lax
from jax.experimental import pallas as pl
from jax.experimental.pallas import tpu as pltpu
from jax.sharding import PartitionSpec as P

HEADS = 4
KEY = 128
VAL = 256
CHUNK = 128
SCALE = KEY ** (-0.5)
F32 = jnp.float32
BF16 = jnp.bfloat16
HIGHEST = lax.Precision.HIGHEST
ALL = ("tensor", "dp")
VMEM_BYTES = 48 * 1024 * 1024


def nn(a, b):
    return lax.dot_general(a, b, (((1,), (0,)), ((), ())), preferred_element_type=F32)


def nt(a, b):
    return lax.dot_general(a, b, (((1,), (1,)), ((), ())), preferred_element_type=F32)


def tn(a, b):
    return lax.dot_general(a, b, (((0,), (0,)), ((), ())), preferred_element_type=F32)


def triangle(lower):
    rows = lax.broadcasted_iota(jnp.int32, (CHUNK, CHUNK), 0)
    cols = lax.broadcasted_iota(jnp.int32, (CHUNK, CHUNK), 1)
    return rows >= cols if lower else rows <= cols


def split_sum(tri, x, terms):
    total = None
    for _ in range(terms):
        part = x.astype(BF16)
        x = x - part.astype(F32)
        term = nn(tri, part)
        total = term if total is None else total + term
    return total


def head_cols(h, width):
    return h // 2, slice((h % 2) * width, (h % 2 + 1) * width)


def head_pick(h, first, second):
    return (first if h % 2 == 0 else second)[h // 2]


def gate_kernel(info, low_ref, second_ref, bias_ref, k_ref, v0_ref, v1_ref, seg_ref, cum_ref, sig_ref, state_ref):
    c = pl.program_id(0)

    @pl.when(c == 0)
    def _():
        state_ref[...] = jnp.zeros_like(state_ref)

    logit = (
        jnp.dot(low_ref[...], second_ref[...], precision=HIGHEST, preferred_element_type=F32)
        + bias_ref[...]
    )
    e = jnp.exp(-jnp.abs(logit))
    decays = (jnp.minimum(logit, 0.0) - jnp.log1p(e)) * (1.0 / 16.0)
    sig_ref[...] = (jnp.where(logit >= 0, e, 1.0) / (1.0 + e)).astype(BF16)
    tri = triangle(True).astype(F32).astype(BF16)
    cum = split_sum(tri, decays, 3)
    cum_ref[...] = cum
    final = cum[CHUNK - 1 :, :]
    tail = (seg_ref[...] == info[1, c]).astype(F32)
    retain = (info[1, c] == info[0, c]).astype(F32)
    tail_decay = jnp.exp(final - cum) * tail
    keep = jnp.exp(final) * retain
    for h in range(HEADS):
        p, kc = head_cols(h, KEY)
        hk = slice(h * KEY, (h + 1) * KEY)
        kt = (k_ref[p, :, kc].astype(F32) * tail_decay[:, hk]).astype(BF16)
        state_ref[h] = state_ref[h] * keep[:, hk].reshape(KEY, 1) + tn(kt, head_pick(h, v0_ref, v1_ref))


def core_kernel(
    info, q_ref, k_ref, v0_ref, v1_ref, og0_ref, og1_ref, cum_ref, seg_ref, row_ref, first_ref, gain_ref,
    mixed_ref, core_ref, states_ref, state,
):
    c = pl.program_id(0)

    @pl.when(c == 0)
    def _():
        state[...] = first_ref[...].astype(F32)

    before, last = info[0, c], info[1, c]
    seg = seg_ref[...]
    mask = triangle(True) & (seg == row_ref[0])
    running = (seg == before).astype(F32)
    tail = (seg == last).astype(F32)
    retain = (last == before).astype(F32)
    cum = cum_ref[...]
    final = cum[CHUNK - 1 :, :]
    mid = cum[CHUNK // 2 - 1 : CHUNK // 2, :]
    up, down = jnp.exp(cum - mid), jnp.exp(mid - cum)
    whole = jnp.exp(cum) * running
    rest = jnp.exp(final - cum) * tail
    keep = jnp.exp(final) * retain
    for h in range(HEADS):
        p, kc = head_cols(h, KEY)
        hk = slice(h * KEY, (h + 1) * KEY)
        q = q_ref[p, :, kc].astype(F32) * SCALE
        k = k_ref[p, :, kc].astype(F32)
        v = head_pick(h, v0_ref, v1_ref)
        s = state[h]
        s_low = s.astype(BF16)
        states_ref[0, h] = s_low
        scores = nt((q * up[:, hk]).astype(BF16), (k * down[:, hk]).astype(BF16))
        scores = jnp.where(mask, scores, 0.0).astype(BF16)
        core = nn((q * whole[:, hk]).astype(BF16), s_low) + nn(scores, v)
        state[h] = s * keep[:, hk].reshape(KEY, 1) + tn((k * rest[:, hk]).astype(BF16), v)
        normed = core * lax.rsqrt(jnp.mean(core * core, axis=-1, keepdims=True) + 1.0)
        og = head_pick(h, og0_ref, og1_ref).astype(F32)
        hv = slice(h * VAL, (h + 1) * VAL)
        mixed_ref[:, hv] = (normed * gain_ref[...] * (og * jax.nn.sigmoid(og))).astype(BF16)
        core_ref[:, hv] = core.astype(BF16)


def post_kernel(
    info, dm_ref, core_ref, og0_ref, og1_ref, q_ref, cum_ref, seg_ref, gain_ref,
    dcore_ref, dog_ref, dgain_ref, dstate_ref, prefix,
):
    c = pl.program_id(0)

    @pl.when(c == 0)
    def _():
        prefix[...] = jnp.zeros_like(prefix)
        dgain_ref[...] = jnp.zeros_like(dgain_ref)
        dstate_ref[...] = jnp.zeros_like(dstate_ref)

    running = (seg_ref[...] == info[0, 0]).astype(F32)
    cum = cum_ref[...]
    decay = jnp.exp(cum + prefix[...]) * running * SCALE
    prefix[...] += cum[CHUNK - 1 :, :]
    gain = gain_ref[...]
    total = jnp.zeros((1, VAL), F32)
    for h in range(HEADS):
        p, kc = head_cols(h, KEY)
        hk = slice(h * KEY, (h + 1) * KEY)
        hv = slice(h * VAL, (h + 1) * VAL)
        core = core_ref[:, hv].astype(F32)
        scale = lax.rsqrt(jnp.mean(core * core, axis=-1, keepdims=True) + 1.0)
        normed = core * scale
        og = head_pick(h, og0_ref, og1_ref).astype(F32)
        sig = jax.nn.sigmoid(og)
        silu = og * sig
        dm = dm_ref[:, hv].astype(F32)
        both = dm * normed
        total += jnp.sum(both * silu, axis=0, keepdims=True)
        dog_ref[p, :, head_cols(h, VAL)[1]] = (both * gain * (sig * (1.0 + og * (1.0 - sig)))).astype(BF16)
        dn = dm * gain * silu
        dcore = scale * (dn - normed * jnp.mean(dn * normed, axis=-1, keepdims=True))
        dcore = dcore.astype(BF16)
        dcore_ref[:, hv] = dcore
        qa = (q_ref[p, :, kc].astype(F32) * decay[:, hk]).astype(BF16)
        dstate_ref[h] += tn(qa, dcore)
    dgain_ref[...] += total


def back_kernel(
    info, q_ref, k_ref, v0_ref, v1_ref, dog_ref, cum_ref, sig_ref, states_ref, dcore_ref, seg_ref, row_ref,
    first_ref, second_ref, low_ref, da_ref, db_ref, drank_ref, dsecond_ref, dbias_ref, dstate,
):
    i = pl.program_id(0)
    c = pl.num_programs(0) - 1 - i

    @pl.when(i == 0)
    def _():
        dstate[...] = first_ref[...].astype(F32)
        dsecond_ref[...] = jnp.zeros_like(dsecond_ref)
        dbias_ref[...] = jnp.zeros_like(dbias_ref)

    before, last = info[0, c], info[1, c]
    seg = seg_ref[...]
    mask = triangle(True) & (seg == row_ref[0])
    upper = triangle(False).astype(F32).astype(BF16)
    running = (seg == before).astype(F32)
    tail = (seg == last).astype(F32)
    retain = (last == before).astype(F32)
    cum = cum_ref[...]
    final = cum[CHUNK - 1 :, :]
    mid = cum[CHUNK // 2 - 1 : CHUNK // 2, :]
    up, down = jnp.exp(cum - mid), jnp.exp(mid - cum)
    whole = jnp.exp(cum) * running
    rest = jnp.exp(final - cum) * tail
    keep = jnp.exp(final) * retain
    logits = []
    for h in range(HEADS):
        p, kc = head_cols(h, KEY)
        hk = slice(h * KEY, (h + 1) * KEY)
        hv = slice(h * VAL, (h + 1) * VAL)
        q = q_ref[p, :, kc].astype(F32) * SCALE
        k = k_ref[p, :, kc].astype(F32)
        v = head_pick(h, v0_ref, v1_ref)
        do = dcore_ref[:, hv]
        s = states_ref[0, h]
        ds = dstate[h]
        ds_low = ds.astype(BF16)
        q_up = (q * up[:, hk]).astype(BF16)
        k_down = (k * down[:, hk]).astype(BF16)
        q_whole = (q * whole[:, hk]).astype(BF16)
        k_rest = (k * rest[:, hk]).astype(BF16)
        scores = jnp.where(mask, nt(q_up, k_down), 0.0).astype(BF16)
        dscores = jnp.where(mask, nt(do, v), 0.0).astype(BF16)
        dq_up = nn(dscores, k_down)
        dk_down = tn(dscores, q_up)
        dq_whole = nt(do, s)
        dk_rest = nt(v, ds_low)
        dv = tn(scores, do) + nn(k_rest, ds_low)
        dq = dq_up * up[:, hk] + dq_whole * whole[:, hk]
        dk = dk_down * down[:, hk] + dk_rest * rest[:, hk]
        from_rest = k_rest.astype(F32) * dk_rest
        dcum = (
            q_up.astype(F32) * dq_up
            - k_down.astype(F32) * dk_down
            + q_whole.astype(F32) * dq_whole
            - from_rest
        )
        kept = keep[:, hk].reshape(KEY, 1)
        through = jnp.sum(s.astype(F32) * ds, axis=1, keepdims=True) * kept
        dfinal = through.reshape(1, KEY) + jnp.sum(from_rest, axis=0, keepdims=True)
        ddecay = split_sum(upper, dcum, 2) + dfinal
        dstate[h] = ds * kept + tn(q_whole, do)
        logits.append(ddecay * (sig_ref[:, hk].astype(F32) * (1.0 / 16.0)))
        da_ref[p, :, kc] = (dq * SCALE).astype(BF16)
        da_ref[p, :, slice(256 + kc.start, 256 + kc.stop)] = dk.astype(BF16)
        if h % 2 == 0:
            da_ref[p, :, 512:] = dv.astype(BF16)
        else:
            db_ref[p, :, :256] = dv.astype(BF16)
    db_ref[:, :, 256:] = dog_ref[...]
    dlogit = jnp.concatenate(logits, axis=1)
    dbias_ref[...] += jnp.sum(dlogit, axis=0, keepdims=True)
    low = dlogit.astype(BF16)
    dsecond_ref[...] += tn(low_ref[...].astype(BF16), low)
    drank_ref[...] = nt(low, second_ref[...].astype(BF16))


def shape(dims, dtype):
    return jax.ShapeDtypeStruct(dims, dtype)


def call(kernel, blocks, in_specs, out_specs, out_shape, scratch, cost):
    return pl.pallas_call(
        kernel,
        grid_spec=pltpu.PrefetchScalarGridSpec(
            num_scalar_prefetch=1,
            grid=(blocks,),
            in_specs=in_specs,
            out_specs=out_specs,
            scratch_shapes=scratch,
        ),
        out_shape=out_shape,
        compiler_params=pltpu.CompilerParams(
            dimension_semantics=("arbitrary",), vmem_limit_bytes=VMEM_BYTES
        ),
        cost_estimate=pl.CostEstimate(flops=cost, bytes_accessed=16 << 20, transcendentals=1 << 20),
    )


def specs(blocks, backward=False):
    def at(c):
        return blocks - 1 - c if backward else c

    def proj(width, place):
        return pl.BlockSpec((2, CHUNK, width), lambda c, _: (0, at(c), place))

    def rows(width):
        return pl.BlockSpec((CHUNK, width), lambda c, _: (at(c), 0))

    def full(*dims):
        return pl.BlockSpec(dims, lambda c, _: (0,) * len(dims))

    row = pl.BlockSpec((1, 1, CHUNK), lambda c, _: (at(c), 0, 0))
    states = pl.BlockSpec((1, HEADS, KEY, VAL), lambda c, _: (at(c), 0, 0, 0))
    return proj, rows, full, row, states


def rms(x, eps):
    return x * lax.rsqrt(jnp.mean(x * x, axis=-1, keepdims=True) + eps)


def rms_back(x, gain, eps, grad):
    scale = lax.rsqrt(jnp.mean(x * x, axis=-1, keepdims=True) + eps)
    normed = x * scale
    dn = grad * gain
    back = scale * (dn - normed * jnp.mean(dn * normed, axis=-1, keepdims=True))
    return back, jnp.sum(grad * normed, axis=0)


def gather(shard):
    return lax.all_gather(shard, ALL, axis=0, tiled=True).reshape(2, -1, shard.shape[1])


def swap(x, stride):
    if stride == 0:
        return lax.ppermute(x, "tensor", [(0, 1), (1, 0)])
    return lax.ppermute(x, "dp", [(i, i ^ stride) for i in range(lax.axis_size("dp"))])


def own_bit(stride):
    return lax.axis_index("tensor") if stride == 0 else (lax.axis_index("dp") // stride) % 2


def long_strides():
    strides, stride = [], 4
    while stride < lax.axis_size("dp"):
        strides.append(stride)
        stride *= 2
    return strides


def grow(x, stride):
    other = swap(x, stride)
    return jnp.where(own_bit(stride) == 0, jnp.stack([x, other]), jnp.stack([other, x]))


def gather_steps(shard, mid):
    for stride in long_strides()[::-1] + list(mid) + [1]:
        shard = grow(shard, stride)
    steps = len(shard.shape) - 2
    z = steps - 3
    x_at, t_at = (2, 1) if mid[0] == 2 else (1, 2)
    z_axes = list(range(3, 3 + z))[::-1]
    order = [t_at] + z_axes + [x_at, 0, steps, steps + 1]
    return shard.transpose(order).reshape(2, -1, shard.shape[-1])


def by_core(act):
    rows = act.shape[0]
    z = len(long_strides())
    own = act.shape[1] // lax.axis_size("dp")
    split = act.reshape((rows,) + (2,) * (z + 2) + (own,))
    split = split.transpose([0, z + 2, z + 1] + list(range(1, z + 1))[::-1] + [z + 3])
    core = own_bit(1)
    other = lax.dynamic_index_in_dim(split, 1 - core, 1, keepdims=False).reshape(rows, -1)
    mine = lax.dynamic_index_in_dim(split, core, 1, keepdims=False).reshape(rows, -1)
    return other, mine


def halve(x, stride, axis):
    bit = own_bit(stride)
    send = lax.dynamic_index_in_dim(x, 1 - bit, axis, keepdims=False)
    keep = lax.dynamic_index_in_dim(x, bit, axis, keepdims=False)
    return keep + swap(send, stride)


def scatter(parts, equation, act):
    other, mine = by_core(act)
    sent = [jnp.einsum(equation, other, part, preferred_element_type=F32).astype(BF16) for part in parts]
    got = [swap(part, 1) for part in sent]
    kept = [jnp.einsum(equation, mine, part, preferred_element_type=F32).astype(BF16) for part in parts]
    kept = lax.optimization_barrier(kept)
    done = []
    for place, (x, extra) in enumerate(zip(kept, got)):
        x = x + extra
        cols = x.shape[-1]
        x = x.reshape((2, 2) + (2,) * len(long_strides()) + (-1, cols))
        if place % 2 == 0:
            x = halve(halve(x, 2, 1), 0, 0)
        else:
            x = halve(halve(x, 0, 0), 2, 0)
        for stride in long_strides():
            x = halve(x, stride, 0)
        done.append(x.astype(F32))
    return done


def total_sum(x):
    x = x + lax.ppermute(x, "tensor", [(0, 1), (1, 0)])
    n = lax.axis_size("dp")
    stride = 1
    while stride < n:
        x = x + lax.ppermute(x, "dp", [(i, i ^ stride) for i in range(n)])
        stride *= 2
    return x


def local(
    hidden_in, lengths, cotangent, query_weight, key_weight, value_weight, outgate_weight,
    output_weight, gate_weight, up_weight, down_weight, mixer_gain, feed_gain, low_first,
    low_second, decay_bias, head_gain,
):
    rows, width = hidden_in.shape
    blocks = rows // CHUNK
    place = lax.axis_index("tensor")
    half = gate_weight.shape[1]

    starts = jnp.cumsum(lengths[0]) - lengths[0]
    spots = place * rows + jnp.arange(-1, rows, dtype=jnp.int32)
    segments = jnp.sum((spots[:, None] >= starts[None, 1:]).astype(jnp.int32), axis=1)
    segments = jnp.where(spots < 0, -1, segments)
    seg = segments[1:].reshape(rows, 1)
    seg_row = segments[1:].reshape(blocks, 1, CHUNK)
    info = jnp.stack([segments[:-1].reshape(blocks, CHUNK)[:, 0], seg_row[:, 0, -1]])

    w_in_a = gather_steps(
        jnp.concatenate([query_weight, key_weight, value_weight[:, :256]], axis=1), (2, 0)
    )
    w_in_b = gather_steps(jnp.concatenate([value_weight[:, 256:], outgate_weight], axis=1), (0, 2))
    w_gu = gather(jnp.concatenate([gate_weight, up_weight, output_weight.T], axis=1))
    w_out = w_gu[..., 2 * half :]
    w_gu = w_gu[..., : 2 * half]
    w_down = gather(down_weight.T)

    resid = hidden_in.astype(F32)
    normed_a = (rms(resid, 1e-6) * mixer_gain).astype(BF16)
    proj_a = jnp.einsum("td,pdc->ptc", normed_a, w_in_a, preferred_element_type=F32).astype(BF16)
    proj_b = jnp.einsum("td,pdc->ptc", normed_a, w_in_b, preferred_element_type=F32).astype(BF16)
    lowrank = jnp.dot(normed_a.astype(F32), low_first, precision=HIGHEST)
    gain = head_gain.reshape(1, VAL)
    p_spec, r_spec, f_spec, row_spec, s_spec = specs(blocks)
    state_f32 = shape((HEADS, KEY, VAL), F32)
    cum, sig, final_state = call(
        gate_kernel,
        blocks,
        [r_spec(16), f_spec(16, 512), f_spec(1, 512), p_spec(256, 1), p_spec(256, 2),
         p_spec(256, 0), r_spec(1)],
        [r_spec(512), r_spec(512), f_spec(HEADS, KEY, VAL)],
        [shape((rows, 512), F32), shape((rows, 512), BF16), state_f32],
        [],
        1 << 29,
    )(info, lowrank, low_second, decay_bias.reshape(1, 512), proj_a, proj_a, proj_b, seg)
    state_in = lax.ppermute(final_state.astype(BF16), "tensor", [(0, 1)])
    mixed, core, states = call(
        core_kernel,
        blocks,
        [p_spec(256, 0), p_spec(256, 1), p_spec(256, 2), p_spec(256, 0), p_spec(256, 1), p_spec(256, 2),
         r_spec(512), r_spec(1), row_spec, f_spec(HEADS, KEY, VAL), f_spec(1, VAL)],
        [r_spec(1024), r_spec(1024), s_spec],
        [shape((rows, 1024), BF16), shape((rows, 1024), BF16),
         shape((blocks, HEADS, KEY, VAL), BF16)],
        [pltpu.VMEM((HEADS, KEY, VAL), F32)],
        1 << 30,
    )(info, proj_a, proj_a, proj_a, proj_b, proj_b, proj_b, cum, seg, seg_row, state_in, gain)
    middle = resid + nt(mixed[:, :512], w_out[0]) + nt(mixed[:, 512:], w_out[1])

    normed_b = (rms(middle, 1e-6) * feed_gain).astype(BF16)
    pre = jnp.einsum("td,pdc->ptc", normed_b, w_gu, preferred_element_type=F32).astype(BF16)
    gate_pre, up_pre = pre[..., :half].astype(F32), pre[..., half:].astype(F32)
    sig_gate = jax.nn.sigmoid(gate_pre)
    silu = gate_pre * sig_gate
    activ = (silu * up_pre).astype(BF16)
    feed_out = nt(activ[0], w_down[0]) + nt(activ[1], w_down[1])
    block_out = (middle + feed_out).astype(BF16)

    own_down = scatter([activ[..., :768], activ[..., 768:]], "to,ptc->poc", cotangent)
    d_activ = jnp.einsum("to,poc->ptc", cotangent, w_down, preferred_element_type=F32)
    d_gate = (d_activ * up_pre * (sig_gate * (1.0 + gate_pre * (1.0 - sig_gate)))).astype(BF16)
    d_up = (d_activ * silu).astype(BF16)
    own_gate, own_up = scatter([d_gate, d_up], "td,ptc->pdc", normed_b)
    d_pre = jnp.concatenate([d_gate, d_up], axis=-1)
    d_normed_b = nt(d_pre[0], w_gu[0]) + nt(d_pre[1], w_gu[1])
    back, feed_gain_grad = rms_back(middle, feed_gain, 1e-6, d_normed_b)
    d_middle = cotangent.astype(F32) + back
    d_mix = d_middle.astype(BF16)

    mixed_split = mixed.reshape(rows, 2, 512).transpose(1, 0, 2)
    own_out = scatter([mixed_split[..., :256], mixed_split[..., 256:]], "to,ptc->poc", d_mix)
    d_mixed = jnp.concatenate([nn(d_mix, w_out[0]), nn(d_mix, w_out[1])], axis=1).astype(BF16)
    d_core, d_og, head_gain_grad, d_state = call(
        post_kernel,
        blocks,
        [r_spec(1024), r_spec(1024), p_spec(256, 1), p_spec(256, 2), p_spec(256, 0), r_spec(512), r_spec(1),
         f_spec(1, VAL)],
        [r_spec(1024), p_spec(512, 0), f_spec(1, VAL), f_spec(HEADS, KEY, VAL)],
        [shape((rows, 1024), BF16), shape((2, rows, 512), BF16), shape((1, VAL), F32), state_f32],
        [pltpu.VMEM((1, 512), F32)],
        1 << 29,
    )(info, d_mixed, core, proj_b, proj_b, proj_a, cum, seg, gain)
    d_state_in = lax.ppermute(d_state.astype(BF16), "tensor", [(1, 0)])
    p_spec, r_spec, f_spec, row_spec, s_spec = specs(blocks, True)
    d_a, d_b, d_rank, low_second_grad, bias_grad = call(
        back_kernel,
        blocks,
        [p_spec(256, 0), p_spec(256, 1), p_spec(256, 2), p_spec(256, 0), p_spec(512, 0), r_spec(512), r_spec(512), s_spec,
         r_spec(1024), r_spec(1), row_spec, f_spec(HEADS, KEY, VAL), f_spec(16, 512), r_spec(16)],
        [p_spec(768, 0), p_spec(768, 0), r_spec(16), f_spec(16, 512), f_spec(1, 512)],
        [shape((2, rows, 768), BF16), shape((2, rows, 768), BF16), shape((rows, 16), F32), shape((16, 512), F32),
         shape((1, 512), F32)],
        [pltpu.VMEM((HEADS, KEY, VAL), F32)],
        3 << 30,
    )(info, proj_a, proj_a, proj_a, proj_b, d_og, cum, sig, states, d_core, seg, seg_row, d_state_in, low_second, lowrank)
    own_a, own_b = scatter([d_a, d_b], "td,ptc->pdc", normed_a)
    low_first_grad = tn(normed_a, d_rank.astype(BF16))
    d_normed_a = (
        nt(d_a[0], w_in_a[0])
        + nt(d_a[1], w_in_a[1])
        + nt(d_b[0], w_in_b[0])
        + nt(d_b[1], w_in_b[1])
        + nt(d_rank.astype(BF16), low_first.astype(BF16))
    )
    back, mixer_gain_grad = rms_back(resid, mixer_gain, 1e-6, d_normed_a)
    input_grad = (d_middle + back).astype(BF16)

    parts = (mixer_gain_grad, feed_gain_grad, low_first_grad, low_second_grad, bias_grad, head_gain_grad)
    flat = total_sum(jnp.concatenate([part.reshape(-1, 128) for part in parts]))
    small, spot = [], 0
    for part, dims in zip(
        parts, ((width,), (width,), low_first.shape, low_second.shape, (512,), (VAL,))
    ):
        size = part.size // 128
        small.append(flat[spot : spot + size].reshape(dims))
        spot += size
    return (
        block_out,
        input_grad,
        own_a[:, :256],
        own_a[:, 256:512],
        jnp.concatenate([own_a[:, 512:], own_b[:, :256]], axis=1),
        own_b[:, 256:],
        jnp.concatenate([part.T for part in own_out], axis=0),
        own_gate,
        own_up,
        jnp.concatenate([part.T for part in own_down], axis=0),
        *small,
    )


def solution(mesh):
    tokens = P(("dp", "tensor"))
    split_in = P("dp", "tensor")
    split_out = P("tensor", "dp")
    weights = (split_in,) * 4 + (split_out,) + (split_in,) * 2 + (split_out,)
    in_specs = (tokens, P("dp", None), tokens) + weights + (P(),) * 6
    out_specs = (tokens, tokens) + weights + (P(),) * 6
    return jax.shard_map(local, mesh=mesh, in_specs=in_specs, out_specs=out_specs, check_vma=False)
```

```python
import jax
import jax.numpy as jnp
from jax import lax
from jax.experimental import pallas as pl
from jax.experimental.pallas import tpu as pltpu
from jax.sharding import PartitionSpec as P

HEADS = 4
KEY = 128
VAL = 256
CHUNK = 128
SCALE = KEY ** (-0.5)
F32 = jnp.float32
BF16 = jnp.bfloat16
HIGHEST = lax.Precision.HIGHEST
ALL = ("tensor", "dp")
VMEM_BYTES = 48 * 1024 * 1024


def nn(a, b):
    return lax.dot_general(a, b, (((1,), (0,)), ((), ())), preferred_element_type=F32)


def nt(a, b):
    return lax.dot_general(a, b, (((1,), (1,)), ((), ())), preferred_element_type=F32)


def tn(a, b):
    return lax.dot_general(a, b, (((0,), (0,)), ((), ())), preferred_element_type=F32)


def triangle(lower):
    rows = lax.broadcasted_iota(jnp.int32, (CHUNK, CHUNK), 0)
    cols = lax.broadcasted_iota(jnp.int32, (CHUNK, CHUNK), 1)
    return rows >= cols if lower else rows <= cols


def split_sum(tri, x, terms):
    total = None
    for _ in range(terms):
        part = x.astype(BF16)
        x = x - part.astype(F32)
        term = nn(tri, part)
        total = term if total is None else total + term
    return total


def head_cols(h, width):
    return h // 2, slice((h % 2) * width, (h % 2 + 1) * width)


def head_pick(h, first, second):
    return (first if h % 2 == 0 else second)[h // 2]


def gate_kernel(info, low_ref, second_ref, bias_ref, k_ref, v0_ref, v1_ref, seg_ref, cum_ref, sig_ref, state_ref):
    c = pl.program_id(0)

    @pl.when(c == 0)
    def _():
        state_ref[...] = jnp.zeros_like(state_ref)

    logit = (
        jnp.dot(low_ref[...], second_ref[...], precision=HIGHEST, preferred_element_type=F32)
        + bias_ref[...]
    )
    e = jnp.exp(-jnp.abs(logit))
    decays = (jnp.minimum(logit, 0.0) - jnp.log1p(e)) * (1.0 / 16.0)
    sig_ref[...] = (jnp.where(logit >= 0, e, 1.0) / (1.0 + e)).astype(BF16)
    tri = triangle(True).astype(F32).astype(BF16)
    cum = split_sum(tri, decays, 3)
    cum_ref[...] = cum
    final = cum[CHUNK - 1 :, :]
    tail = (seg_ref[...] == info[1, c]).astype(F32)
    retain = (info[1, c] == info[0, c]).astype(F32)
    tail_decay = jnp.exp(final - cum) * tail
    keep = jnp.exp(final) * retain
    for h in range(HEADS):
        p, kc = head_cols(h, KEY)
        hk = slice(h * KEY, (h + 1) * KEY)
        kt = (k_ref[p, :, kc].astype(F32) * tail_decay[:, hk]).astype(BF16)
        state_ref[h] = state_ref[h] * keep[:, hk].reshape(KEY, 1) + tn(kt, head_pick(h, v0_ref, v1_ref))


def core_kernel(
    info, q_ref, k_ref, v0_ref, v1_ref, og0_ref, og1_ref, cum_ref, seg_ref, row_ref, first_ref, gain_ref,
    mixed_ref, core_ref, states_ref, state,
):
    c = pl.program_id(0)

    @pl.when(c == 0)
    def _():
        state[...] = first_ref[...].astype(F32)

    before, last = info[0, c], info[1, c]
    seg = seg_ref[...]
    mask = triangle(True) & (seg == row_ref[0])
    running = (seg == before).astype(F32)
    tail = (seg == last).astype(F32)
    retain = (last == before).astype(F32)
    cum = cum_ref[...]
    final = cum[CHUNK - 1 :, :]
    mid = cum[CHUNK // 2 - 1 : CHUNK // 2, :]
    up, down = jnp.exp(cum - mid), jnp.exp(mid - cum)
    whole = jnp.exp(cum) * running
    rest = jnp.exp(final - cum) * tail
    keep = jnp.exp(final) * retain
    for h in range(HEADS):
        p, kc = head_cols(h, KEY)
        hk = slice(h * KEY, (h + 1) * KEY)
        q = q_ref[p, :, kc].astype(F32) * SCALE
        k = k_ref[p, :, kc].astype(F32)
        v = head_pick(h, v0_ref, v1_ref)
        s = state[h]
        s_low = s.astype(BF16)
        states_ref[0, h] = s_low
        scores = nt((q * up[:, hk]).astype(BF16), (k * down[:, hk]).astype(BF16))
        scores = jnp.where(mask, scores, 0.0).astype(BF16)
        core = nn((q * whole[:, hk]).astype(BF16), s_low) + nn(scores, v)
        state[h] = s * keep[:, hk].reshape(KEY, 1) + tn((k * rest[:, hk]).astype(BF16), v)
        normed = core * lax.rsqrt(jnp.mean(core * core, axis=-1, keepdims=True) + 1.0)
        og = head_pick(h, og0_ref, og1_ref).astype(F32)
        hv = slice(h * VAL, (h + 1) * VAL)
        mixed_ref[:, hv] = (normed * gain_ref[...] * (og * jax.nn.sigmoid(og))).astype(BF16)
        core_ref[:, hv] = core.astype(BF16)


def post_kernel(
    info, dm_ref, core_ref, og0_ref, og1_ref, q_ref, cum_ref, seg_ref, gain_ref,
    dcore_ref, dog_ref, dgain_ref, dstate_ref, prefix,
):
    c = pl.program_id(0)

    @pl.when(c == 0)
    def _():
        prefix[...] = jnp.zeros_like(prefix)
        dgain_ref[...] = jnp.zeros_like(dgain_ref)
        dstate_ref[...] = jnp.zeros_like(dstate_ref)

    running = (seg_ref[...] == info[0, 0]).astype(F32)
    cum = cum_ref[...]
    decay = jnp.exp(cum + prefix[...]) * running * SCALE
    prefix[...] += cum[CHUNK - 1 :, :]
    gain = gain_ref[...]
    total = jnp.zeros((1, VAL), F32)
    for h in range(HEADS):
        p, kc = head_cols(h, KEY)
        hk = slice(h * KEY, (h + 1) * KEY)
        hv = slice(h * VAL, (h + 1) * VAL)
        core = core_ref[:, hv].astype(F32)
        scale = lax.rsqrt(jnp.mean(core * core, axis=-1, keepdims=True) + 1.0)
        normed = core * scale
        og = head_pick(h, og0_ref, og1_ref).astype(F32)
        sig = jax.nn.sigmoid(og)
        silu = og * sig
        dm = dm_ref[:, hv].astype(F32)
        both = dm * normed
        total += jnp.sum(both * silu, axis=0, keepdims=True)
        dog_ref[p, :, head_cols(h, VAL)[1]] = (both * gain * (sig * (1.0 + og * (1.0 - sig)))).astype(BF16)
        dn = dm * gain * silu
        dcore = scale * (dn - normed * jnp.mean(dn * normed, axis=-1, keepdims=True))
        dcore = dcore.astype(BF16)
        dcore_ref[:, hv] = dcore
        qa = (q_ref[p, :, kc].astype(F32) * decay[:, hk]).astype(BF16)
        dstate_ref[h] += tn(qa, dcore)
    dgain_ref[...] += total


def back_kernel(
    info, q_ref, k_ref, v0_ref, v1_ref, dog_ref, cum_ref, sig_ref, states_ref, dcore_ref, seg_ref, row_ref,
    first_ref, second_ref, low_ref, da_ref, db_ref, drank_ref, dsecond_ref, dbias_ref, dstate,
):
    i = pl.program_id(0)
    c = pl.num_programs(0) - 1 - i

    @pl.when(i == 0)
    def _():
        dstate[...] = first_ref[...].astype(F32)
        dsecond_ref[...] = jnp.zeros_like(dsecond_ref)
        dbias_ref[...] = jnp.zeros_like(dbias_ref)

    before, last = info[0, c], info[1, c]
    seg = seg_ref[...]
    mask = triangle(True) & (seg == row_ref[0])
    upper = triangle(False).astype(F32).astype(BF16)
    running = (seg == before).astype(F32)
    tail = (seg == last).astype(F32)
    retain = (last == before).astype(F32)
    cum = cum_ref[...]
    final = cum[CHUNK - 1 :, :]
    mid = cum[CHUNK // 2 - 1 : CHUNK // 2, :]
    up, down = jnp.exp(cum - mid), jnp.exp(mid - cum)
    whole = jnp.exp(cum) * running
    rest = jnp.exp(final - cum) * tail
    keep = jnp.exp(final) * retain
    logits = []
    for h in range(HEADS):
        p, kc = head_cols(h, KEY)
        hk = slice(h * KEY, (h + 1) * KEY)
        hv = slice(h * VAL, (h + 1) * VAL)
        q = q_ref[p, :, kc].astype(F32) * SCALE
        k = k_ref[p, :, kc].astype(F32)
        v = head_pick(h, v0_ref, v1_ref)
        do = dcore_ref[:, hv]
        s = states_ref[0, h]
        ds = dstate[h]
        ds_low = ds.astype(BF16)
        q_up = (q * up[:, hk]).astype(BF16)
        k_down = (k * down[:, hk]).astype(BF16)
        q_whole = (q * whole[:, hk]).astype(BF16)
        k_rest = (k * rest[:, hk]).astype(BF16)
        scores = jnp.where(mask, nt(q_up, k_down), 0.0).astype(BF16)
        dscores = jnp.where(mask, nt(do, v), 0.0).astype(BF16)
        dq_up = nn(dscores, k_down)
        dk_down = tn(dscores, q_up)
        dq_whole = nt(do, s)
        dk_rest = nt(v, ds_low)
        dv = tn(scores, do) + nn(k_rest, ds_low)
        dq = dq_up * up[:, hk] + dq_whole * whole[:, hk]
        dk = dk_down * down[:, hk] + dk_rest * rest[:, hk]
        from_rest = k_rest.astype(F32) * dk_rest
        dcum = (
            q_up.astype(F32) * dq_up
            - k_down.astype(F32) * dk_down
            + q_whole.astype(F32) * dq_whole
            - from_rest
        )
        kept = keep[:, hk].reshape(KEY, 1)
        through = jnp.sum(s.astype(F32) * ds, axis=1, keepdims=True) * kept
        dfinal = through.reshape(1, KEY) + jnp.sum(from_rest, axis=0, keepdims=True)
        ddecay = split_sum(upper, dcum, 2) + dfinal
        dstate[h] = ds * kept + tn(q_whole, do)
        logits.append(ddecay * (sig_ref[:, hk].astype(F32) * (1.0 / 16.0)))
        da_ref[p, :, kc] = (dq * SCALE).astype(BF16)
        da_ref[p, :, slice(256 + kc.start, 256 + kc.stop)] = dk.astype(BF16)
        if h % 2 == 0:
            da_ref[p, :, 512:] = dv.astype(BF16)
        else:
            db_ref[p, :, :256] = dv.astype(BF16)
    db_ref[:, :, 256:] = dog_ref[...]
    dlogit = jnp.concatenate(logits, axis=1)
    dbias_ref[...] += jnp.sum(dlogit, axis=0, keepdims=True)
    low = dlogit.astype(BF16)
    dsecond_ref[...] += tn(low_ref[...].astype(BF16), low)
    drank_ref[...] = nt(low, second_ref[...].astype(BF16))


def shape(dims, dtype):
    return jax.ShapeDtypeStruct(dims, dtype)


def call(kernel, blocks, in_specs, out_specs, out_shape, scratch, cost):
    return pl.pallas_call(
        kernel,
        grid_spec=pltpu.PrefetchScalarGridSpec(
            num_scalar_prefetch=1,
            grid=(blocks,),
            in_specs=in_specs,
            out_specs=out_specs,
            scratch_shapes=scratch,
        ),
        out_shape=out_shape,
        compiler_params=pltpu.CompilerParams(
            dimension_semantics=("arbitrary",), vmem_limit_bytes=VMEM_BYTES
        ),
        cost_estimate=pl.CostEstimate(flops=cost, bytes_accessed=16 << 20, transcendentals=1 << 20),
    )


def specs(blocks, backward=False):
    def at(c):
        return blocks - 1 - c if backward else c

    def proj(width, place):
        return pl.BlockSpec((2, CHUNK, width), lambda c, _: (0, at(c), place))

    def rows(width):
        return pl.BlockSpec((CHUNK, width), lambda c, _: (at(c), 0))

    def full(*dims):
        return pl.BlockSpec(dims, lambda c, _: (0,) * len(dims))

    row = pl.BlockSpec((1, 1, CHUNK), lambda c, _: (at(c), 0, 0))
    states = pl.BlockSpec((1, HEADS, KEY, VAL), lambda c, _: (at(c), 0, 0, 0))
    return proj, rows, full, row, states


def rms(x, eps):
    return x * lax.rsqrt(jnp.mean(x * x, axis=-1, keepdims=True) + eps)


def rms_back(x, gain, eps, grad):
    scale = lax.rsqrt(jnp.mean(x * x, axis=-1, keepdims=True) + eps)
    normed = x * scale
    dn = grad * gain
    back = scale * (dn - normed * jnp.mean(dn * normed, axis=-1, keepdims=True))
    return back, jnp.sum(grad * normed, axis=0)


def gather(shard):
    return lax.all_gather(shard, ALL, axis=0, tiled=True).reshape(2, -1, shard.shape[1])


def swap(x, stride):
    if stride == 0:
        return lax.ppermute(x, "tensor", [(0, 1), (1, 0)])
    return lax.ppermute(x, "dp", [(i, i ^ stride) for i in range(lax.axis_size("dp"))])


def own_bit(stride):
    return lax.axis_index("tensor") if stride == 0 else (lax.axis_index("dp") // stride) % 2


def long_strides():
    strides, stride = [], 4
    while stride < lax.axis_size("dp"):
        strides.append(stride)
        stride *= 2
    return strides


def grow(x, stride):
    other = swap(x, stride)
    return jnp.where(own_bit(stride) == 0, jnp.stack([x, other]), jnp.stack([other, x]))


def gather_steps(shard, mid):
    for stride in long_strides()[::-1] + list(mid) + [1]:
        shard = grow(shard, stride)
    steps = len(shard.shape) - 2
    z = steps - 3
    x_at, t_at = (2, 1) if mid[0] == 2 else (1, 2)
    z_axes = list(range(3, 3 + z))[::-1]
    order = [t_at] + z_axes + [x_at, 0, steps, steps + 1]
    return shard.transpose(order).reshape(2, -1, shard.shape[-1])


def by_core(act):
    rows = act.shape[0]
    z = len(long_strides())
    own = act.shape[1] // lax.axis_size("dp")
    split = act.reshape((rows,) + (2,) * (z + 2) + (own,))
    split = split.transpose([0, z + 2, z + 1] + list(range(1, z + 1))[::-1] + [z + 3])
    core = own_bit(1)
    other = lax.dynamic_index_in_dim(split, 1 - core, 1, keepdims=False).reshape(rows, -1)
    mine = lax.dynamic_index_in_dim(split, core, 1, keepdims=False).reshape(rows, -1)
    return other, mine


def fence(*values):
    return lax.optimization_barrier(values)


def during(sends, work, *inputs):
    arrays, inputs = fence([array for array, _ in sends], inputs)
    got = [swap(array, stride) for array, (_, stride) in zip(arrays, sends)]
    return fence(work(*inputs), got)


def products(equation, act, parts):
    return [jnp.einsum(equation, act, part, preferred_element_type=F32).astype(BF16) for part in parts]


class Halving:
    def __init__(self, parts, got, firsts):
        self.orders = [[2, 0] if first == 2 else [0, 2] for first in firsts]
        self.orders = [order + long_strides() for order in self.orders]
        self.parts = [
            (part + extra).reshape((2, 2) + (2,) * len(long_strides()) + (-1, part.shape[-1]))
            for part, extra in zip(parts, got)
        ]

    def sends(self):
        self.kept, out = [], []
        for i, part in enumerate(self.parts):
            stride = self.orders[i][0]
            axis = 1 if stride == 2 and len(self.orders[i]) == len(long_strides()) + 2 else 0
            bit = own_bit(stride)
            self.kept.append(lax.dynamic_index_in_dim(part, bit, axis, keepdims=False))
            out.append((lax.dynamic_index_in_dim(part, 1 - bit, axis, keepdims=False), stride))
        return out

    def receive(self, got):
        self.parts = [kept + extra for kept, extra in zip(self.kept, got)]
        self.orders = [order[1:] for order in self.orders]

    def finish(self):
        while self.orders[0]:
            sends = self.sends()
            self.receive([swap(array, stride) for array, stride in sends])
        return [part.astype(F32) for part in self.parts]


def total_sum(x):
    x = x + swap(x, 0)
    stride = 1
    while stride < lax.axis_size("dp"):
        x = x + swap(x, stride)
        stride *= 2
    return x


def local(
    hidden_in, lengths, cotangent, query_weight, key_weight, value_weight, outgate_weight,
    output_weight, gate_weight, up_weight, down_weight, mixer_gain, feed_gain, low_first,
    low_second, decay_bias, head_gain,
):
    rows, width = hidden_in.shape
    blocks = rows // CHUNK
    place = lax.axis_index("tensor")
    half = gate_weight.shape[1]

    starts = jnp.cumsum(lengths[0]) - lengths[0]
    spots = place * rows + jnp.arange(-1, rows, dtype=jnp.int32)
    segments = jnp.sum((spots[:, None] >= starts[None, 1:]).astype(jnp.int32), axis=1)
    segments = jnp.where(spots < 0, -1, segments)
    seg = segments[1:].reshape(rows, 1)
    seg_row = segments[1:].reshape(blocks, 1, CHUNK)
    info = jnp.stack([segments[:-1].reshape(blocks, CHUNK)[:, 0], seg_row[:, 0, -1]])

    w_in_a = gather_steps(
        jnp.concatenate([query_weight, key_weight, value_weight[:, :256]], axis=1), (2, 0)
    )
    w_in_b = gather_steps(jnp.concatenate([value_weight[:, 256:], outgate_weight], axis=1), (0, 2))
    w_rest = gather(
        jnp.concatenate([gate_weight, up_weight, output_weight.T, down_weight.T], axis=1)
    )
    w_gu, w_out = w_rest[..., : 2 * half], w_rest[..., 2 * half : 2 * half + 512]
    w_down = w_rest[..., 2 * half + 512 :]

    resid = hidden_in.astype(F32)
    normed_a = (rms(resid, 1e-6) * mixer_gain).astype(BF16)
    proj_a = jnp.einsum("td,pdc->ptc", normed_a, w_in_a, preferred_element_type=F32).astype(BF16)
    proj_v = jnp.einsum(
        "td,pdc->ptc", normed_a, w_in_b[..., :256], preferred_element_type=F32
    ).astype(BF16)
    lowrank = jnp.dot(normed_a.astype(F32), low_first, precision=HIGHEST)
    gain = head_gain.reshape(1, VAL)
    p_spec, r_spec, f_spec, row_spec, s_spec = specs(blocks)
    state_f32 = shape((HEADS, KEY, VAL), F32)
    cum, sig, final_state = call(
        gate_kernel,
        blocks,
        [r_spec(16), f_spec(16, 512), f_spec(1, 512), p_spec(256, 1), p_spec(256, 2),
         p_spec(256, 0), r_spec(1)],
        [r_spec(512), r_spec(512), f_spec(HEADS, KEY, VAL)],
        [shape((rows, 512), F32), shape((rows, 512), BF16), state_f32],
        [],
        1 << 29,
    )(info, lowrank, low_second, decay_bias.reshape(1, 512), proj_a, proj_a, proj_v, seg)
    def outgate_product(act, weight):
        return jnp.einsum("td,pdc->ptc", act, weight, preferred_element_type=F32).astype(BF16)

    proj_og, (state_in,) = during(
        [(final_state.astype(BF16), 0)], outgate_product, normed_a, w_in_b[..., 256:]
    )
    state_in = jnp.where(place == 0, jnp.zeros_like(state_in), state_in)
    mixed, core, states = call(
        core_kernel,
        blocks,
        [p_spec(256, 0), p_spec(256, 1), p_spec(256, 2), p_spec(256, 0), p_spec(256, 0), p_spec(256, 1),
         r_spec(512), r_spec(1), row_spec, f_spec(HEADS, KEY, VAL), f_spec(1, VAL)],
        [r_spec(1024), r_spec(1024), s_spec],
        [shape((rows, 1024), BF16), shape((rows, 1024), BF16),
         shape((blocks, HEADS, KEY, VAL), BF16)],
        [pltpu.VMEM((HEADS, KEY, VAL), F32)],
        1 << 30,
    )(info, proj_a, proj_a, proj_a, proj_v, proj_og, proj_og, cum, seg, seg_row, state_in, gain)
    middle = resid + nt(mixed[:, :512], w_out[0]) + nt(mixed[:, 512:], w_out[1])

    normed_b = (rms(middle, 1e-6) * feed_gain).astype(BF16)
    pre = jnp.einsum("td,pdc->ptc", normed_b, w_gu, preferred_element_type=F32).astype(BF16)
    activ = (jax.nn.silu(pre[..., :half].astype(F32)) * pre[..., half:].astype(F32)).astype(BF16)

    ff_out, ff_in, mix_in = "to,ptc->poc", "td,ptc->pdc", "td,ptc->pdc"
    other, mine = by_core(cotangent)
    halves = [activ[..., :768], activ[..., 768:]]
    sent = products(ff_out, other, halves)
    kept, got = during([(part, 1) for part in sent], lambda a, *b: products(ff_out, a, b), mine, *halves)
    down = Halving(kept, got, (2, 0))

    def activation_back(dout, weight, gate_pre, up_pre):
        d_activ = jnp.einsum("to,poc->ptc", dout, weight, preferred_element_type=F32)
        gate_pre, up_pre = gate_pre.astype(F32), up_pre.astype(F32)
        sig = jax.nn.sigmoid(gate_pre)
        d_gate = (d_activ * up_pre * (sig * (1.0 + gate_pre * (1.0 - sig)))).astype(BF16)
        return d_gate, (d_activ * (gate_pre * sig)).astype(BF16)

    (d_gate, d_up), got = during(
        down.sends(), activation_back, cotangent, w_down, pre[..., :half], pre[..., half:]
    )
    down.receive(got)

    other, mine = by_core(normed_b)
    sent, got = during(
        down.sends(), lambda a, *b: products(ff_in, a, b), other, d_gate, d_up
    )
    down.receive(got)

    def mine_and_out(act, *operands):
        grads = products(ff_in, act, operands[:2])
        return grads, nt(operands[2][0], operands[3][0]) + nt(operands[2][1], operands[3][1])

    (kept, feed_out), got = during(
        [(part, 1) for part in sent] + down.sends(), mine_and_out, mine, d_gate, d_up, activ, w_down
    )
    block_out = (middle + feed_out).astype(BF16)
    down.receive(got[2:])
    gate_up = Halving(kept, got[:2], (2, 0))

    def middle_back(d_gate, d_up, w_gu, middle, w_out):
        d_normed_b = (
            nt(d_gate[0], w_gu[0, :, :half])
            + nt(d_up[0], w_gu[0, :, half:])
            + nt(d_gate[1], w_gu[1, :, :half])
            + nt(d_up[1], w_gu[1, :, half:])
        )
        back, feed_gain_grad = rms_back(middle, feed_gain, 1e-6, d_normed_b)
        d_middle = cotangent.astype(F32) + back
        d_mix = d_middle.astype(BF16)
        d_mixed = jnp.concatenate([nn(d_mix, w_out[0]), nn(d_mix, w_out[1])], axis=1).astype(BF16)
        return d_middle, d_mix, d_mixed, feed_gain_grad

    (d_middle, d_mix, d_mixed, feed_gain_grad), got = during(
        gate_up.sends() + down.sends(), middle_back, d_gate, d_up, w_gu, middle, w_out
    )
    gate_up.receive(got[:2])
    down.receive(got[2:])
    own_down = down.finish()

    mixed_split = mixed.reshape(rows, 2, 512).transpose(1, 0, 2)
    mixed_halves = [mixed_split[..., :256], mixed_split[..., 256:]]

    def post_back(d_mixed, d_mix, *mixed_halves):
        d_core, d_og, head_gain_grad, d_state = call(
            post_kernel,
            blocks,
            [r_spec(1024), r_spec(1024), p_spec(256, 0), p_spec(256, 1), p_spec(256, 0), r_spec(512),
             r_spec(1), f_spec(1, VAL)],
            [r_spec(1024), p_spec(512, 0), f_spec(1, VAL), f_spec(HEADS, KEY, VAL)],
            [shape((rows, 1024), BF16), shape((2, rows, 512), BF16), shape((1, VAL), F32), state_f32],
            [pltpu.VMEM((1, 512), F32)],
            1 << 29,
        )(info, d_mixed, core, proj_og, proj_og, proj_a, cum, seg, gain)
        other, mine = by_core(d_mix)
        (sent, kept), (d_state_in,) = during(
            [(d_state.astype(BF16), 0)],
            lambda a, b, *c: (products(ff_out, a, c), products(ff_out, b, c)),
            other, mine, *mixed_halves,
        )
        return d_core, d_og, head_gain_grad, d_state_in, sent, kept

    (d_core, d_og, head_gain_grad, d_state_in, sent, kept), got = during(
        gate_up.sends(), post_back, d_mixed, d_mix, *mixed_halves
    )
    gate_up.receive(got)
    d_state_in = jnp.where(place == 1, jnp.zeros_like(d_state_in), d_state_in)
    p_spec, r_spec, f_spec, row_spec, s_spec = specs(blocks, True)

    def core_back(d_core, d_og, d_state_in):
        return call(
            back_kernel,
            blocks,
            [p_spec(256, 0), p_spec(256, 1), p_spec(256, 2), p_spec(256, 0), p_spec(512, 0),
             r_spec(512), r_spec(512), s_spec, r_spec(1024), r_spec(1), row_spec,
             f_spec(HEADS, KEY, VAL), f_spec(16, 512), r_spec(16)],
            [p_spec(768, 0), p_spec(768, 0), r_spec(16), f_spec(16, 512), f_spec(1, 512)],
            [shape((2, rows, 768), BF16), shape((2, rows, 768), BF16), shape((rows, 16), F32),
             shape((16, 512), F32), shape((1, 512), F32)],
            [pltpu.VMEM((HEADS, KEY, VAL), F32)],
            3 << 30,
        )(info, proj_a, proj_a, proj_a, proj_v, d_og, cum, sig, states, d_core, seg, seg_row,
          d_state_in, low_second, lowrank)

    (d_a, d_b, d_rank, low_second_grad, bias_grad), got = during(
        gate_up.sends() + [(part, 1) for part in sent], core_back, d_core, d_og, d_state_in
    )
    gate_up.receive(got[:2])
    out = Halving(kept, got[2:], (2, 0))

    other, mine = by_core(normed_a)
    sent, got = during(
        gate_up.sends() + out.sends(), lambda a, *b: products(mix_in, a, b), other, d_a, d_b
    )
    gate_up.receive(got[:2])
    out.receive(got[2:])
    own_gate, own_up = gate_up.finish()
    kept, got = during(
        [(part, 1) for part in sent] + out.sends(), lambda a, *b: products(mix_in, a, b), mine, d_a, d_b
    )
    out.receive(got[2:])
    mix = Halving(kept, got[:2], (2, 0))

    def input_back(d_a, d_b, d_rank, w_a, w_b):
        low_first_grad = tn(normed_a, d_rank.astype(BF16))
        d_normed_a = (
            nt(d_a[0], w_a[0])
            + nt(d_a[1], w_a[1])
            + nt(d_b[0], w_b[0])
            + nt(d_b[1], w_b[1])
            + nt(d_rank.astype(BF16), low_first.astype(BF16))
        )
        return d_normed_a, low_first_grad

    (d_normed_a, low_first_grad), got = during(
        mix.sends() + out.sends(), input_back, d_a, d_b, d_rank, w_in_a, w_in_b
    )
    mix.receive(got[:2])
    out.receive(got[2:])

    def input_end(d_normed_a, d_middle):
        back, mixer_gain_grad = rms_back(resid, mixer_gain, 1e-6, d_normed_a)
        return (d_middle + back).astype(BF16), mixer_gain_grad

    (input_grad, mixer_gain_grad), got = during(
        mix.sends() + out.sends(), input_end, d_normed_a, d_middle
    )
    mix.receive(got[:2])
    out.receive(got[2:])
    own_out = out.finish()
    own_a, own_b = mix.finish()

    parts = (mixer_gain_grad, feed_gain_grad, low_first_grad, low_second_grad, bias_grad, head_gain_grad)
    flat = total_sum(jnp.concatenate([part.reshape(-1, 128) for part in parts]))
    small, spot = [], 0
    for part, dims in zip(
        parts, ((width,), (width,), low_first.shape, low_second.shape, (512,), (VAL,))
    ):
        size = part.size // 128
        small.append(flat[spot : spot + size].reshape(dims))
        spot += size
    return (
        block_out,
        input_grad,
        own_a[:, :256],
        own_a[:, 256:512],
        jnp.concatenate([own_a[:, 512:], own_b[:, :256]], axis=1),
        own_b[:, 256:],
        jnp.concatenate([part.T for part in own_out], axis=0),
        own_gate,
        own_up,
        jnp.concatenate([part.T for part in own_down], axis=0),
        *small,
    )


def solution(mesh):
    tokens = P(("dp", "tensor"))
    split_in = P("dp", "tensor")
    split_out = P("tensor", "dp")
    weights = (split_in,) * 4 + (split_out,) + (split_in,) * 2 + (split_out,)
    in_specs = (tokens, P("dp", None), tokens) + weights + (P(),) * 6
    out_specs = (tokens, tokens) + weights + (P(),) * 6
    return jax.shard_map(local, mesh=mesh, in_specs=in_specs, out_specs=out_specs, check_vma=False)
```

```python
import functools

import jax
import jax.numpy as jnp
from jax import lax
from jax.experimental import pallas as pl
from jax.experimental.pallas import tpu as pltpu
from jax.sharding import PartitionSpec as P

HEADS = 4
KEY = 128
VAL = 256
CHUNK = 128
SCALE = KEY ** (-0.5)
F32 = jnp.float32
BF16 = jnp.bfloat16
HIGHEST = lax.Precision.HIGHEST
ALL = ("tensor", "dp")
VMEM_BYTES = 56 * 1024 * 1024
TILE = 256


def nn(a, b):
    return lax.dot_general(a, b, (((1,), (0,)), ((), ())), preferred_element_type=F32)


def nt(a, b):
    return lax.dot_general(a, b, (((1,), (1,)), ((), ())), preferred_element_type=F32)


def tn(a, b):
    return lax.dot_general(a, b, (((0,), (0,)), ((), ())), preferred_element_type=F32)


def triangle(lower):
    rows = lax.broadcasted_iota(jnp.int32, (CHUNK, CHUNK), 0)
    cols = lax.broadcasted_iota(jnp.int32, (CHUNK, CHUNK), 1)
    return rows >= cols if lower else rows <= cols


def split_sum(tri, x, terms):
    total = None
    for _ in range(terms):
        part = x.astype(BF16)
        x = x - part.astype(F32)
        term = nn(tri, part)
        total = term if total is None else total + term
    return total


def head_cols(h, width):
    return h // 2, slice((h % 2) * width, (h % 2 + 1) * width)


def head_pick(h, first, second):
    return (first if h % 2 == 0 else second)[h // 2]


def gate_kernel(info, low_ref, second_ref, bias_ref, k_ref, v0_ref, v1_ref, seg_ref, cum_ref, sig_ref, state_ref):
    c = pl.program_id(0)

    @pl.when(c == 0)
    def _():
        state_ref[...] = jnp.zeros_like(state_ref)

    logit = (
        jnp.dot(low_ref[...], second_ref[...], precision=HIGHEST, preferred_element_type=F32)
        + bias_ref[...]
    )
    e = jnp.exp(-jnp.abs(logit))
    decays = (jnp.minimum(logit, 0.0) - jnp.log1p(e)) * (1.0 / 16.0)
    sig_ref[...] = (jnp.where(logit >= 0, e, 1.0) / (1.0 + e)).astype(BF16)
    tri = triangle(True).astype(F32).astype(BF16)
    cum = split_sum(tri, decays, 3)
    cum_ref[...] = cum
    final = cum[CHUNK - 1 :, :]
    tail = (seg_ref[...] == info[1, c]).astype(F32)
    retain = (info[1, c] == info[0, c]).astype(F32)
    tail_decay = jnp.exp(final - cum) * tail
    keep = jnp.exp(final) * retain
    for h in range(HEADS):
        p, kc = head_cols(h, KEY)
        hk = slice(h * KEY, (h + 1) * KEY)
        kt = (k_ref[p, :, kc].astype(F32) * tail_decay[:, hk]).astype(BF16)
        state_ref[h] = state_ref[h] * keep[:, hk].reshape(KEY, 1) + tn(kt, head_pick(h, v0_ref, v1_ref))


def core_kernel(
    info, q_ref, k_ref, v0_ref, v1_ref, og0_ref, og1_ref, cum_ref, seg_ref, row_ref, first_ref, gain_ref,
    mixed_ref, mixed_a_ref, mixed_b_ref, core_ref, states_ref, state,
):
    c = pl.program_id(0)

    @pl.when(c == 0)
    def _():
        state[...] = first_ref[...].astype(F32)

    before, last = info[0, c], info[1, c]
    seg = seg_ref[...]
    mask = triangle(True) & (seg == row_ref[0])
    running = (seg == before).astype(F32)
    tail = (seg == last).astype(F32)
    retain = (last == before).astype(F32)
    cum = cum_ref[...]
    final = cum[CHUNK - 1 :, :]
    mid = cum[CHUNK // 2 - 1 : CHUNK // 2, :]
    up, down = jnp.exp(cum - mid), jnp.exp(mid - cum)
    whole = jnp.exp(cum) * running
    rest = jnp.exp(final - cum) * tail
    keep = jnp.exp(final) * retain
    for h in range(HEADS):
        p, kc = head_cols(h, KEY)
        hk = slice(h * KEY, (h + 1) * KEY)
        q = q_ref[p, :, kc].astype(F32) * SCALE
        k = k_ref[p, :, kc].astype(F32)
        v = head_pick(h, v0_ref, v1_ref)
        s = state[h]
        s_low = s.astype(BF16)
        states_ref[0, h] = s_low
        scores = nt((q * up[:, hk]).astype(BF16), (k * down[:, hk]).astype(BF16))
        scores = jnp.where(mask, scores, 0.0).astype(BF16)
        core = nn((q * whole[:, hk]).astype(BF16), s_low) + nn(scores, v)
        state[h] = s * keep[:, hk].reshape(KEY, 1) + tn((k * rest[:, hk]).astype(BF16), v)
        normed = core * lax.rsqrt(jnp.mean(core * core, axis=-1, keepdims=True) + 1.0)
        og = head_pick(h, og0_ref, og1_ref).astype(F32)
        hv = slice(h * VAL, (h + 1) * VAL)
        mixed = (normed * gain_ref[...] * (og * jax.nn.sigmoid(og))).astype(BF16)
        mixed_ref[:, hv] = mixed
        (mixed_a_ref if h % 2 == 0 else mixed_b_ref)[p] = mixed
        core_ref[:, hv] = core.astype(BF16)


def post_kernel(
    info, dm_ref, core_ref, og0_ref, og1_ref, q_ref, cum_ref, seg_ref, gain_ref,
    dcore_ref, dog_ref, dgain_ref, dstate_ref, prefix,
):
    c = pl.program_id(0)

    @pl.when(c == 0)
    def _():
        prefix[...] = jnp.zeros_like(prefix)
        dgain_ref[...] = jnp.zeros_like(dgain_ref)
        dstate_ref[...] = jnp.zeros_like(dstate_ref)

    running = (seg_ref[...] == info[0, 0]).astype(F32)
    cum = cum_ref[...]
    decay = jnp.exp(cum + prefix[...]) * running * SCALE
    prefix[...] += cum[CHUNK - 1 :, :]
    gain = gain_ref[...]
    total = jnp.zeros((1, VAL), F32)
    for h in range(HEADS):
        p, kc = head_cols(h, KEY)
        hk = slice(h * KEY, (h + 1) * KEY)
        hv = slice(h * VAL, (h + 1) * VAL)
        core = core_ref[:, hv].astype(F32)
        scale = lax.rsqrt(jnp.mean(core * core, axis=-1, keepdims=True) + 1.0)
        normed = core * scale
        og = head_pick(h, og0_ref, og1_ref).astype(F32)
        sig = jax.nn.sigmoid(og)
        silu = og * sig
        dm = dm_ref[:, hv].astype(F32)
        both = dm * normed
        total += jnp.sum(both * silu, axis=0, keepdims=True)
        dog_ref[p, :, head_cols(h, VAL)[1]] = (both * gain * (sig * (1.0 + og * (1.0 - sig)))).astype(BF16)
        dn = dm * gain * silu
        dcore = scale * (dn - normed * jnp.mean(dn * normed, axis=-1, keepdims=True))
        dcore = dcore.astype(BF16)
        dcore_ref[:, hv] = dcore
        qa = (q_ref[p, :, kc].astype(F32) * decay[:, hk]).astype(BF16)
        dstate_ref[h] += tn(qa, dcore)
    dgain_ref[...] += total


def back_kernel(
    info, q_ref, k_ref, v0_ref, v1_ref, dog_ref, cum_ref, sig_ref, states_ref, dcore_ref, seg_ref, row_ref,
    first_ref, second_ref, low_ref, da_ref, db_ref, drank_ref, dsecond_ref, dbias_ref, dstate,
):
    i = pl.program_id(0)
    c = pl.num_programs(0) - 1 - i

    @pl.when(i == 0)
    def _():
        dstate[...] = first_ref[...].astype(F32)
        dsecond_ref[...] = jnp.zeros_like(dsecond_ref)
        dbias_ref[...] = jnp.zeros_like(dbias_ref)

    before, last = info[0, c], info[1, c]
    seg = seg_ref[...]
    mask = triangle(True) & (seg == row_ref[0])
    upper = triangle(False).astype(F32).astype(BF16)
    running = (seg == before).astype(F32)
    tail = (seg == last).astype(F32)
    retain = (last == before).astype(F32)
    cum = cum_ref[...]
    final = cum[CHUNK - 1 :, :]
    mid = cum[CHUNK // 2 - 1 : CHUNK // 2, :]
    up, down = jnp.exp(cum - mid), jnp.exp(mid - cum)
    whole = jnp.exp(cum) * running
    rest = jnp.exp(final - cum) * tail
    keep = jnp.exp(final) * retain
    logits = []
    for h in range(HEADS):
        p, kc = head_cols(h, KEY)
        hk = slice(h * KEY, (h + 1) * KEY)
        hv = slice(h * VAL, (h + 1) * VAL)
        q = q_ref[p, :, kc].astype(F32) * SCALE
        k = k_ref[p, :, kc].astype(F32)
        v = head_pick(h, v0_ref, v1_ref)
        do = dcore_ref[:, hv]
        s = states_ref[0, h]
        ds = dstate[h]
        ds_low = ds.astype(BF16)
        q_up = (q * up[:, hk]).astype(BF16)
        k_down = (k * down[:, hk]).astype(BF16)
        q_whole = (q * whole[:, hk]).astype(BF16)
        k_rest = (k * rest[:, hk]).astype(BF16)
        scores = jnp.where(mask, nt(q_up, k_down), 0.0).astype(BF16)
        dscores = jnp.where(mask, nt(do, v), 0.0).astype(BF16)
        dq_up = nn(dscores, k_down)
        dk_down = tn(dscores, q_up)
        dq_whole = nt(do, s)
        dk_rest = nt(v, ds_low)
        dv = tn(scores, do) + nn(k_rest, ds_low)
        dq = dq_up * up[:, hk] + dq_whole * whole[:, hk]
        dk = dk_down * down[:, hk] + dk_rest * rest[:, hk]
        from_rest = k_rest.astype(F32) * dk_rest
        dcum = (
            q_up.astype(F32) * dq_up
            - k_down.astype(F32) * dk_down
            + q_whole.astype(F32) * dq_whole
            - from_rest
        )
        kept = keep[:, hk].reshape(KEY, 1)
        through = jnp.sum(s.astype(F32) * ds, axis=1, keepdims=True) * kept
        dfinal = through.reshape(1, KEY) + jnp.sum(from_rest, axis=0, keepdims=True)
        ddecay = split_sum(upper, dcum, 2) + dfinal
        dstate[h] = ds * kept + tn(q_whole, do)
        logits.append(ddecay * (sig_ref[:, hk].astype(F32) * (1.0 / 16.0)))
        da_ref[p, :, kc] = (dq * SCALE).astype(BF16)
        da_ref[p, :, slice(256 + kc.start, 256 + kc.stop)] = dk.astype(BF16)
        if h % 2 == 0:
            da_ref[p, :, 512:] = dv.astype(BF16)
        else:
            db_ref[p, :, :256] = dv.astype(BF16)
    db_ref[:, :, 256:] = dog_ref[...]
    dlogit = jnp.concatenate(logits, axis=1)
    dbias_ref[...] += jnp.sum(dlogit, axis=0, keepdims=True)
    low = dlogit.astype(BF16)
    dsecond_ref[...] += tn(low_ref[...].astype(BF16), low)
    drank_ref[...] = nt(low, second_ref[...].astype(BF16))


def rms_rows(x):
    scale = lax.rsqrt(jnp.mean(x * x, axis=-1, keepdims=True) + 1e-6)
    return x * scale, scale


def rms_rows_back(normed, scale, gain, grad):
    dn = grad * gain
    return scale * (dn - normed * jnp.mean(dn * normed, axis=-1, keepdims=True))


def output_rows(w_refs, p):
    return jnp.concatenate([ref[p] for ref in w_refs], axis=1)


def middle_kernel(mixed_ref, w0, w1, w2, w3, hidden_ref, gain_ref, middle_ref, normed_ref):
    middle = hidden_ref[...].astype(F32)
    for p in range(2):
        middle += nt(mixed_ref[:, p * 512 : (p + 1) * 512], output_rows((w0, w1, w2, w3), p))
    middle_ref[...] = middle
    normed_ref[...] = (rms_rows(middle)[0] * gain_ref[...]).astype(BF16)


def ff_kernel(normed_ref, wg_ref, wu_ref, gate_ref, up_ref, first_ref, second_ref):
    gate = nn(normed_ref[...], wg_ref[0])
    up = nn(normed_ref[...], wu_ref[0])
    gate_ref[0] = gate.astype(BF16)
    up_ref[0] = up.astype(BF16)
    activ = (gate * jax.nn.sigmoid(gate) * up).astype(BF16)
    cut = first_ref.shape[-1]
    first_ref[0] = activ[:, :cut]
    second_ref[0] = activ[:, cut:]


def ff_back_kernel(dout_ref, wd_ref, gate_ref, up_ref, dgate_ref, dup_ref):
    d_activ = nn(dout_ref[...], wd_ref[0])
    gate, up = gate_ref[0].astype(F32), up_ref[0].astype(F32)
    sig = jax.nn.sigmoid(gate)
    dgate_ref[0] = (d_activ * up * (sig * (1.0 + gate * (1.0 - sig)))).astype(BF16)
    dup_ref[0] = (d_activ * (gate * sig)).astype(BF16)


def feed_kernel(first_ref, second_ref, wd_ref, middle_ref, out_ref):
    total = middle_ref[...]
    cut = first_ref.shape[-1]
    for p in range(2):
        total += nt(first_ref[p], wd_ref[p, :, :cut]) + nt(second_ref[p], wd_ref[p, :, cut:])
    out_ref[...] = total.astype(BF16)


def middle_back_kernel(
    dgate_ref, dup_ref, wg_ref, wu_ref, w0, w1, w2, w3, middle_ref, dout_ref, gain_ref,
    dmiddle_ref, dmix_ref, dmixed_ref, dgain_ref,
):
    @pl.when(pl.program_id(0) == 0)
    def _():
        dgain_ref[...] = jnp.zeros_like(dgain_ref)

    grad = nt(dgate_ref[0], wg_ref[0]) + nt(dup_ref[0], wu_ref[0])
    grad += nt(dgate_ref[1], wg_ref[1]) + nt(dup_ref[1], wu_ref[1])
    normed, scale = rms_rows(middle_ref[...])
    dgain_ref[...] += jnp.sum(grad * normed, axis=0, keepdims=True)
    dmiddle = dout_ref[...].astype(F32) + rms_rows_back(normed, scale, gain_ref[...], grad)
    dmiddle_ref[...] = dmiddle
    dmix = dmiddle.astype(BF16)
    dmix_ref[...] = dmix
    for p in range(2):
        dmixed_ref[:, p * 512 : (p + 1) * 512] = nn(dmix, output_rows((w0, w1, w2, w3), p)).astype(BF16)


def input_back_kernel(
    da_ref, db_ref, wa_ref, wb_ref, drank_ref, first_ref, hidden_ref, dmiddle_ref, gain_ref,
    out_ref, dgain_ref,
):
    @pl.when(pl.program_id(0) == 0)
    def _():
        dgain_ref[...] = jnp.zeros_like(dgain_ref)

    grad = nt(drank_ref[...].astype(BF16), first_ref[...].astype(BF16))
    for p in range(2):
        grad += nt(da_ref[p], wa_ref[p]) + nt(db_ref[p], wb_ref[p])
    normed, scale = rms_rows(hidden_ref[...].astype(F32))
    dgain_ref[...] += jnp.sum(grad * normed, axis=0, keepdims=True)
    back = rms_rows_back(normed, scale, gain_ref[...], grad)
    out_ref[...] = (dmiddle_ref[...] + back).astype(BF16)


def grad_other_kernel(pairs, bits, *refs):
    out = refs[-1]
    rows = refs[0].shape[1] * refs[0].shape[2]
    at = 0
    for i in range(pairs):
        left, right = refs[2 * i], refs[2 * i + 1]
        cols = right.shape[-1]
        result = nn(left[0].reshape(rows, left.shape[-1]), right[0]).astype(BF16)
        out[0, :, :, at : at + cols] = result.reshape(out.shape[1], out.shape[2], cols)
        at += cols


def grad_mine_kernel(pairs, bits, *refs):
    got, send, keep = refs[2 * pairs :]
    first = pl.program_id(0) == 0
    at = 0
    for i in range(pairs):
        left, right = refs[2 * i], refs[2 * i + 1]
        cols = slice(at, at + right.shape[-1])
        at += right.shape[-1]
        result = (nn(left[0, 0], right[0]) + got[0, 0, :, cols].astype(F32)).astype(BF16)

        @pl.when(first)
        def _(result=result, cols=cols):
            send[0, :, cols] = result

        @pl.when(jnp.logical_not(first))
        def _(result=result, cols=cols):
            keep[0, :, cols] = result


def add(x, y):
    return (x.astype(F32) + y.astype(F32)).astype(BF16)


def fold_kernel(bits, ka, ga, kb, gb, sa, na, sb, nb):
    p, x = bits[2], bits[1]
    sa[...] = add(ka[1 - p], ga[1 - p])
    na[...] = add(ka[p], ga[p])
    sb[...] = add(kb[1 - x], gb[1 - x])
    nb[...] = add(kb[x], gb[x])


def join_kernel(bits, ka, ga, kb, gb, send, keep):
    z, cut = bits[3], ka.shape[-1]
    send[:, :cut] = add(ka[1 - z], ga[1 - z])
    send[:, cut:] = add(kb[1 - z], gb[1 - z])
    keep[:, :cut] = add(ka[z], ga[z])
    keep[:, cut:] = add(kb[z], gb[z])


def shape(dims, dtype):
    return jax.ShapeDtypeStruct(dims, dtype)


def call(kernel, grid, in_specs, out_specs, out_shape, scratch, cost, prefetch=1):
    grid = grid if isinstance(grid, tuple) else (grid,)
    return pl.pallas_call(
        kernel,
        grid_spec=pltpu.PrefetchScalarGridSpec(
            num_scalar_prefetch=prefetch,
            grid=grid,
            in_specs=in_specs,
            out_specs=out_specs,
            scratch_shapes=scratch,
        ),
        out_shape=out_shape,
        compiler_params=pltpu.CompilerParams(
            dimension_semantics=("arbitrary",) * len(grid), vmem_limit_bytes=VMEM_BYTES
        ),
        cost_estimate=pl.CostEstimate(flops=cost, bytes_accessed=16 << 20, transcendentals=1 << 20),
    )


def specs(blocks, backward=False):
    def at(c):
        return blocks - 1 - c if backward else c

    def proj(width, place):
        return pl.BlockSpec((2, CHUNK, width), lambda c, _: (0, at(c), place))

    def rows(width):
        return pl.BlockSpec((CHUNK, width), lambda c, _: (at(c), 0))

    def full(*dims):
        return pl.BlockSpec(dims, lambda c, _: (0,) * len(dims))

    row = pl.BlockSpec((1, 1, CHUNK), lambda c, _: (at(c), 0, 0))
    states = pl.BlockSpec((1, HEADS, KEY, VAL), lambda c, _: (at(c), 0, 0, 0))
    return proj, rows, full, row, states


def rms(x, eps):
    return x * lax.rsqrt(jnp.mean(x * x, axis=-1, keepdims=True) + eps)


def rms_back(x, gain, eps, grad):
    scale = lax.rsqrt(jnp.mean(x * x, axis=-1, keepdims=True) + eps)
    normed = x * scale
    dn = grad * gain
    back = scale * (dn - normed * jnp.mean(dn * normed, axis=-1, keepdims=True))
    return back, jnp.sum(grad * normed, axis=0)


def gather(shard):
    return lax.all_gather(shard, ALL, axis=0, tiled=True).reshape(2, -1, shard.shape[1])


def swap(x, stride):
    if stride == 0:
        return lax.ppermute(x, "tensor", [(0, 1), (1, 0)])
    return lax.ppermute(x, "dp", [(i, i ^ stride) for i in range(lax.axis_size("dp"))])


def own_bit(stride):
    return lax.axis_index("tensor") if stride == 0 else (lax.axis_index("dp") // stride) % 2


def long_strides():
    strides, stride = [], 4
    while stride < lax.axis_size("dp"):
        strides.append(stride)
        stride *= 2
    return strides


def grow(x, stride):
    other = swap(x, stride)
    return jnp.where(own_bit(stride) == 0, jnp.stack([x, other]), jnp.stack([other, x]))


def gather_steps(shard, mid):
    for stride in long_strides()[::-1] + list(mid) + [1]:
        shard = grow(shard, stride)
    steps = len(shard.shape) - 2
    z = steps - 3
    x_at, t_at = (2, 1) if mid[0] == 2 else (1, 2)
    z_axes = list(range(3, 3 + z))[::-1]
    order = [t_at] + z_axes + [x_at, 0, steps, steps + 1]
    return shard.transpose(order).reshape(2, -1, shard.shape[-1])


def owner_rows(act):
    rows = act.shape[0]
    z = len(long_strides())
    own = act.shape[1] // lax.axis_size("dp")
    split = act.reshape((rows,) + (2,) * (z + 2) + (own,))
    split = split.transpose([z + 2, z + 1] + list(range(1, z + 1))[::-1] + [z + 3, 0])
    return split.reshape(2, 2, -1, rows)


def fence(*values):
    return lax.optimization_barrier(values)


def during(sends, work, *inputs):
    arrays, inputs = fence([array for array, _ in sends], inputs)
    got = [swap(array, stride) for array, (_, stride) in zip(arrays, sends)]
    return fence(work(*inputs), got)


def grad_other(bits, pairs):
    own, rows = pairs[0][0].shape[2:]
    cols = sum(right.shape[-1] for _, right in pairs)
    in_specs = []
    for _, right in pairs:
        in_specs.append(pl.BlockSpec((1, 2, own, rows), lambda p, b: (1 - b[0], 0, 0, 0)))
        in_specs.append(pl.BlockSpec((1, rows, right.shape[-1]), lambda p, b: (p, 0, 0)))
    return call(
        functools.partial(grad_other_kernel, len(pairs)),
        2,
        in_specs,
        pl.BlockSpec((1, 2, own, cols), lambda p, b: (p, 0, 0, 0)),
        shape((2, 2, own, cols), BF16),
        [],
        8 * own * rows * cols,
    )(bits, *[array for pair in pairs for array in pair])


def grad_mine(bits, pairs, got, by_x):
    own, rows = pairs[0][0].shape[2:]
    cols = got.shape[-1]

    def x_of(s, j, b):
        return b[1] ^ 1 ^ s if by_x else j

    def p_of(s, j, b):
        return j if by_x else b[2] ^ 1 ^ s

    in_specs = []
    for _, right in pairs:
        in_specs.append(
            pl.BlockSpec((1, 1, own, rows), lambda s, j, b: (b[0], x_of(s, j, b), 0, 0))
        )
        in_specs.append(
            pl.BlockSpec((1, rows, right.shape[-1]), lambda s, j, b: (p_of(s, j, b), 0, 0))
        )
    in_specs.append(
        pl.BlockSpec((1, 1, own, cols), lambda s, j, b: (p_of(s, j, b), x_of(s, j, b), 0, 0))
    )
    return call(
        functools.partial(grad_mine_kernel, len(pairs)),
        (2, 2),
        in_specs,
        [
            pl.BlockSpec((1, own, cols), lambda s, j, b: (jnp.where(s == 0, j, 1), 0, 0)),
            pl.BlockSpec((1, own, cols), lambda s, j, b: (jnp.where(s == 0, 0, j), 0, 0)),
        ],
        [shape((2, own, cols), BF16)] * 2,
        [],
        8 * own * rows * cols,
    )(bits, *[array for pair in pairs for array in pair], got)


def whole(kernel, bits, arrays, outs):
    def spec(dims):
        return pl.BlockSpec(dims, lambda i, b: (0,) * len(dims))

    return call(
        kernel, 1, [spec(a.shape) for a in arrays], [spec(dims) for dims in outs],
        [shape(dims, BF16) for dims in outs], [], 1 << 20,
    )(bits, *arrays)


class Halving:
    def __init__(self, bits, first, second):
        self.bits, self.stage = bits, 0
        (sa, ka), (sb, kb) = first, second
        self.keep, self.out, self.cut = [ka, kb], [(sa, 2), (sb, 0)], ka.shape[-1]

    def sends(self):
        return self.out

    def receive(self, got):
        strides = long_strides()
        if self.stage == 0:
            (ka, kb), (ga, gb) = self.keep, got
            half_a, half_b = ka.shape[1:], kb.shape[1:]
            sa, na, sb, nb = whole(
                fold_kernel, self.bits, [ka, ga, kb, gb], [half_a, half_a, half_b, half_b]
            )
            self.keep, self.out = [na, nb], [(sa, 0), (sb, 2)]
        elif self.stage == 1:
            arrays = [
                a.reshape(2, -1, a.shape[-1]) for a in (self.keep[0], got[0], self.keep[1], got[1])
            ]
            dims = (arrays[0].shape[1], arrays[0].shape[2] + arrays[2].shape[2])
            send, self.keep = whole(join_kernel, self.bits, arrays, [dims, dims])
            self.out = [(send, strides[0])]
        else:
            total = self.keep + got[0]
            place = self.stage - 1
            if place < len(strides):
                total = total.reshape(2, -1, total.shape[-1])
                bit = own_bit(strides[place])
                self.keep = lax.dynamic_index_in_dim(total, bit, 0, keepdims=False)
                send = lax.dynamic_index_in_dim(total, 1 - bit, 0, keepdims=False)
                self.out = [(send, strides[place])]
            else:
                self.keep, self.out = total.astype(F32), []
        self.stage += 1

    def finish(self):
        while self.out:
            self.receive([swap(array, stride) for array, stride in self.out])
        return self.keep[:, : self.cut], self.keep[:, self.cut :]


def total_sum(x):
    x = x + swap(x, 0)
    stride = 1
    while stride < lax.axis_size("dp"):
        x = x + swap(x, stride)
        stride *= 2
    return x


def local(
    hidden_in, lengths, cotangent, query_weight, key_weight, value_weight, outgate_weight,
    output_weight, gate_weight, up_weight, down_weight, mixer_gain, feed_gain, low_first,
    low_second, decay_bias, head_gain,
):
    rows, width = hidden_in.shape
    blocks = rows // CHUNK
    place = lax.axis_index("tensor")
    half = gate_weight.shape[1]

    starts = jnp.cumsum(lengths[0]) - lengths[0]
    spots = place * rows + jnp.arange(-1, rows, dtype=jnp.int32)
    segments = jnp.sum((spots[:, None] >= starts[None, 1:]).astype(jnp.int32), axis=1)
    segments = jnp.where(spots < 0, -1, segments)
    seg = segments[1:].reshape(rows, 1)
    seg_row = segments[1:].reshape(blocks, 1, CHUNK)
    info = jnp.stack([segments[:-1].reshape(blocks, CHUNK)[:, 0], seg_row[:, 0, -1]])

    w_in_a = gather_steps(
        jnp.concatenate([query_weight, key_weight, value_weight[:, :256]], axis=1), (2, 0)
    )
    w_in_b = gather_steps(jnp.concatenate([value_weight[:, 256:], outgate_weight], axis=1), (0, 2))
    w_rest = gather(
        jnp.concatenate([gate_weight, up_weight, down_weight.T, output_weight.T], axis=1)
    )
    dp_at = lax.axis_index("dp")
    bits = jnp.stack([dp_at % 2, (dp_at // 2) % 2, place, (dp_at // 4) % 2]).astype(jnp.int32)

    resid = hidden_in.astype(F32)
    normed_a = (rms(resid, 1e-6) * mixer_gain).astype(BF16)
    proj_a = jnp.einsum("td,pdc->ptc", normed_a, w_in_a, preferred_element_type=F32).astype(BF16)
    proj_v = jnp.einsum(
        "td,pdc->ptc", normed_a, w_in_b[..., :256], preferred_element_type=F32
    ).astype(BF16)
    lowrank = jnp.dot(normed_a.astype(F32), low_first, precision=HIGHEST)
    gain = head_gain.reshape(1, VAL)
    p_spec, r_spec, f_spec, row_spec, s_spec = specs(blocks)
    state_f32 = shape((HEADS, KEY, VAL), F32)
    cum, sig, final_state = call(
        gate_kernel,
        blocks,
        [r_spec(16), f_spec(16, 512), f_spec(1, 512), p_spec(256, 1), p_spec(256, 2),
         p_spec(256, 0), r_spec(1)],
        [r_spec(512), r_spec(512), f_spec(HEADS, KEY, VAL)],
        [shape((rows, 512), F32), shape((rows, 512), BF16), state_f32],
        [],
        1 << 29,
    )(info, lowrank, low_second, decay_bias.reshape(1, 512), proj_a, proj_a, proj_v, seg)
    def outgate_product(act, weight):
        return jnp.einsum("td,pdc->ptc", act, weight, preferred_element_type=F32).astype(BF16)

    proj_og, (state_in,) = during(
        [(final_state.astype(BF16), 0)], outgate_product, normed_a, w_in_b[..., 256:]
    )
    state_in = jnp.where(place == 0, jnp.zeros_like(state_in), state_in)
    mixed, mixed_a, mixed_b, core, states = call(
        core_kernel,
        blocks,
        [p_spec(256, 0), p_spec(256, 1), p_spec(256, 2), p_spec(256, 0), p_spec(256, 0), p_spec(256, 1),
         r_spec(512), r_spec(1), row_spec, f_spec(HEADS, KEY, VAL), f_spec(1, VAL)],
        [r_spec(1024), p_spec(256, 0), p_spec(256, 0), r_spec(1024), s_spec],
        [shape((rows, 1024), BF16), shape((2, rows, 256), BF16), shape((2, rows, 256), BF16),
         shape((rows, 1024), BF16),
         shape((blocks, HEADS, KEY, VAL), BF16)],
        [pltpu.VMEM((HEADS, KEY, VAL), F32)],
        1 << 30,
    )(info, proj_a, proj_a, proj_a, proj_v, proj_og, proj_og, cum, seg, seg_row, state_in, gain)

    tiles = rows // TILE
    cut = 768
    place_out = 3 * half // 128

    def tile(cols):
        return pl.BlockSpec((TILE, cols), lambda m: (m, 0))

    def tile_pair(cols):
        return pl.BlockSpec((2, TILE, cols), lambda m: (0, m, 0))

    def keep(*dims, at=None):
        return pl.BlockSpec(dims, lambda m: at or (0,) * len(dims))

    def part(cols):
        return pl.BlockSpec((1, TILE, cols), lambda p, m: (p, m, 0))

    def part_weight(at):
        return pl.BlockSpec((1, width, half), lambda p, m: (p, 0, at))

    part_rows = pl.BlockSpec((TILE, width), lambda p, m: (m, 0))
    w_out = [keep(2, width, 128, at=(0, 0, place_out + i)) for i in range(4)]
    gain_b, gain_a = feed_gain.reshape(1, width), mixer_gain.reshape(1, width)
    middle, normed_b = call(
        middle_kernel,
        tiles,
        [tile(1024), *w_out, tile(width), keep(1, width)],
        [tile(width), tile(width)],
        [shape((rows, width), F32), shape((rows, width), BF16)],
        [],
        2 * rows * width * 1024,
        0,
    )(mixed, w_rest, w_rest, w_rest, w_rest, hidden_in, gain_b)
    wide = shape((2, rows, half), BF16)
    gate_pre, up_pre, activ_a, activ_b = call(
        ff_kernel,
        (2, tiles),
        [part_rows, part_weight(0), part_weight(1)],
        [part(half), part(half), part(cut), part(half - cut)],
        [wide, wide, shape((2, rows, cut), BF16), shape((2, rows, half - cut), BF16)],
        [],
        8 * rows * width * half,
        0,
    )(normed_b, w_rest, w_rest)

    def ff_back(dout, weight, gate_pre, up_pre):
        return call(
            ff_back_kernel,
            (2, tiles),
            [part_rows, part_weight(2), part(half), part(half)],
            [part(half), part(half)],
            [wide, wide],
            [],
            4 * rows * width * half,
            0,
        )(dout, weight, gate_pre, up_pre)

    dout_rows = owner_rows(cotangent)
    sent = [grad_other(bits, [(dout_rows, activ)]) for activ in (activ_a, activ_b)]
    (d_gate, d_up), got = during(
        [(array, 1) for array in sent], ff_back, cotangent, w_rest, gate_pre, up_pre
    )
    down = Halving(
        bits,
        grad_mine(bits, [(dout_rows, activ_a)], got[0], True),
        grad_mine(bits, [(dout_rows, activ_b)], got[1], False),
    )

    def feed_and_other(activ_a, activ_b, weight, middle, normed_rows, d_gate, d_up):
        block_out = call(
            feed_kernel,
            tiles,
            [tile_pair(cut), tile_pair(half - cut), keep(2, width, half, at=(0, 0, 2)), tile(width)],
            tile(width),
            shape((rows, width), BF16),
            [],
            4 * rows * width * half,
            0,
        )(activ_a, activ_b, weight, middle)
        return block_out, [grad_other(bits, [(normed_rows, grad)]) for grad in (d_gate, d_up)]

    normed_rows = owner_rows(normed_b)
    (block_out, sent), got = during(
        down.sends(), feed_and_other, activ_a, activ_b, w_rest, middle, normed_rows, d_gate, d_up
    )
    down.receive(got)

    def middle_back(d_gate, d_up, weight, middle, dout):
        return call(
            middle_back_kernel,
            tiles,
            [tile_pair(half), tile_pair(half), keep(2, width, half), keep(2, width, half, at=(0, 0, 1)),
             *w_out, tile(width), tile(width), keep(1, width)],
            [tile(width), tile(width), tile(1024), keep(1, width)],
            [shape((rows, width), F32), shape((rows, width), BF16), shape((rows, 1024), BF16),
             shape((1, width), F32)],
            [],
            8 * rows * width * half,
            0,
        )(d_gate, d_up, weight, weight, weight, weight, weight, weight, middle, dout, gain_b)

    (d_middle, d_mix, d_mixed, feed_gain_grad), got = during(
        [(array, 1) for array in sent] + down.sends(), middle_back, d_gate, d_up, w_rest, middle, cotangent
    )
    down.receive(got[2:])

    def mine_grads(normed_rows, d_gate, d_up, got_gate, got_up):
        return (
            grad_mine(bits, [(normed_rows, d_gate)], got_gate, True),
            grad_mine(bits, [(normed_rows, d_up)], got_up, False),
        )

    (first, second), got = during(down.sends(), mine_grads, normed_rows, d_gate, d_up, *got[:2])
    down.receive(got)
    gate_up = Halving(bits, first, second)

    p_back, r_back, f_back, row_back, s_back = specs(blocks, True)

    def mixer_back(d_mixed):
        d_core, d_og, head_gain_grad, d_state = call(
            post_kernel,
            blocks,
            [r_spec(1024), r_spec(1024), p_spec(256, 0), p_spec(256, 1), p_spec(256, 0), r_spec(512),
             r_spec(1), f_spec(1, VAL)],
            [r_spec(1024), p_spec(512, 0), f_spec(1, VAL), f_spec(HEADS, KEY, VAL)],
            [shape((rows, 1024), BF16), shape((2, rows, 512), BF16), shape((1, VAL), F32), state_f32],
            [pltpu.VMEM((1, 512), F32)],
            1 << 29,
        )(info, d_mixed, core, proj_og, proj_og, proj_a, cum, seg, gain)
        mix_rows, (d_state_in,) = during([(d_state.astype(BF16), 0)], owner_rows, d_mix)
        d_state_in = jnp.where(place == 1, jnp.zeros_like(d_state_in), d_state_in)
        d_a, d_b, d_rank, low_second_grad, bias_grad = call(
            back_kernel,
            blocks,
            [p_back(256, 0), p_back(256, 1), p_back(256, 2), p_back(256, 0), p_back(512, 0),
             r_back(512), r_back(512), s_back, r_back(1024), r_back(1), row_back,
             f_back(HEADS, KEY, VAL), f_back(16, 512), r_back(16)],
            [p_back(768, 0), p_back(768, 0), r_back(16), f_back(16, 512), f_back(1, 512)],
            [shape((2, rows, 768), BF16), shape((2, rows, 768), BF16), shape((rows, 16), F32),
             shape((16, 512), F32), shape((1, 512), F32)],
            [pltpu.VMEM((HEADS, KEY, VAL), F32)],
            3 << 30,
        )(info, proj_a, proj_a, proj_a, proj_v, d_og, cum, sig, states, d_core, seg, seg_row,
          d_state_in, low_second, lowrank)
        return mix_rows, head_gain_grad, d_a, d_b, d_rank, low_second_grad, bias_grad

    (mix_rows, head_gain_grad, d_a, d_b, d_rank, low_second_grad, bias_grad), got = during(
        gate_up.sends() + down.sends(), mixer_back, d_mixed
    )
    gate_up.receive(got[:2])
    down.receive(got[2:])
    own_down = down.finish()

    def other_mix(normed_rows, mix_rows, d_a, d_b, mixed_a, mixed_b):
        return (
            grad_other(bits, [(normed_rows, d_a), (mix_rows, mixed_a)]),
            grad_other(bits, [(normed_rows, d_b), (mix_rows, mixed_b)]),
        )

    def mine_mix(normed_rows, mix_rows, d_a, d_b, mixed_a, mixed_b, got_a, got_b):
        return (
            grad_mine(bits, [(normed_rows, d_a), (mix_rows, mixed_a)], got_a, True),
            grad_mine(bits, [(normed_rows, d_b), (mix_rows, mixed_b)], got_b, False),
        )

    mix_operands = (owner_rows(normed_a), mix_rows, d_a, d_b, mixed_a, mixed_b)
    sent, got = during(gate_up.sends(), other_mix, *mix_operands)
    gate_up.receive(got)

    def input_back(d_a, d_b, w_a, w_b, d_rank, d_middle):
        low_first_grad = tn(normed_a, d_rank.astype(BF16))
        input_grad, mixer_gain_grad = call(
            input_back_kernel,
            tiles,
            [tile_pair(768), tile_pair(768), keep(2, width, 768), keep(2, width, 768), tile(16),
             keep(width, 16), tile(width), tile(width), keep(1, width)],
            [tile(width), keep(1, width)],
            [shape((rows, width), BF16), shape((1, width), F32)],
            [],
            4 * rows * width * 1536,
            0,
        )(d_a, d_b, w_a, w_b, d_rank, low_first, hidden_in, d_middle, gain_a)
        return input_grad, mixer_gain_grad, low_first_grad

    (input_grad, mixer_gain_grad, low_first_grad), got = during(
        [(array, 1) for array in sent] + gate_up.sends(),
        input_back, d_a, d_b, w_in_a, w_in_b, d_rank, d_middle,
    )
    gate_up.receive(got[2:])
    (first, second), got = during(gate_up.sends(), mine_mix, *mix_operands, *got[:2])
    gate_up.receive(got)
    mix = Halving(bits, first, second)
    own_gate, own_up = gate_up.finish()
    own_a, own_b = mix.finish()
    own_out = [own_a[:, 768:], own_b[:, 768:]]

    parts = (mixer_gain_grad, feed_gain_grad, low_first_grad, low_second_grad, bias_grad, head_gain_grad)
    flat = total_sum(jnp.concatenate([part.reshape(-1, 128) for part in parts]))
    small, spot = [], 0
    for part, dims in zip(
        parts, ((width,), (width,), low_first.shape, low_second.shape, (512,), (VAL,))
    ):
        size = part.size // 128
        small.append(flat[spot : spot + size].reshape(dims))
        spot += size
    return (
        block_out,
        input_grad,
        own_a[:, :256],
        own_a[:, 256:512],
        jnp.concatenate([own_a[:, 512:768], own_b[:, :256]], axis=1),
        own_b[:, 256:768],
        jnp.concatenate([part.T for part in own_out], axis=0),
        own_gate,
        own_up,
        jnp.concatenate([part.T for part in own_down], axis=0),
        *small,
    )


def solution(mesh):
    tokens = P(("dp", "tensor"))
    split_in = P("dp", "tensor")
    split_out = P("tensor", "dp")
    weights = (split_in,) * 4 + (split_out,) + (split_in,) * 2 + (split_out,)
    in_specs = (tokens, P("dp", None), tokens) + weights + (P(),) * 6
    out_specs = (tokens, tokens) + weights + (P(),) * 6
    return jax.shard_map(local, mesh=mesh, in_specs=in_specs, out_specs=out_specs, check_vma=False)
```

```python
import functools

import jax
import jax.numpy as jnp
from jax import lax
from jax.experimental import pallas as pl
from jax.experimental.pallas import tpu as pltpu
from jax.sharding import PartitionSpec as P

HEADS = 4
KEY = 128
VAL = 256
CHUNK = 128
SCALE = KEY ** (-0.5)
F32 = jnp.float32
BF16 = jnp.bfloat16
HIGHEST = lax.Precision.HIGHEST
ALL = ("tensor", "dp")
VMEM_BYTES = 56 * 1024 * 1024
TILE = 256
WIDE = 512


def nn(a, b):
    return lax.dot_general(a, b, (((1,), (0,)), ((), ())), preferred_element_type=F32)


def nt(a, b):
    return lax.dot_general(a, b, (((1,), (1,)), ((), ())), preferred_element_type=F32)


def tn(a, b):
    return lax.dot_general(a, b, (((0,), (0,)), ((), ())), preferred_element_type=F32)


def triangle(lower):
    rows = lax.broadcasted_iota(jnp.int32, (CHUNK, CHUNK), 0)
    cols = lax.broadcasted_iota(jnp.int32, (CHUNK, CHUNK), 1)
    return rows >= cols if lower else rows <= cols


def split_sum(tri, x, terms):
    total = None
    for _ in range(terms):
        part = x.astype(BF16)
        x = x - part.astype(F32)
        term = nn(tri, part)
        total = term if total is None else total + term
    return total


def head_cols(h, width):
    return h // 2, slice((h % 2) * width, (h % 2 + 1) * width)


def head_pick(h, first, second):
    return (first if h % 2 == 0 else second)[h // 2]


def gate_kernel(info, low_ref, second_ref, bias_ref, k_ref, v0_ref, v1_ref, seg_ref, cum_ref, sig_ref, state_ref):
    c = pl.program_id(0)

    @pl.when(c == 0)
    def _():
        state_ref[...] = jnp.zeros_like(state_ref)

    logit = (
        jnp.dot(low_ref[...], second_ref[...], precision=HIGHEST, preferred_element_type=F32)
        + bias_ref[...]
    )
    e = jnp.exp(-jnp.abs(logit))
    decays = (jnp.minimum(logit, 0.0) - jnp.log1p(e)) * (1.0 / 16.0)
    sig_ref[...] = (jnp.where(logit >= 0, e, 1.0) / (1.0 + e)).astype(BF16)
    tri = triangle(True).astype(F32).astype(BF16)
    cum = split_sum(tri, decays, 3)
    cum_ref[...] = cum
    final = cum[CHUNK - 1 :, :]
    tail = (seg_ref[...] == info[1, c]).astype(F32)
    retain = (info[1, c] == info[0, c]).astype(F32)
    tail_decay = jnp.exp(final - cum) * tail
    keep = jnp.exp(final) * retain
    for h in range(HEADS):
        p, kc = head_cols(h, KEY)
        hk = slice(h * KEY, (h + 1) * KEY)
        kt = (k_ref[p, :, kc].astype(F32) * tail_decay[:, hk]).astype(BF16)
        state_ref[h] = state_ref[h] * keep[:, hk].reshape(KEY, 1) + tn(kt, head_pick(h, v0_ref, v1_ref))


def core_kernel(
    info, q_ref, k_ref, v0_ref, v1_ref, og0_ref, og1_ref, cum_ref, seg_ref, row_ref, first_ref, gain_ref,
    mixed_ref, mixed_a_ref, mixed_b_ref, core_ref, states_ref, state,
):
    c = pl.program_id(0)

    @pl.when(c == 0)
    def _():
        state[...] = first_ref[...].astype(F32)

    before, last = info[0, c], info[1, c]
    seg = seg_ref[...]
    mask = triangle(True) & (seg == row_ref[0])
    running = (seg == before).astype(F32)
    tail = (seg == last).astype(F32)
    retain = (last == before).astype(F32)
    cum = cum_ref[...]
    final = cum[CHUNK - 1 :, :]
    mid = cum[CHUNK // 2 - 1 : CHUNK // 2, :]
    up, down = jnp.exp(cum - mid), jnp.exp(mid - cum)
    whole = jnp.exp(cum) * running
    rest = jnp.exp(final - cum) * tail
    keep = jnp.exp(final) * retain
    for h in range(HEADS):
        p, kc = head_cols(h, KEY)
        hk = slice(h * KEY, (h + 1) * KEY)
        q = q_ref[p, :, kc].astype(F32) * SCALE
        k = k_ref[p, :, kc].astype(F32)
        v = head_pick(h, v0_ref, v1_ref)
        s = state[h]
        s_low = s.astype(BF16)
        states_ref[0, h] = s_low
        scores = nt((q * up[:, hk]).astype(BF16), (k * down[:, hk]).astype(BF16))
        scores = jnp.where(mask, scores, 0.0).astype(BF16)
        core = nn((q * whole[:, hk]).astype(BF16), s_low) + nn(scores, v)
        state[h] = s * keep[:, hk].reshape(KEY, 1) + tn((k * rest[:, hk]).astype(BF16), v)
        normed = core * lax.rsqrt(jnp.mean(core * core, axis=-1, keepdims=True) + 1.0)
        og = head_pick(h, og0_ref, og1_ref).astype(F32)
        hv = slice(h * VAL, (h + 1) * VAL)
        mixed = (normed * gain_ref[...] * (og * jax.nn.sigmoid(og))).astype(BF16)
        mixed_ref[:, hv] = mixed
        (mixed_a_ref if h % 2 == 0 else mixed_b_ref)[p] = mixed
        core_ref[:, hv] = core.astype(BF16)


def post_kernel(
    info, dm_ref, core_ref, og0_ref, og1_ref, q_ref, cum_ref, seg_ref, gain_ref,
    dcore_ref, dog_ref, dgain_ref, dstate_ref, prefix,
):
    c = pl.program_id(0)

    @pl.when(c == 0)
    def _():
        prefix[...] = jnp.zeros_like(prefix)
        dgain_ref[...] = jnp.zeros_like(dgain_ref)
        dstate_ref[...] = jnp.zeros_like(dstate_ref)

    running = (seg_ref[...] == info[0, 0]).astype(F32)
    cum = cum_ref[...]
    decay = jnp.exp(cum + prefix[...]) * running * SCALE
    prefix[...] += cum[CHUNK - 1 :, :]
    gain = gain_ref[...]
    total = jnp.zeros((1, VAL), F32)
    for h in range(HEADS):
        p, kc = head_cols(h, KEY)
        hk = slice(h * KEY, (h + 1) * KEY)
        hv = slice(h * VAL, (h + 1) * VAL)
        core = core_ref[:, hv].astype(F32)
        scale = lax.rsqrt(jnp.mean(core * core, axis=-1, keepdims=True) + 1.0)
        normed = core * scale
        og = head_pick(h, og0_ref, og1_ref).astype(F32)
        sig = jax.nn.sigmoid(og)
        silu = og * sig
        dm = dm_ref[:, hv].astype(F32)
        both = dm * normed
        total += jnp.sum(both * silu, axis=0, keepdims=True)
        dog_ref[p, :, head_cols(h, VAL)[1]] = (both * gain * (sig * (1.0 + og * (1.0 - sig)))).astype(BF16)
        dn = dm * gain * silu
        dcore = scale * (dn - normed * jnp.mean(dn * normed, axis=-1, keepdims=True))
        dcore = dcore.astype(BF16)
        dcore_ref[:, hv] = dcore
        qa = (q_ref[p, :, kc].astype(F32) * decay[:, hk]).astype(BF16)
        dstate_ref[h] += tn(qa, dcore)
    dgain_ref[...] += total


def back_kernel(
    info, q_ref, k_ref, v0_ref, v1_ref, dog_ref, cum_ref, sig_ref, states_ref, dcore_ref, seg_ref, row_ref,
    first_ref, second_ref, low_ref, da_ref, db_ref, drank_ref, dsecond_ref, dbias_ref, dstate,
):
    i = pl.program_id(0)
    c = pl.num_programs(0) - 1 - i

    @pl.when(i == 0)
    def _():
        dstate[...] = first_ref[...].astype(F32)
        dsecond_ref[...] = jnp.zeros_like(dsecond_ref)
        dbias_ref[...] = jnp.zeros_like(dbias_ref)

    before, last = info[0, c], info[1, c]
    seg = seg_ref[...]
    mask = triangle(True) & (seg == row_ref[0])
    upper = triangle(False).astype(F32).astype(BF16)
    running = (seg == before).astype(F32)
    tail = (seg == last).astype(F32)
    retain = (last == before).astype(F32)
    cum = cum_ref[...]
    final = cum[CHUNK - 1 :, :]
    mid = cum[CHUNK // 2 - 1 : CHUNK // 2, :]
    up, down = jnp.exp(cum - mid), jnp.exp(mid - cum)
    whole = jnp.exp(cum) * running
    rest = jnp.exp(final - cum) * tail
    keep = jnp.exp(final) * retain
    logits = []
    for h in range(HEADS):
        p, kc = head_cols(h, KEY)
        hk = slice(h * KEY, (h + 1) * KEY)
        hv = slice(h * VAL, (h + 1) * VAL)
        q = q_ref[p, :, kc].astype(F32) * SCALE
        k = k_ref[p, :, kc].astype(F32)
        v = head_pick(h, v0_ref, v1_ref)
        do = dcore_ref[:, hv]
        s = states_ref[0, h]
        ds = dstate[h]
        ds_low = ds.astype(BF16)
        q_up = (q * up[:, hk]).astype(BF16)
        k_down = (k * down[:, hk]).astype(BF16)
        q_whole = (q * whole[:, hk]).astype(BF16)
        k_rest = (k * rest[:, hk]).astype(BF16)
        scores = jnp.where(mask, nt(q_up, k_down), 0.0).astype(BF16)
        dscores = jnp.where(mask, nt(do, v), 0.0).astype(BF16)
        dq_up = nn(dscores, k_down)
        dk_down = tn(dscores, q_up)
        dq_whole = nt(do, s)
        dk_rest = nt(v, ds_low)
        dv = tn(scores, do) + nn(k_rest, ds_low)
        dq = dq_up * up[:, hk] + dq_whole * whole[:, hk]
        dk = dk_down * down[:, hk] + dk_rest * rest[:, hk]
        from_rest = k_rest.astype(F32) * dk_rest
        dcum = (
            q_up.astype(F32) * dq_up
            - k_down.astype(F32) * dk_down
            + q_whole.astype(F32) * dq_whole
            - from_rest
        )
        kept = keep[:, hk].reshape(KEY, 1)
        through = jnp.sum(s.astype(F32) * ds, axis=1, keepdims=True) * kept
        dfinal = through.reshape(1, KEY) + jnp.sum(from_rest, axis=0, keepdims=True)
        ddecay = split_sum(upper, dcum, 2) + dfinal
        dstate[h] = ds * kept + tn(q_whole, do)
        logits.append(ddecay * (sig_ref[:, hk].astype(F32) * (1.0 / 16.0)))
        da_ref[p, :, kc] = (dq * SCALE).astype(BF16)
        da_ref[p, :, slice(256 + kc.start, 256 + kc.stop)] = dk.astype(BF16)
        if h % 2 == 0:
            da_ref[p, :, 512:] = dv.astype(BF16)
        else:
            db_ref[p, :, :256] = dv.astype(BF16)
    db_ref[:, :, 256:] = dog_ref[...]
    dlogit = jnp.concatenate(logits, axis=1)
    dbias_ref[...] += jnp.sum(dlogit, axis=0, keepdims=True)
    low = dlogit.astype(BF16)
    dsecond_ref[...] += tn(low_ref[...].astype(BF16), low)
    drank_ref[...] = nt(low, second_ref[...].astype(BF16))


def rms_rows(x):
    scale = lax.rsqrt(jnp.mean(x * x, axis=-1, keepdims=True) + 1e-6)
    return x * scale, scale


def rms_rows_back(normed, scale, gain, grad):
    dn = grad * gain
    return scale * (dn - normed * jnp.mean(dn * normed, axis=-1, keepdims=True))


def output_rows(w_refs, p):
    return jnp.concatenate([ref[p] for ref in w_refs], axis=1)


def middle_kernel(mixed_ref, w0, w1, w2, w3, hidden_ref, gain_ref, middle_ref, normed_ref, cols_ref):
    middle = hidden_ref[...].astype(F32)
    for p in range(2):
        middle += nt(mixed_ref[:, p * 512 : (p + 1) * 512], output_rows((w0, w1, w2, w3), p))
    middle_ref[...] = middle
    normed = (rms_rows(middle)[0] * gain_ref[...]).astype(BF16)
    normed_ref[...] = normed
    cols_ref[...] = normed.T


def ff_kernel(normed_ref, wg_ref, wu_ref, gate_ref, up_ref, first_ref, second_ref):
    gate = nn(normed_ref[...], wg_ref[0])
    up = nn(normed_ref[...], wu_ref[0])
    gate_ref[0] = gate.astype(BF16)
    up_ref[0] = up.astype(BF16)
    activ = (gate * jax.nn.sigmoid(gate) * up).astype(BF16)
    cut = first_ref.shape[-1]
    first_ref[0] = activ[:, :cut]
    second_ref[0] = activ[:, cut:]


def ff_back_kernel(dout_ref, wd_ref, gate_ref, up_ref, dgate_ref, dup_ref):
    d_activ = nn(dout_ref[...], wd_ref[0])
    gate, up = gate_ref[0].astype(F32), up_ref[0].astype(F32)
    sig = jax.nn.sigmoid(gate)
    dgate_ref[0] = (d_activ * up * (sig * (1.0 + gate * (1.0 - sig)))).astype(BF16)
    dup_ref[0] = (d_activ * (gate * sig)).astype(BF16)


def feed_kernel(first_ref, second_ref, wd_ref, middle_ref, out_ref, total):
    p, m = pl.program_id(0), pl.program_id(1)
    cut = first_ref.shape[-1]
    part = nt(first_ref[0], wd_ref[0, :, :cut]) + nt(second_ref[0], wd_ref[0, :, cut:])

    @pl.when(p == 0)
    def _():
        total[m] = part

    @pl.when(p == 1)
    def _():
        out_ref[...] = (middle_ref[...] + total[m] + part).astype(BF16)


def middle_back_kernel(
    dgate_ref, dup_ref, wg_ref, wu_ref, w0, w1, w2, w3, middle_ref, dout_ref, gain_ref,
    dmiddle_ref, dmix_ref, cols_ref, dmixed_ref, dgain_ref, total,
):
    p, m = pl.program_id(0), pl.program_id(1)
    part = nt(dgate_ref[0], wg_ref[0]) + nt(dup_ref[0], wu_ref[0])

    @pl.when((p == 0) & (m == 0))
    def _():
        dgain_ref[...] = jnp.zeros_like(dgain_ref)

    @pl.when(p == 0)
    def _():
        total[m] = part

    @pl.when(p == 1)
    def _():
        grad = total[m] + part
        normed, scale = rms_rows(middle_ref[...])
        dgain_ref[...] += jnp.sum(grad * normed, axis=0, keepdims=True)
        dmiddle = dout_ref[...].astype(F32) + rms_rows_back(normed, scale, gain_ref[...], grad)
        dmiddle_ref[...] = dmiddle
        dmix = dmiddle.astype(BF16)
        dmix_ref[...] = dmix
        cols_ref[...] = dmix.T
        for q in range(2):
            dmixed_ref[:, q * 512 : (q + 1) * 512] = nn(
                dmix, output_rows((w0, w1, w2, w3), q)
            ).astype(BF16)


def input_back_kernel(
    da_ref, db_ref, wa_ref, wb_ref, drank_ref, first_ref, hidden_ref, dmiddle_ref, gain_ref,
    out_ref, dgain_ref,
):
    @pl.when(pl.program_id(0) == 0)
    def _():
        dgain_ref[...] = jnp.zeros_like(dgain_ref)

    grad = nt(drank_ref[...].astype(BF16), first_ref[...].astype(BF16))
    for p in range(2):
        grad += nt(da_ref[p], wa_ref[p]) + nt(db_ref[p], wb_ref[p])
    normed, scale = rms_rows(hidden_ref[...].astype(F32))
    dgain_ref[...] += jnp.sum(grad * normed, axis=0, keepdims=True)
    back = rms_rows_back(normed, scale, gain_ref[...], grad)
    out_ref[...] = (dmiddle_ref[...] + back).astype(BF16)


def grad_other_kernel(counts, bits, *refs):
    outs = refs[2 * sum(counts) :]
    rows = refs[0].shape[1] * refs[0].shape[2]
    i = 0
    for count, out in zip(counts, outs):
        at = 0
        for _ in range(count):
            left, right = refs[2 * i], refs[2 * i + 1]
            cols = right.shape[-1]
            result = nn(left[0].reshape(rows, left.shape[-1]), right[0]).astype(BF16)
            out[0, :, :, at : at + cols] = result.reshape(out.shape[1], out.shape[2], cols)
            at += cols
            i += 1


def grad_mine_kernel(counts, bits, *refs):
    got_a, got_b, send_a, keep_a, send_b, keep_b = refs[2 * sum(counts) :]
    own = send_a.shape[1]
    step, x = pl.program_id(0), bits[1]
    at = 0
    for i in range(counts[0]):
        left, right = refs[2 * i], refs[2 * i + 1]
        cols = slice(at, at + right.shape[-1])
        at += right.shape[-1]
        result = nn(left[0].reshape(2 * own, left.shape[-1]), right[0])
        low = (result[:own] + got_a[0, 0, :, cols].astype(F32)).astype(BF16)
        high = (result[own:] + got_a[0, 1, :, cols].astype(F32)).astype(BF16)

        @pl.when(x == 0)
        def _(low=low, high=high, cols=cols):
            send_a[0, :, cols] = high
            keep_a[0, :, cols] = low

        @pl.when(x == 1)
        def _(low=low, high=high, cols=cols):
            send_a[0, :, cols] = low
            keep_a[0, :, cols] = high

    at = 0
    for i in range(counts[0], sum(counts)):
        left, right = refs[2 * i], refs[2 * i + 1]
        cols = slice(at, at + right.shape[-1])
        at += right.shape[-1]
        result = nn(left[0].reshape(2 * own, left.shape[-1]), right[0])
        low = (result[:own] + got_b[0, 0, :, cols].astype(F32)).astype(BF16)
        high = (result[own:] + got_b[0, 1, :, cols].astype(F32)).astype(BF16)

        @pl.when(step == 0)
        def _(low=low, high=high, cols=cols):
            send_b[0, :, cols] = low
            send_b[1, :, cols] = high

        @pl.when(step == 1)
        def _(low=low, high=high, cols=cols):
            keep_b[0, :, cols] = low
            keep_b[1, :, cols] = high


def add(x, y):
    return (x.astype(F32) + y.astype(F32)).astype(BF16)


def fold_kernel(bits, ka, ga, kb, gb, sa, na, sb, nb):
    p, x = bits[2], bits[1]
    sa[...] = add(ka[1 - p], ga[1 - p])
    na[...] = add(ka[p], ga[p])
    sb[...] = add(kb[1 - x], gb[1 - x])
    nb[...] = add(kb[x], gb[x])


def join_kernel(bits, ka, ga, kb, gb, send, keep):
    z, cut = bits[3], ka.shape[-1]
    send[:, :cut] = add(ka[1 - z], ga[1 - z])
    send[:, cut:] = add(kb[1 - z], gb[1 - z])
    keep[:, :cut] = add(ka[z], ga[z])
    keep[:, cut:] = add(kb[z], gb[z])


def shape(dims, dtype):
    return jax.ShapeDtypeStruct(dims, dtype)


def call(kernel, grid, in_specs, out_specs, out_shape, scratch, cost, prefetch=1):
    grid = grid if isinstance(grid, tuple) else (grid,)
    return pl.pallas_call(
        kernel,
        grid_spec=pltpu.PrefetchScalarGridSpec(
            num_scalar_prefetch=prefetch,
            grid=grid,
            in_specs=in_specs,
            out_specs=out_specs,
            scratch_shapes=scratch,
        ),
        out_shape=out_shape,
        compiler_params=pltpu.CompilerParams(
            dimension_semantics=("arbitrary",) * len(grid), vmem_limit_bytes=VMEM_BYTES
        ),
        cost_estimate=pl.CostEstimate(flops=cost, bytes_accessed=16 << 20, transcendentals=1 << 20),
    )


def specs(blocks, backward=False):
    def at(c):
        return blocks - 1 - c if backward else c

    def proj(width, place):
        return pl.BlockSpec((2, CHUNK, width), lambda c, _: (0, at(c), place))

    def rows(width):
        return pl.BlockSpec((CHUNK, width), lambda c, _: (at(c), 0))

    def full(*dims):
        return pl.BlockSpec(dims, lambda c, _: (0,) * len(dims))

    row = pl.BlockSpec((1, 1, CHUNK), lambda c, _: (at(c), 0, 0))
    states = pl.BlockSpec((1, HEADS, KEY, VAL), lambda c, _: (at(c), 0, 0, 0))
    return proj, rows, full, row, states


def rms(x, eps):
    return x * lax.rsqrt(jnp.mean(x * x, axis=-1, keepdims=True) + eps)


def rms_back(x, gain, eps, grad):
    scale = lax.rsqrt(jnp.mean(x * x, axis=-1, keepdims=True) + eps)
    normed = x * scale
    dn = grad * gain
    back = scale * (dn - normed * jnp.mean(dn * normed, axis=-1, keepdims=True))
    return back, jnp.sum(grad * normed, axis=0)


def gather(shard):
    return lax.all_gather(shard, ALL, axis=0, tiled=True).reshape(2, -1, shard.shape[1])


def swap(x, stride):
    if stride == 0:
        return lax.ppermute(x, "tensor", [(0, 1), (1, 0)])
    return lax.ppermute(x, "dp", [(i, i ^ stride) for i in range(lax.axis_size("dp"))])


def own_bit(stride):
    return lax.axis_index("tensor") if stride == 0 else (lax.axis_index("dp") // stride) % 2


def long_strides():
    strides, stride = [], 4
    while stride < lax.axis_size("dp"):
        strides.append(stride)
        stride *= 2
    return strides


def grow(x, stride):
    other = swap(x, stride)
    return jnp.where(own_bit(stride) == 0, jnp.stack([x, other]), jnp.stack([other, x]))


def gather_steps(shard, mid):
    for stride in long_strides()[::-1] + list(mid) + [1]:
        shard = grow(shard, stride)
    steps = len(shard.shape) - 2
    z = steps - 3
    x_at, t_at = (2, 1) if mid[0] == 2 else (1, 2)
    z_axes = list(range(3, 3 + z))[::-1]
    order = [t_at] + z_axes + [x_at, 0, steps, steps + 1]
    return shard.transpose(order).reshape(2, -1, shard.shape[-1])


def owner_rows(cols):
    count, rows = cols.shape
    z = len(long_strides())
    own = count // lax.axis_size("dp")
    split = cols.reshape((2,) * (z + 2) + (own, rows))
    split = split.transpose([z + 1, z] + list(range(z))[::-1] + [z + 2, z + 3])
    return split.reshape(2, 2, -1, rows)


class HopSum:
    def __init__(self, x):
        self.x, self.strides = x, [0, 1, 2] + long_strides()

    def sends(self):
        return [(self.x, self.strides[0])] if self.strides else []

    def receive(self, got):
        if self.strides:
            self.x = self.x + got[0]
            self.strides = self.strides[1:]

    def finish(self):
        while self.strides:
            self.receive([swap(array, stride) for array, stride in self.sends()])
        return self.x


def in_flight(movers, work, *inputs, also=()):
    sends = [mover.sends() for mover in movers]
    flat = [pair for group in sends for pair in group] + list(also)
    result, got = during(flat, work, *inputs)
    at = 0
    for mover, group in zip(movers, sends):
        mover.receive(got[at : at + len(group)])
        at += len(group)
    return result, got[at:]


def fence(*values):
    return lax.optimization_barrier(values)


def during(sends, work, *inputs):
    arrays, inputs = fence([array for array, _ in sends], inputs)
    got = [swap(array, stride) for array, (_, stride) in zip(arrays, sends)]
    return fence(work(*inputs), got)


def grad_other(bits, first, second):
    own, rows = first[0][0].shape[2:]
    in_specs, dims = [], []
    for half in (first, second):
        dims.append((2, 2, own, sum(right.shape[-1] for _, right in half)))
        for _, right in half:
            in_specs.append(pl.BlockSpec((1, 2, own, rows), lambda p, b: (1 - b[0], 0, 0, 0)))
            in_specs.append(pl.BlockSpec((1, rows, right.shape[-1]), lambda p, b: (p, 0, 0)))
    return call(
        functools.partial(grad_other_kernel, (len(first), len(second))),
        2,
        in_specs,
        [pl.BlockSpec((1,) + d[1:], lambda p, b: (p, 0, 0, 0)) for d in dims],
        [shape(d, BF16) for d in dims],
        [],
        8 * own * rows * (dims[0][3] + dims[1][3]),
    )(bits, *[array for half in (first, second) for pair in half for array in pair])


def grad_mine(bits, first, second, got):
    own, rows = first[0][0].shape[2:]
    cols_a, cols_b = got[0].shape[-1], got[1].shape[-1]

    def other_first(s, b):
        return b[2] ^ 1 ^ s

    left = pl.BlockSpec((1, 2, own, rows), lambda s, b: (b[0], 0, 0, 0))
    in_specs = []
    for _, right in first:
        in_specs += [left, pl.BlockSpec((1, rows, right.shape[-1]), lambda s, b: (s, 0, 0))]
    for _, right in second:
        in_specs += [
            left,
            pl.BlockSpec((1, rows, right.shape[-1]), lambda s, b: (other_first(s, b), 0, 0)),
        ]
    in_specs.append(pl.BlockSpec((1, 2, own, cols_a), lambda s, b: (s, 0, 0, 0)))
    in_specs.append(pl.BlockSpec((1, 2, own, cols_b), lambda s, b: (other_first(s, b), 0, 0, 0)))
    by_p = pl.BlockSpec((1, own, cols_a), lambda s, b: (s, 0, 0))
    fixed = pl.BlockSpec((2, own, cols_b), lambda s, b: (0, 0, 0))
    send_a, keep_a, send_b, keep_b = call(
        functools.partial(grad_mine_kernel, (len(first), len(second))),
        2,
        in_specs,
        [by_p, by_p, fixed, fixed],
        [shape((2, own, cols_a), BF16)] * 2 + [shape((2, own, cols_b), BF16)] * 2,
        [],
        8 * own * rows * (cols_a + cols_b),
    )(bits, *[array for half in (first, second) for pair in half for array in pair], *got)
    return (send_a, keep_a), (send_b, keep_b)


def whole(kernel, bits, arrays, outs):
    def spec(dims):
        return pl.BlockSpec(dims, lambda i, b: (0,) * len(dims))

    return call(
        kernel, 1, [spec(a.shape) for a in arrays], [spec(dims) for dims in outs],
        [shape(dims, BF16) for dims in outs], [], 1 << 20,
    )(bits, *arrays)


class Halving:
    def __init__(self, bits, first, second):
        self.bits, self.stage = bits, 0
        (sa, ka), (sb, kb) = first, second
        self.keep, self.out, self.cut = [ka, kb], [(sa, 2), (sb, 0)], ka.shape[-1]

    def sends(self):
        return self.out

    def receive(self, got):
        if not self.out:
            return
        strides = long_strides()
        if self.stage == 0:
            (ka, kb), (ga, gb) = self.keep, got
            half_a, half_b = ka.shape[1:], kb.shape[1:]
            sa, na, sb, nb = whole(
                fold_kernel, self.bits, [ka, ga, kb, gb], [half_a, half_a, half_b, half_b]
            )
            self.keep, self.out = [na, nb], [(sa, 0), (sb, 2)]
        elif self.stage == 1:
            arrays = [
                a.reshape(2, -1, a.shape[-1]) for a in (self.keep[0], got[0], self.keep[1], got[1])
            ]
            dims = (arrays[0].shape[1], arrays[0].shape[2] + arrays[2].shape[2])
            send, self.keep = whole(join_kernel, self.bits, arrays, [dims, dims])
            self.out = [(send, strides[0])]
        else:
            total = self.keep + got[0]
            place = self.stage - 1
            if place < len(strides):
                total = total.reshape(2, -1, total.shape[-1])
                bit = own_bit(strides[place])
                self.keep = lax.dynamic_index_in_dim(total, bit, 0, keepdims=False)
                send = lax.dynamic_index_in_dim(total, 1 - bit, 0, keepdims=False)
                self.out = [(send, strides[place])]
            else:
                self.keep, self.out = total.astype(F32), []
        self.stage += 1

    def finish(self):
        while self.out:
            in_flight([self], lambda: ())
        return self.keep[:, : self.cut], self.keep[:, self.cut :]


def local(
    hidden_in, lengths, cotangent, query_weight, key_weight, value_weight, outgate_weight,
    output_weight, gate_weight, up_weight, down_weight, mixer_gain, feed_gain, low_first,
    low_second, decay_bias, head_gain,
):
    rows, width = hidden_in.shape
    blocks = rows // CHUNK
    place = lax.axis_index("tensor")
    half = gate_weight.shape[1]

    starts = jnp.cumsum(lengths[0]) - lengths[0]
    spots = place * rows + jnp.arange(-1, rows, dtype=jnp.int32)
    segments = jnp.sum((spots[:, None] >= starts[None, 1:]).astype(jnp.int32), axis=1)
    segments = jnp.where(spots < 0, -1, segments)
    seg = segments[1:].reshape(rows, 1)
    seg_row = segments[1:].reshape(blocks, 1, CHUNK)
    info = jnp.stack([segments[:-1].reshape(blocks, CHUNK)[:, 0], seg_row[:, 0, -1]])

    w_in_a = gather_steps(
        jnp.concatenate([query_weight, key_weight, value_weight[:, :256]], axis=1), (2, 0)
    )
    w_in_b = gather_steps(jnp.concatenate([value_weight[:, 256:], outgate_weight], axis=1), (0, 2))
    w_rest = gather(
        jnp.concatenate([gate_weight, up_weight, down_weight.T, output_weight.T], axis=1)
    )
    dp_at = lax.axis_index("dp")
    dout_rows = owner_rows(cotangent.T)
    bits = jnp.stack([dp_at % 2, (dp_at // 2) % 2, place, (dp_at // 4) % 2]).astype(jnp.int32)

    resid = hidden_in.astype(F32)
    normed_a = (rms(resid, 1e-6) * mixer_gain).astype(BF16)
    normed_a_rows = owner_rows(normed_a.T)
    proj_a = jnp.einsum("td,pdc->ptc", normed_a, w_in_a, preferred_element_type=F32).astype(BF16)
    proj_v = jnp.einsum(
        "td,pdc->ptc", normed_a, w_in_b[..., :256], preferred_element_type=F32
    ).astype(BF16)
    lowrank = jnp.dot(normed_a.astype(F32), low_first, precision=HIGHEST)
    gain = head_gain.reshape(1, VAL)
    p_spec, r_spec, f_spec, row_spec, s_spec = specs(blocks)
    state_f32 = shape((HEADS, KEY, VAL), F32)
    cum, sig, final_state = call(
        gate_kernel,
        blocks,
        [r_spec(16), f_spec(16, 512), f_spec(1, 512), p_spec(256, 1), p_spec(256, 2),
         p_spec(256, 0), r_spec(1)],
        [r_spec(512), r_spec(512), f_spec(HEADS, KEY, VAL)],
        [shape((rows, 512), F32), shape((rows, 512), BF16), state_f32],
        [],
        1 << 29,
    )(info, lowrank, low_second, decay_bias.reshape(1, 512), proj_a, proj_a, proj_v, seg)
    def outgate_product(act, weight):
        return jnp.einsum("td,pdc->ptc", act, weight, preferred_element_type=F32).astype(BF16)

    proj_og, (state_in,) = during(
        [(final_state.astype(BF16), 0)], outgate_product, normed_a, w_in_b[..., 256:]
    )
    state_in = jnp.where(place == 0, jnp.zeros_like(state_in), state_in)
    mixed, mixed_a, mixed_b, core, states = call(
        core_kernel,
        blocks,
        [p_spec(256, 0), p_spec(256, 1), p_spec(256, 2), p_spec(256, 0), p_spec(256, 0), p_spec(256, 1),
         r_spec(512), r_spec(1), row_spec, f_spec(HEADS, KEY, VAL), f_spec(1, VAL)],
        [r_spec(1024), p_spec(256, 0), p_spec(256, 0), r_spec(1024), s_spec],
        [shape((rows, 1024), BF16), shape((2, rows, 256), BF16), shape((2, rows, 256), BF16),
         shape((rows, 1024), BF16),
         shape((blocks, HEADS, KEY, VAL), BF16)],
        [pltpu.VMEM((HEADS, KEY, VAL), F32)],
        1 << 30,
    )(info, proj_a, proj_a, proj_a, proj_v, proj_og, proj_og, cum, seg, seg_row, state_in, gain)

    tiles, wides = rows // TILE, rows // WIDE
    cut = 768
    place_out = 3 * half // 128

    def tile(cols, size=TILE):
        return pl.BlockSpec((size, cols), lambda m: (m, 0))

    def tile_pair(cols, size=TILE):
        return pl.BlockSpec((2, size, cols), lambda m: (0, m, 0))

    def keep(*dims, at=None):
        return pl.BlockSpec(dims, lambda *_: at or (0,) * len(dims))

    def part(cols):
        return pl.BlockSpec((1, WIDE, cols), lambda p, m: (p, m, 0))

    def part_weight(at):
        return pl.BlockSpec((1, width, half), lambda p, m: (p, 0, at))

    part_rows = pl.BlockSpec((WIDE, width), lambda p, m: (m, 0))
    late_rows = pl.BlockSpec((WIDE, width), lambda p, m: (p * m, 0))
    late_cols = pl.BlockSpec((width, WIDE), lambda p, m: (0, p * m))
    w_out = [keep(2, width, 128, at=(0, 0, place_out + i)) for i in range(4)]
    gain_b, gain_a = feed_gain.reshape(1, width), mixer_gain.reshape(1, width)
    middle, normed_b, normed_b_cols = call(
        middle_kernel,
        tiles,
        [tile(1024), *w_out, tile(width), keep(1, width)],
        [tile(width), tile(width), pl.BlockSpec((width, TILE), lambda m: (0, m))],
        [shape((rows, width), F32), shape((rows, width), BF16), shape((width, rows), BF16)],
        [],
        2 * rows * width * 1024,
        0,
    )(mixed, w_rest, w_rest, w_rest, w_rest, hidden_in, gain_b)
    wide = shape((2, rows, half), BF16)
    gate_pre, up_pre, activ_a, activ_b = call(
        ff_kernel,
        (2, wides),
        [part_rows, part_weight(0), part_weight(1)],
        [part(half), part(half), part(cut), part(half - cut)],
        [wide, wide, shape((2, rows, cut), BF16), shape((2, rows, half - cut), BF16)],
        [],
        8 * rows * width * half,
        0,
    )(normed_b, w_rest, w_rest)

    def ff_back(dout, weight, gate_pre, up_pre):
        return call(
            ff_back_kernel,
            (2, wides),
            [part_rows, part_weight(2), part(half), part(half)],
            [part(half), part(half)],
            [wide, wide],
            [],
            4 * rows * width * half,
            0,
        )(dout, weight, gate_pre, up_pre)

    down_pairs = [(dout_rows, activ_a)], [(dout_rows, activ_b)]
    sent = grad_other(bits, *down_pairs)
    (d_gate, d_up), got = in_flight(
        [], ff_back, cotangent, w_rest, gate_pre, up_pre, also=[(array, 1) for array in sent]
    )
    down = Halving(bits, *grad_mine(bits, *down_pairs, got))

    def other_gate_up(normed_cols, d_gate, d_up):
        normed_rows = owner_rows(normed_cols)
        return normed_rows, grad_other(bits, [(normed_rows, d_gate)], [(normed_rows, d_up)])

    (normed_rows, sent), _ = in_flight([down], other_gate_up, normed_b_cols, d_gate, d_up)

    def middle_back(d_gate, d_up, weight, middle, dout):
        return call(
            middle_back_kernel,
            (2, wides),
            [part(half), part(half), part_weight(0), part_weight(1), *w_out, late_rows, late_rows,
             keep(1, width)],
            [late_rows, late_rows, late_cols, late_rows, keep(1, width)],
            [shape((rows, width), F32), shape((rows, width), BF16), shape((width, rows), BF16),
             shape((rows, 1024), BF16), shape((1, width), F32)],
            [pltpu.VMEM((wides, WIDE, width), F32)],
            8 * rows * width * half,
            0,
        )(d_gate, d_up, weight, weight, weight, weight, weight, weight, middle, dout, gain_b)

    (d_middle, d_mix, d_mix_cols, d_mixed, feed_gain_grad), got = in_flight(
        [down], middle_back, d_gate, d_up, w_rest, middle, cotangent,
        also=[(array, 1) for array in sent],
    )

    d_core, d_og, head_gain_grad, d_state = call(
        post_kernel,
        blocks,
        [r_spec(1024), r_spec(1024), p_spec(256, 0), p_spec(256, 1), p_spec(256, 0), r_spec(512),
         r_spec(1), f_spec(1, VAL)],
        [r_spec(1024), p_spec(512, 0), f_spec(1, VAL), f_spec(HEADS, KEY, VAL)],
        [shape((rows, 1024), BF16), shape((2, rows, 512), BF16), shape((1, VAL), F32), state_f32],
        [pltpu.VMEM((1, 512), F32)],
        1 << 29,
    )(info, d_mixed, core, proj_og, proj_og, proj_a, cum, seg, gain)

    def mine_gate_up(normed_rows, d_gate, d_up, d_mix_cols, *got):
        mix_rows = owner_rows(d_mix_cols)
        return mix_rows, grad_mine(bits, [(normed_rows, d_gate)], [(normed_rows, d_up)], got)

    (mix_rows, halves), (d_state_in,) = in_flight(
        [down], mine_gate_up, normed_rows, d_gate, d_up, d_mix_cols, *got,
        also=[(d_state.astype(BF16), 0)],
    )
    gate_up = Halving(bits, *halves)
    d_state_in = jnp.where(place == 1, jnp.zeros_like(d_state_in), d_state_in)
    p_back, r_back, f_back, row_back, s_back = specs(blocks, True)

    def mixer_back(d_core, d_og, d_state_in, normed_rows, mix_rows, mixed_a, mixed_b):
        d_a, d_b, d_rank, low_second_grad, bias_grad = call(
            back_kernel,
            blocks,
            [p_back(256, 0), p_back(256, 1), p_back(256, 2), p_back(256, 0), p_back(512, 0),
             r_back(512), r_back(512), s_back, r_back(1024), r_back(1), row_back,
             f_back(HEADS, KEY, VAL), f_back(16, 512), r_back(16)],
            [p_back(768, 0), p_back(768, 0), r_back(16), f_back(16, 512), f_back(1, 512)],
            [shape((2, rows, 768), BF16), shape((2, rows, 768), BF16), shape((rows, 16), F32),
             shape((16, 512), F32), shape((1, 512), F32)],
            [pltpu.VMEM((HEADS, KEY, VAL), F32)],
            3 << 30,
        )(info, proj_a, proj_a, proj_a, proj_v, d_og, cum, sig, states, d_core, seg, seg_row,
          d_state_in, low_second, lowrank)
        sent = grad_other(
            bits, [(normed_rows, d_a), (mix_rows, mixed_a)], [(normed_rows, d_b), (mix_rows, mixed_b)]
        )
        low_first_grad = tn(normed_a, d_rank.astype(BF16))
        return d_a, d_b, d_rank, low_first_grad, low_second_grad, bias_grad, sent

    (d_a, d_b, d_rank, low_first_grad, low_second_grad, bias_grad, sent), _ = in_flight(
        [gate_up, down], mixer_back, d_core, d_og, d_state_in, normed_a_rows, mix_rows, mixed_a, mixed_b
    )
    own_down = down.finish()
    parts = (feed_gain_grad, low_first_grad, low_second_grad, bias_grad, head_gain_grad)
    small_sum = HopSum(jnp.concatenate([part.reshape(-1, 128) for part in parts]))

    def input_back(d_a, d_b, w_a, w_b, d_rank, d_middle):
        return call(
            input_back_kernel,
            wides,
            [tile_pair(768, WIDE), tile_pair(768, WIDE), keep(2, width, 768), keep(2, width, 768),
             tile(16, WIDE), keep(width, 16), tile(width, WIDE), tile(width, WIDE), keep(1, width)],
            [tile(width, WIDE), keep(1, width)],
            [shape((rows, width), BF16), shape((1, width), F32)],
            [],
            4 * rows * width * 1536,
            0,
        )(d_a, d_b, w_a, w_b, d_rank, low_first, hidden_in, d_middle, gain_a)

    (input_grad, mixer_gain_grad), got = in_flight(
        [gate_up, small_sum], input_back, d_a, d_b, w_in_a, w_in_b, d_rank, d_middle,
        also=[(array, 1) for array in sent],
    )
    gain_sum = HopSum(mixer_gain_grad.reshape(-1, 128))

    def mine_mix(normed_rows, mix_rows, d_a, d_b, mixed_a, mixed_b, *got):
        return grad_mine(
            bits, [(normed_rows, d_a), (mix_rows, mixed_a)],
            [(normed_rows, d_b), (mix_rows, mixed_b)], got,
        )

    halves, _ = in_flight(
        [gate_up, small_sum, gain_sum], mine_mix, normed_a_rows, mix_rows, d_a, d_b, mixed_a, mixed_b, *got
    )
    mix = Halving(bits, *halves)

    def feed_out(activ_a, activ_b, weight, middle):
        return call(
            feed_kernel,
            (2, wides),
            [part(cut), part(half - cut), part_weight(2), late_rows],
            late_rows,
            shape((rows, width), BF16),
            [pltpu.VMEM((wides, WIDE, width), F32)],
            4 * rows * width * half,
            0,
        )(activ_a, activ_b, weight, middle)

    block_out, _ = in_flight(
        [mix, gate_up, small_sum, gain_sum], feed_out, activ_a, activ_b, w_rest, middle
    )
    while mix.out:
        in_flight([mix, gate_up, small_sum, gain_sum], lambda: ())
    own_gate, own_up = gate_up.finish()
    own_a, own_b = mix.finish()
    own_out = [own_a[:, 768:], own_b[:, 768:]]

    flat = small_sum.finish()
    small, spot = [gain_sum.finish().reshape(width)], 0
    for part, dims in zip(parts, ((width,), low_first.shape, low_second.shape, (512,), (VAL,))):
        size = part.size // 128
        small.append(flat[spot : spot + size].reshape(dims))
        spot += size
    return (
        block_out,
        input_grad,
        own_a[:, :256],
        own_a[:, 256:512],
        jnp.concatenate([own_a[:, 512:768], own_b[:, :256]], axis=1),
        own_b[:, 256:768],
        jnp.concatenate([part.T for part in own_out], axis=0),
        own_gate,
        own_up,
        jnp.concatenate([part.T for part in own_down], axis=0),
        *small,
    )


def solution(mesh):
    tokens = P(("dp", "tensor"))
    split_in = P("dp", "tensor")
    split_out = P("tensor", "dp")
    weights = (split_in,) * 4 + (split_out,) + (split_in,) * 2 + (split_out,)
    in_specs = (tokens, P("dp", None), tokens) + weights + (P(),) * 6
    out_specs = (tokens, tokens) + weights + (P(),) * 6
    return jax.shard_map(local, mesh=mesh, in_specs=in_specs, out_specs=out_specs, check_vma=False)
```

```python
import functools

import jax
import jax.numpy as jnp
from jax import lax
from jax.experimental import pallas as pl
from jax.experimental.pallas import tpu as pltpu
from jax.sharding import PartitionSpec as P

HEADS = 4
KEY = 128
VAL = 256
CHUNK = 128
SCALE = KEY ** (-0.5)
F32 = jnp.float32
BF16 = jnp.bfloat16
HIGHEST = lax.Precision.HIGHEST
ALL = ("tensor", "dp")
VMEM_BYTES = 56 * 1024 * 1024
TILE = 256
WIDE = 512


def nn(a, b):
    return lax.dot_general(a, b, (((1,), (0,)), ((), ())), preferred_element_type=F32)


def nt(a, b):
    return lax.dot_general(a, b, (((1,), (1,)), ((), ())), preferred_element_type=F32)


def tn(a, b):
    return lax.dot_general(a, b, (((0,), (0,)), ((), ())), preferred_element_type=F32)


def triangle(lower):
    rows = lax.broadcasted_iota(jnp.int32, (CHUNK, CHUNK), 0)
    cols = lax.broadcasted_iota(jnp.int32, (CHUNK, CHUNK), 1)
    return rows >= cols if lower else rows <= cols


def split_sum(tri, x, terms):
    total = None
    for _ in range(terms):
        part = x.astype(BF16)
        x = x - part.astype(F32)
        term = nn(tri, part)
        total = term if total is None else total + term
    return total


def head_cols(h, width):
    return h // 2, slice((h % 2) * width, (h % 2 + 1) * width)


def head_pick(h, first, second):
    return (first if h % 2 == 0 else second)[h // 2]


def gate_kernel(info, low_ref, second_ref, bias_ref, k_ref, v0_ref, v1_ref, seg_ref, cum_ref, sig_ref, state_ref):
    c = pl.program_id(0)

    @pl.when(c == 0)
    def _():
        state_ref[...] = jnp.zeros_like(state_ref)

    logit = (
        jnp.dot(low_ref[...], second_ref[...], precision=HIGHEST, preferred_element_type=F32)
        + bias_ref[...]
    )
    e = jnp.exp(-jnp.abs(logit))
    decays = (jnp.minimum(logit, 0.0) - jnp.log1p(e)) * (1.0 / 16.0)
    sig_ref[...] = (jnp.where(logit >= 0, e, 1.0) / (1.0 + e)).astype(BF16)
    tri = triangle(True).astype(F32).astype(BF16)
    cum = split_sum(tri, decays, 3)
    cum_ref[...] = cum
    final = cum[CHUNK - 1 :, :]
    tail = (seg_ref[...] == info[1, c]).astype(F32)
    retain = (info[1, c] == info[0, c]).astype(F32)
    tail_decay = jnp.exp(final - cum) * tail
    keep = jnp.exp(final) * retain
    for h in range(HEADS):
        p, kc = head_cols(h, KEY)
        hk = slice(h * KEY, (h + 1) * KEY)
        kt = (k_ref[p, :, kc].astype(F32) * tail_decay[:, hk]).astype(BF16)
        state_ref[h] = state_ref[h] * keep[:, hk].reshape(KEY, 1) + tn(kt, head_pick(h, v0_ref, v1_ref))


def core_kernel(
    info, q_ref, k_ref, v0_ref, v1_ref, og0_ref, og1_ref, cum_ref, seg_ref, row_ref, first_ref, gain_ref,
    mixed_ref, core_ref, states_ref, state,
):
    c = pl.program_id(0)

    @pl.when(c == 0)
    def _():
        state[...] = first_ref[...].astype(F32)

    before, last = info[0, c], info[1, c]
    seg = seg_ref[...]
    mask = triangle(True) & (seg == row_ref[0])
    running = (seg == before).astype(F32)
    tail = (seg == last).astype(F32)
    retain = (last == before).astype(F32)
    cum = cum_ref[...]
    final = cum[CHUNK - 1 :, :]
    mid = cum[CHUNK // 2 - 1 : CHUNK // 2, :]
    up, down = jnp.exp(cum - mid), jnp.exp(mid - cum)
    whole = jnp.exp(cum) * running
    rest = jnp.exp(final - cum) * tail
    keep = jnp.exp(final) * retain
    for h in range(HEADS):
        p, kc = head_cols(h, KEY)
        hk = slice(h * KEY, (h + 1) * KEY)
        q = q_ref[p, :, kc].astype(F32) * SCALE
        k = k_ref[p, :, kc].astype(F32)
        v = head_pick(h, v0_ref, v1_ref)
        s = state[h]
        s_low = s.astype(BF16)
        states_ref[0, h] = s_low
        scores = nt((q * up[:, hk]).astype(BF16), (k * down[:, hk]).astype(BF16))
        scores = jnp.where(mask, scores, 0.0).astype(BF16)
        core = nn((q * whole[:, hk]).astype(BF16), s_low) + nn(scores, v)
        state[h] = s * keep[:, hk].reshape(KEY, 1) + tn((k * rest[:, hk]).astype(BF16), v)
        normed = core * lax.rsqrt(jnp.mean(core * core, axis=-1, keepdims=True) + 1.0)
        og = head_pick(h, og0_ref, og1_ref).astype(F32)
        hv = slice(h * VAL, (h + 1) * VAL)
        mixed = normed * gain_ref[...] * (og * jax.nn.sigmoid(og))
        mixed_ref[p, :, head_cols(h, VAL)[1]] = mixed.astype(BF16)
        core_ref[:, hv] = core.astype(BF16)


def post_kernel(
    info, dm_ref, core_ref, og0_ref, og1_ref, q_ref, cum_ref, seg_ref, gain_ref,
    dcore_ref, dog_ref, dgain_ref, dstate_ref, prefix,
):
    c = pl.program_id(0)

    @pl.when(c == 0)
    def _():
        prefix[...] = jnp.zeros_like(prefix)
        dgain_ref[...] = jnp.zeros_like(dgain_ref)
        dstate_ref[...] = jnp.zeros_like(dstate_ref)

    running = (seg_ref[...] == info[0, 0]).astype(F32)
    cum = cum_ref[...]
    decay = jnp.exp(cum + prefix[...]) * running * SCALE
    prefix[...] += cum[CHUNK - 1 :, :]
    gain = gain_ref[...]
    total = jnp.zeros((1, VAL), F32)
    for h in range(HEADS):
        p, kc = head_cols(h, KEY)
        hk = slice(h * KEY, (h + 1) * KEY)
        hv = slice(h * VAL, (h + 1) * VAL)
        core = core_ref[:, hv].astype(F32)
        scale = lax.rsqrt(jnp.mean(core * core, axis=-1, keepdims=True) + 1.0)
        normed = core * scale
        og = head_pick(h, og0_ref, og1_ref).astype(F32)
        sig = jax.nn.sigmoid(og)
        silu = og * sig
        dm = dm_ref[:, hv].astype(F32)
        both = dm * normed
        total += jnp.sum(both * silu, axis=0, keepdims=True)
        dog_ref[p, :, head_cols(h, VAL)[1]] = (both * gain * (sig * (1.0 + og * (1.0 - sig)))).astype(BF16)
        dn = dm * gain * silu
        dcore = scale * (dn - normed * jnp.mean(dn * normed, axis=-1, keepdims=True))
        dcore = dcore.astype(BF16)
        dcore_ref[:, hv] = dcore
        qa = (q_ref[p, :, kc].astype(F32) * decay[:, hk]).astype(BF16)
        dstate_ref[h] += tn(qa, dcore)
    dgain_ref[...] += total


def back_kernel(
    info, q_ref, k_ref, v0_ref, v1_ref, cum_ref, sig_ref, states_ref, dcore_ref, seg_ref, row_ref,
    first_ref, second_ref, low_ref, dqk_ref, dv_ref, drank_ref, dsecond_ref, dbias_ref, dstate,
):
    i = pl.program_id(0)
    c = pl.num_programs(0) - 1 - i

    @pl.when(i == 0)
    def _():
        dstate[...] = first_ref[...].astype(F32)
        dsecond_ref[...] = jnp.zeros_like(dsecond_ref)
        dbias_ref[...] = jnp.zeros_like(dbias_ref)

    before, last = info[0, c], info[1, c]
    seg = seg_ref[...]
    mask = triangle(True) & (seg == row_ref[0])
    upper = triangle(False).astype(F32).astype(BF16)
    running = (seg == before).astype(F32)
    tail = (seg == last).astype(F32)
    retain = (last == before).astype(F32)
    cum = cum_ref[...]
    final = cum[CHUNK - 1 :, :]
    mid = cum[CHUNK // 2 - 1 : CHUNK // 2, :]
    up, down = jnp.exp(cum - mid), jnp.exp(mid - cum)
    whole = jnp.exp(cum) * running
    rest = jnp.exp(final - cum) * tail
    keep = jnp.exp(final) * retain
    logits = []
    for h in range(HEADS):
        p, kc = head_cols(h, KEY)
        hk = slice(h * KEY, (h + 1) * KEY)
        hv = slice(h * VAL, (h + 1) * VAL)
        q = q_ref[p, :, kc].astype(F32) * SCALE
        k = k_ref[p, :, kc].astype(F32)
        v = head_pick(h, v0_ref, v1_ref)
        do = dcore_ref[:, hv]
        s = states_ref[0, h]
        ds = dstate[h]
        ds_low = ds.astype(BF16)
        q_up = (q * up[:, hk]).astype(BF16)
        k_down = (k * down[:, hk]).astype(BF16)
        q_whole = (q * whole[:, hk]).astype(BF16)
        k_rest = (k * rest[:, hk]).astype(BF16)
        scores = jnp.where(mask, nt(q_up, k_down), 0.0).astype(BF16)
        dscores = jnp.where(mask, nt(do, v), 0.0).astype(BF16)
        dq_up = nn(dscores, k_down)
        dk_down = tn(dscores, q_up)
        dq_whole = nt(do, s)
        dk_rest = nt(v, ds_low)
        dv = tn(scores, do) + nn(k_rest, ds_low)
        dq = dq_up * up[:, hk] + dq_whole * whole[:, hk]
        dk = dk_down * down[:, hk] + dk_rest * rest[:, hk]
        from_rest = k_rest.astype(F32) * dk_rest
        dcum = (
            q_up.astype(F32) * dq_up
            - k_down.astype(F32) * dk_down
            + q_whole.astype(F32) * dq_whole
            - from_rest
        )
        kept = keep[:, hk].reshape(KEY, 1)
        through = jnp.sum(s.astype(F32) * ds, axis=1, keepdims=True) * kept
        dfinal = through.reshape(1, KEY) + jnp.sum(from_rest, axis=0, keepdims=True)
        ddecay = split_sum(upper, dcum, 2) + dfinal
        dstate[h] = ds * kept + tn(q_whole, do)
        logits.append(ddecay * (sig_ref[:, hk].astype(F32) * (1.0 / 16.0)))
        dqk_ref[p, :, kc] = (dq * SCALE).astype(BF16)
        dqk_ref[p, :, slice(256 + kc.start, 256 + kc.stop)] = dk.astype(BF16)
        dv_ref[p, :, head_cols(h, VAL)[1]] = dv.astype(BF16)
    dlogit = jnp.concatenate(logits, axis=1)
    dbias_ref[...] += jnp.sum(dlogit, axis=0, keepdims=True)
    low = dlogit.astype(BF16)
    dsecond_ref[...] += tn(low_ref[...].astype(BF16), low)
    drank_ref[...] = nt(low, second_ref[...].astype(BF16))


def rms_rows(x):
    scale = lax.rsqrt(jnp.mean(x * x, axis=-1, keepdims=True) + 1e-6)
    return x * scale, scale


def rms_rows_back(normed, scale, gain, grad):
    dn = grad * gain
    return scale * (dn - normed * jnp.mean(dn * normed, axis=-1, keepdims=True))


def output_rows(w_refs, p):
    return jnp.concatenate([ref[p] for ref in w_refs], axis=1)


def middle_kernel(mixed_ref, w0, w1, w2, w3, hidden_ref, gain_ref, middle_ref, normed_ref, cols_ref):
    middle = hidden_ref[...].astype(F32)
    for p in range(2):
        middle += nt(mixed_ref[p], output_rows((w0, w1, w2, w3), p))
    middle_ref[...] = middle
    normed = (rms_rows(middle)[0] * gain_ref[...]).astype(BF16)
    normed_ref[...] = normed
    cols_ref[...] = normed.T


def ff_kernel(normed_ref, dout_ref, wg_ref, wu_ref, wd_ref, first_ref, second_ref, dpre_ref):
    gate = nn(normed_ref[...], wg_ref[0])
    up = nn(normed_ref[...], wu_ref[0])
    sig = jax.nn.sigmoid(gate)
    silu = gate * sig
    activ = (silu * up).astype(BF16)
    cut = first_ref.shape[-1]
    first_ref[0] = activ[:, :cut]
    second_ref[0] = activ[:, cut:]
    d_activ = nn(dout_ref[...], wd_ref[0])
    dpre_ref[0, 0] = (d_activ * up * (sig * (1.0 + gate * (1.0 - sig)))).astype(BF16)
    dpre_ref[1, 0] = (d_activ * silu).astype(BF16)


def feed_kernel(first_ref, second_ref, wd_ref, middle_ref, out_ref, total):
    p, m = pl.program_id(0), pl.program_id(1)
    cut = first_ref.shape[-1]
    part = nt(first_ref[0], wd_ref[0, :, :cut]) + nt(second_ref[0], wd_ref[0, :, cut:])

    @pl.when(p == 0)
    def _():
        total[m] = part

    @pl.when(p == 1)
    def _():
        out_ref[...] = (middle_ref[...] + total[m] + part).astype(BF16)


def middle_back_kernel(
    dpre_ref, wg_ref, wu_ref, w0, w1, w2, w3, middle_ref, dout_ref, gain_ref,
    dmiddle_ref, dmix_ref, cols_ref, dmixed_ref, dgain_ref, total,
):
    p, m = pl.program_id(0), pl.program_id(1)
    part = nt(dpre_ref[0, 0], wg_ref[0]) + nt(dpre_ref[1, 0], wu_ref[0])

    @pl.when((p == 0) & (m == 0))
    def _():
        dgain_ref[...] = jnp.zeros_like(dgain_ref)

    @pl.when(p == 0)
    def _():
        total[m] = part

    @pl.when(p == 1)
    def _():
        grad = total[m] + part
        normed, scale = rms_rows(middle_ref[...])
        dgain_ref[...] += jnp.sum(grad * normed, axis=0, keepdims=True)
        dmiddle = dout_ref[...].astype(F32) + rms_rows_back(normed, scale, gain_ref[...], grad)
        dmiddle_ref[...] = dmiddle
        dmix = dmiddle.astype(BF16)
        dmix_ref[...] = dmix
        cols_ref[...] = dmix.T
        for q in range(2):
            dmixed_ref[:, q * 512 : (q + 1) * 512] = nn(
                dmix, output_rows((w0, w1, w2, w3), q)
            ).astype(BF16)


def input_back_kernel(
    dqk_ref, dv_ref, dog_ref, wa_ref, wb_ref, drank_ref, first_ref, hidden_ref, dmiddle_ref, gain_ref,
    out_ref, dgain_ref,
):
    @pl.when(pl.program_id(0) == 0)
    def _():
        dgain_ref[...] = jnp.zeros_like(dgain_ref)

    grad = nt(drank_ref[...].astype(BF16), first_ref[...].astype(BF16))
    for p in range(2):
        grad += nt(dqk_ref[p], wa_ref[p, :, :512]) + nt(dv_ref[p, :, :256], wa_ref[p, :, 512:])
        grad += nt(dv_ref[p, :, 256:], wb_ref[p, :, :256]) + nt(dog_ref[p], wb_ref[p, :, 256:])
    normed, scale = rms_rows(hidden_ref[...].astype(F32))
    dgain_ref[...] += jnp.sum(grad * normed, axis=0, keepdims=True)
    back = rms_rows_back(normed, scale, gain_ref[...], grad)
    out_ref[...] = (dmiddle_ref[...] + back).astype(BF16)


def grad_other_kernel(stacked, bits, *refs):
    out_a, out_b = refs[-2:]
    step = pl.program_id(0)
    for place, out in enumerate((out_a, out_b)):
        left, right = refs[:2] if stacked else refs[2 * place : 2 * place + 2]

        @pl.when(step // 2 == place)
        def _(left=left, right=right, out=out):
            rows, cols = left.shape[1] * left.shape[2], right.shape[-1]
            result = nn(left[0].reshape(rows, left.shape[-1]), right[...].reshape(-1, cols))
            out[0] = result.astype(BF16).reshape(out.shape[1:])


def grad_mine_kernel(stacked, bits, *refs):
    got_a, got_b, send_a, keep_a, send_b, keep_b = refs[-6:]
    step, x = pl.program_id(0), bits[1]
    own = send_a.shape[1]

    def result(left, right, got):
        cols = right.shape[-1]
        both = nn(left[0].reshape(2 * own, left.shape[-1]), right[...].reshape(-1, cols))
        low = (both[:own] + got[0, 0].astype(F32)).astype(BF16)
        high = (both[own:] + got[0, 1].astype(F32)).astype(BF16)
        return low, high

    @pl.when(step < 2)
    def _():
        low, high = result(refs[0], refs[1], got_a)

        @pl.when(x == 0)
        def _():
            send_a[0] = high
            keep_a[0] = low

        @pl.when(x == 1)
        def _():
            send_a[0] = low
            keep_a[0] = high

    @pl.when(step >= 2)
    def _():
        low, high = result(*(refs[:2] if stacked else refs[2:4]), got_b)

        @pl.when(step == 2)
        def _():
            send_b[0] = low
            send_b[1] = high

        @pl.when(step == 3)
        def _():
            keep_b[0] = low
            keep_b[1] = high


def add(x, y):
    return (x.astype(F32) + y.astype(F32)).astype(BF16)


def fold_kernel(bits, ka, ga, kb, gb, sa, na, sb, nb):
    p, x = bits[2], bits[1]
    sa[...] = add(ka[1 - p], ga[1 - p])
    na[...] = add(ka[p], ga[p])
    sb[...] = add(kb[1 - x], gb[1 - x])
    nb[...] = add(kb[x], gb[x])


def join_kernel(bits, ka, ga, kb, gb, send, keep):
    z, cut = bits[3], ka.shape[-1]
    send[:, :cut] = add(ka[1 - z], ga[1 - z])
    send[:, cut:] = add(kb[1 - z], gb[1 - z])
    keep[:, :cut] = add(ka[z], ga[z])
    keep[:, cut:] = add(kb[z], gb[z])


def shape(dims, dtype):
    return jax.ShapeDtypeStruct(dims, dtype)


def call(kernel, grid, in_specs, out_specs, out_shape, scratch, cost, prefetch=1):
    grid = grid if isinstance(grid, tuple) else (grid,)
    return pl.pallas_call(
        kernel,
        grid_spec=pltpu.PrefetchScalarGridSpec(
            num_scalar_prefetch=prefetch,
            grid=grid,
            in_specs=in_specs,
            out_specs=out_specs,
            scratch_shapes=scratch,
        ),
        out_shape=out_shape,
        compiler_params=pltpu.CompilerParams(
            dimension_semantics=("arbitrary",) * len(grid), vmem_limit_bytes=VMEM_BYTES
        ),
        cost_estimate=pl.CostEstimate(flops=cost, bytes_accessed=16 << 20, transcendentals=1 << 20),
    )


def specs(blocks, backward=False):
    def at(c):
        return blocks - 1 - c if backward else c

    def proj(width, place):
        return pl.BlockSpec((2, CHUNK, width), lambda c, _: (0, at(c), place))

    def rows(width):
        return pl.BlockSpec((CHUNK, width), lambda c, _: (at(c), 0))

    def full(*dims):
        return pl.BlockSpec(dims, lambda c, _: (0,) * len(dims))

    row = pl.BlockSpec((1, 1, CHUNK), lambda c, _: (at(c), 0, 0))
    states = pl.BlockSpec((1, HEADS, KEY, VAL), lambda c, _: (at(c), 0, 0, 0))
    return proj, rows, full, row, states


def rms(x, eps):
    return x * lax.rsqrt(jnp.mean(x * x, axis=-1, keepdims=True) + eps)


def rms_back(x, gain, eps, grad):
    scale = lax.rsqrt(jnp.mean(x * x, axis=-1, keepdims=True) + eps)
    normed = x * scale
    dn = grad * gain
    back = scale * (dn - normed * jnp.mean(dn * normed, axis=-1, keepdims=True))
    return back, jnp.sum(grad * normed, axis=0)


def gather(shard):
    return lax.all_gather(shard, ALL, axis=0, tiled=True).reshape(2, -1, shard.shape[1])


def swap(x, stride):
    if isinstance(stride, tuple):
        places = 2 * lax.axis_size("dp")
        return lax.ppermute(x, ("dp", "tensor"), [(i, i ^ stride[1]) for i in range(places)])
    if stride == 0:
        return lax.ppermute(x, "tensor", [(0, 1), (1, 0)])
    return lax.ppermute(x, "dp", [(i, i ^ stride) for i in range(lax.axis_size("dp"))])


def own_bit(stride):
    return lax.axis_index("tensor") if stride == 0 else (lax.axis_index("dp") // stride) % 2


def long_strides():
    strides, stride = [], 4
    while stride < lax.axis_size("dp"):
        strides.append(stride)
        stride *= 2
    return strides


def in_place(x, mid):
    steps = len(x.shape) - 2
    x_at, t_at = (2, 1) if mid[0] == 2 else (1, 2)
    z_axes = list(range(3, steps))[::-1]
    order = [t_at] + z_axes + [x_at, 0, steps, steps + 1]
    return x.transpose(order).reshape(2, -1, x.shape[-1])


def owner_rows(cols):
    count, rows = cols.shape
    z = len(long_strides())
    own = count // lax.axis_size("dp")
    split = cols.reshape((2,) * (z + 2) + (own, rows))
    split = split.transpose([z + 1, z] + list(range(z))[::-1] + [z + 2, z + 3])
    return split.reshape(2, 2, -1, rows)


class HopSum:
    def __init__(self, x):
        bits = [2 * stride for stride in long_strides()[::-1]] + [4, 1, 2]
        self.x, self.hops = x, [bits[i : i + 2] for i in range(0, len(bits), 2)]

    def sends(self):
        if not self.hops:
            return []
        hop = self.hops[0]
        return [(self.x, ("all", mask)) for mask in (hop if len(hop) == 1 else [*hop, sum(hop)])]

    def receive(self, got):
        if self.hops:
            self.x = self.x + sum(got)
            self.hops = self.hops[1:]

    def finish(self):
        while self.hops:
            in_flight([self], lambda: ())
        return self.x


class Growing:
    def __init__(self, x, strides):
        self.x, self.strides = x, list(strides)

    def sends(self):
        return [(self.x, self.strides[0])]

    def receive(self, got):
        bit, self.strides = own_bit(self.strides[0]), self.strides[1:]
        low, high = jnp.stack([self.x, got[0]]), jnp.stack([got[0], self.x])
        self.x = jnp.where(bit == 0, low, high)


def in_flight(movers, work, *inputs, also=()):
    sends = [mover.sends() for mover in movers]
    flat = [pair for group in sends for pair in group] + list(also)
    result, got = during(flat, work, *inputs)
    at = 0
    for mover, group in zip(movers, sends):
        mover.receive(got[at : at + len(group)])
        at += len(group)
    return result, got[at:]


def fence(*values):
    return lax.optimization_barrier(values)


def during(sends, work, *inputs):
    arrays, inputs = fence([array for array, _ in sends], inputs)
    got = [swap(array, stride) for array, (_, stride) in zip(arrays, sends)]
    return fence(work(*inputs), got)


def half_specs(pairs, core, second_part):
    specs, operands = [], []
    for place, (left, right) in enumerate(pairs):
        own, rows = left.shape[2:]
        specs.append(pl.BlockSpec((1, 2, own, rows), lambda s, b: (core(b), 0, 0, 0)))
        cols = right.shape[-1]

        def part(s, b, place=place):
            return jnp.minimum(s, 1) if place == 0 else second_part(jnp.maximum(s - 2, 0), b)

        if len(pairs) == 1:

            def at(s, b):
                return s // 2, jnp.where(s < 2, s, second_part(s - 2, b)), 0, 0

            specs.append(pl.BlockSpec((1, 1, rows, cols), at))
        else:
            specs.append(pl.BlockSpec((1, rows, cols), lambda s, b, part=part: (part(s, b), 0, 0)))
        operands += [left, right]
    return specs, operands


def grad_other(bits, *pairs):
    in_specs, operands = half_specs(pairs, lambda b: 1 - b[0], lambda s, b: s)
    own, rows = pairs[0][0].shape[2:]
    dims = [(2, 2, own, pairs[0][1].shape[-1]), (2, 2, own, pairs[-1][1].shape[-1])]
    return call(
        functools.partial(grad_other_kernel, len(pairs) == 1),
        4,
        in_specs,
        [
            pl.BlockSpec((1,) + dims[0][1:], lambda s, b: (jnp.minimum(s, 1), 0, 0, 0)),
            pl.BlockSpec((1,) + dims[1][1:], lambda s, b: (jnp.maximum(s - 2, 0), 0, 0, 0)),
        ],
        [shape(d, BF16) for d in dims],
        [],
        8 * own * rows * (dims[0][3] + dims[1][3]),
    )(bits, *operands)


def grad_mine(bits, pairs, got):
    def other_first(s, b):
        return b[2] ^ 1 ^ s

    in_specs, operands = half_specs(pairs, lambda b: b[0], other_first)
    own, rows = pairs[0][0].shape[2:]
    cols_a, cols_b = got[0].shape[-1], got[1].shape[-1]
    in_specs.append(
        pl.BlockSpec((1, 2, own, cols_a), lambda s, b: (jnp.minimum(s, 1), 0, 0, 0))
    )
    in_specs.append(
        pl.BlockSpec(
            (1, 2, own, cols_b), lambda s, b: (other_first(jnp.maximum(s - 2, 0), b), 0, 0, 0)
        )
    )
    by_p = pl.BlockSpec((1, own, cols_a), lambda s, b: (jnp.minimum(s, 1), 0, 0))
    fixed = pl.BlockSpec((2, own, cols_b), lambda s, b: (0, 0, 0))
    send_a, keep_a, send_b, keep_b = call(
        functools.partial(grad_mine_kernel, len(pairs) == 1),
        4,
        in_specs,
        [by_p, by_p, fixed, fixed],
        [shape((2, own, cols_a), BF16)] * 2 + [shape((2, own, cols_b), BF16)] * 2,
        [],
        8 * own * rows * (cols_a + cols_b),
    )(bits, *operands, *got)
    return (send_a, keep_a), (send_b, keep_b)


def whole(kernel, bits, arrays, outs):
    def spec(dims):
        return pl.BlockSpec(dims, lambda i, b: (0,) * len(dims))

    return call(
        kernel, 1, [spec(a.shape) for a in arrays], [spec(dims) for dims in outs],
        [shape(dims, BF16) for dims in outs], [], 1 << 20,
    )(bits, *arrays)


class Halving:
    def __init__(self, bits, first, second):
        self.bits, self.stage = bits, 0
        (sa, ka), (sb, kb) = first, second
        self.keep, self.out, self.cut = [ka, kb], [(sa, 2), (sb, 0)], ka.shape[-1]

    def sends(self):
        return self.out

    def receive(self, got):
        if not self.out:
            return
        strides = long_strides()
        if self.stage == 0:
            (ka, kb), (ga, gb) = self.keep, got
            half_a, half_b = ka.shape[1:], kb.shape[1:]
            sa, na, sb, nb = whole(
                fold_kernel, self.bits, [ka, ga, kb, gb], [half_a, half_a, half_b, half_b]
            )
            self.keep, self.out = [na, nb], [(sa, 0), (sb, 2)]
        elif self.stage == 1:
            arrays = [
                a.reshape(2, -1, a.shape[-1]) for a in (self.keep[0], got[0], self.keep[1], got[1])
            ]
            dims = (arrays[0].shape[1], arrays[0].shape[2] + arrays[2].shape[2])
            send, self.keep = whole(join_kernel, self.bits, arrays, [dims, dims])
            self.out = [(send, strides[0])]
        else:
            total = self.keep + got[0]
            place = self.stage - 1
            if place < len(strides):
                total = total.reshape(2, -1, total.shape[-1])
                bit = own_bit(strides[place])
                self.keep = lax.dynamic_index_in_dim(total, bit, 0, keepdims=False)
                send = lax.dynamic_index_in_dim(total, 1 - bit, 0, keepdims=False)
                self.out = [(send, strides[place])]
            else:
                self.keep, self.out = total.astype(F32), []
        self.stage += 1

    def finish(self):
        while self.out:
            in_flight([self], lambda: ())
        return self.keep[:, : self.cut], self.keep[:, self.cut :]


def local(
    hidden_in, lengths, cotangent, query_weight, key_weight, value_weight, outgate_weight,
    output_weight, gate_weight, up_weight, down_weight, mixer_gain, feed_gain, low_first,
    low_second, decay_bias, head_gain,
):
    rows, width = hidden_in.shape
    blocks = rows // CHUNK
    place = lax.axis_index("tensor")
    half = gate_weight.shape[1]

    starts = jnp.cumsum(lengths[0]) - lengths[0]
    spots = place * rows + jnp.arange(-1, rows, dtype=jnp.int32)
    segments = jnp.sum((spots[:, None] >= starts[None, 1:]).astype(jnp.int32), axis=1)
    segments = jnp.where(spots < 0, -1, segments)
    seg = segments[1:].reshape(rows, 1)
    seg_row = segments[1:].reshape(blocks, 1, CHUNK)
    info = jnp.stack([segments[:-1].reshape(blocks, CHUNK)[:, 0], seg_row[:, 0, -1]])

    w_rest = gather(
        jnp.concatenate([gate_weight, up_weight, down_weight.T, output_weight.T], axis=1)
    )
    dp_at = lax.axis_index("dp")
    bits = jnp.stack([dp_at % 2, (dp_at // 2) % 2, place, (dp_at // 4) % 2]).astype(jnp.int32)
    growing = Growing(
        jnp.concatenate([query_weight, key_weight, value_weight, outgate_weight], axis=1),
        long_strides()[::-1],
    )

    def norm(hidden_in):
        return (rms(hidden_in.astype(F32), 1e-6) * mixer_gain).astype(BF16)

    normed_a, _ = in_flight([growing], norm, hidden_in)
    while growing.strides:
        in_flight([growing], lambda: ())
    growing_a = Growing(growing.x[..., :768], (2, 0, 1))
    growing_b = Growing(growing.x[..., 768:], (0, 2, 1))

    def early(normed_a, cotangent):
        lowrank = jnp.dot(normed_a.astype(F32), low_first, precision=HIGHEST)
        return lowrank, owner_rows(cotangent.T), owner_rows(normed_a.T)

    (lowrank, dout_rows, normed_a_rows), _ = in_flight(
        [growing_a, growing_b], early, normed_a, cotangent
    )
    in_flight([growing_a, growing_b], lambda: ())
    in_flight([growing_a, growing_b], lambda: ())
    w_in_a, w_in_b = in_place(growing_a.x, (2, 0)), in_place(growing_b.x, (0, 2))

    proj_a = jnp.einsum("td,pdc->ptc", normed_a, w_in_a, preferred_element_type=F32).astype(BF16)
    proj_v = jnp.einsum(
        "td,pdc->ptc", normed_a, w_in_b[..., :256], preferred_element_type=F32
    ).astype(BF16)
    gain = head_gain.reshape(1, VAL)
    p_spec, r_spec, f_spec, row_spec, s_spec = specs(blocks)
    state_f32 = shape((HEADS, KEY, VAL), F32)
    cum, sig, final_state = call(
        gate_kernel,
        blocks,
        [r_spec(16), f_spec(16, 512), f_spec(1, 512), p_spec(256, 1), p_spec(256, 2),
         p_spec(256, 0), r_spec(1)],
        [r_spec(512), r_spec(512), f_spec(HEADS, KEY, VAL)],
        [shape((rows, 512), F32), shape((rows, 512), BF16), state_f32],
        [],
        1 << 29,
    )(info, lowrank, low_second, decay_bias.reshape(1, 512), proj_a, proj_a, proj_v, seg)
    def outgate_product(act, weight):
        return jnp.einsum("td,pdc->ptc", act, weight, preferred_element_type=F32).astype(BF16)

    proj_og, (state_in,) = during(
        [(final_state.astype(BF16), 0)], outgate_product, normed_a, w_in_b[..., 256:]
    )
    state_in = jnp.where(place == 0, jnp.zeros_like(state_in), state_in)
    mixed, core, states = call(
        core_kernel,
        blocks,
        [p_spec(256, 0), p_spec(256, 1), p_spec(256, 2), p_spec(256, 0), p_spec(256, 0), p_spec(256, 1),
         r_spec(512), r_spec(1), row_spec, f_spec(HEADS, KEY, VAL), f_spec(1, VAL)],
        [p_spec(512, 0), r_spec(1024), s_spec],
        [shape((2, rows, 512), BF16), shape((rows, 1024), BF16),
         shape((blocks, HEADS, KEY, VAL), BF16)],
        [pltpu.VMEM((HEADS, KEY, VAL), F32)],
        1 << 30,
    )(info, proj_a, proj_a, proj_a, proj_v, proj_og, proj_og, cum, seg, seg_row, state_in, gain)

    tiles, wides = rows // TILE, rows // WIDE
    cut = 768
    place_out = 3 * half // 128

    def tile(cols, size=TILE):
        return pl.BlockSpec((size, cols), lambda m: (m, 0))

    def tile_pair(cols, size=TILE):
        return pl.BlockSpec((2, size, cols), lambda m: (0, m, 0))

    def keep(*dims, at=None):
        return pl.BlockSpec(dims, lambda *_: at or (0,) * len(dims))

    def part(cols):
        return pl.BlockSpec((1, WIDE, cols), lambda p, m: (p, m, 0))

    def part_weight(at):
        return pl.BlockSpec((1, width, half), lambda p, m: (p, 0, at))

    part_pair = pl.BlockSpec((2, 1, WIDE, half), lambda p, m: (0, p, m, 0))
    part_rows = pl.BlockSpec((WIDE, width), lambda p, m: (m, 0))
    late_rows = pl.BlockSpec((WIDE, width), lambda p, m: (p * m, 0))
    late_cols = pl.BlockSpec((width, WIDE), lambda p, m: (0, p * m))
    w_out = [keep(2, width, 128, at=(0, 0, place_out + i)) for i in range(4)]
    gain_b, gain_a = feed_gain.reshape(1, width), mixer_gain.reshape(1, width)
    middle, normed_b, normed_b_cols = call(
        middle_kernel,
        tiles,
        [tile_pair(512), *w_out, tile(width), keep(1, width)],
        [tile(width), tile(width), pl.BlockSpec((width, TILE), lambda m: (0, m))],
        [shape((rows, width), F32), shape((rows, width), BF16), shape((width, rows), BF16)],
        [],
        2 * rows * width * 1024,
        0,
    )(mixed, w_rest, w_rest, w_rest, w_rest, hidden_in, gain_b)
    activ_a, activ_b, d_pre = call(
        ff_kernel,
        (2, wides),
        [part_rows, part_rows, part_weight(0), part_weight(1), part_weight(2)],
        [part(cut), part(half - cut), part_pair],
        [shape((2, rows, cut), BF16), shape((2, rows, half - cut), BF16),
         shape((2, 2, rows, half), BF16)],
        [],
        12 * rows * width * half,
        0,
    )(normed_b, cotangent, w_rest, w_rest, w_rest)

    down_pairs = [(dout_rows, activ_a), (dout_rows, activ_b)]
    sent = grad_other(bits, *down_pairs)

    def other_gate_up(normed_cols, d_pre):
        normed_rows = owner_rows(normed_cols)
        return normed_rows, grad_other(bits, (normed_rows, d_pre))

    (normed_rows, sent), got = in_flight(
        [], other_gate_up, normed_b_cols, d_pre, also=[(array, 1) for array in sent]
    )

    def middle_back(d_pre, weight, middle, dout):
        return call(
            middle_back_kernel,
            (2, wides),
            [part_pair, part_weight(0), part_weight(1), *w_out, late_rows, late_rows, keep(1, width)],
            [late_rows, late_rows, late_cols, late_rows, keep(1, width)],
            [shape((rows, width), F32), shape((rows, width), BF16), shape((width, rows), BF16),
             shape((rows, 1024), BF16), shape((1, width), F32)],
            [pltpu.VMEM((wides, WIDE, width), F32)],
            8 * rows * width * half,
            0,
        )(d_pre, weight, weight, weight, weight, weight, weight, middle, dout, gain_b)

    down = Halving(bits, *grad_mine(bits, down_pairs, got))
    (d_middle, d_mix, d_mix_cols, d_mixed, feed_gain_grad), got = in_flight(
        [down], middle_back, d_pre, w_rest, middle, cotangent, also=[(array, 1) for array in sent]
    )

    def post_back(d_mixed):
        return call(
            post_kernel,
            blocks,
            [r_spec(1024), r_spec(1024), p_spec(256, 0), p_spec(256, 1), p_spec(256, 0), r_spec(512),
             r_spec(1), f_spec(1, VAL)],
            [r_spec(1024), p_spec(512, 0), f_spec(1, VAL), f_spec(HEADS, KEY, VAL)],
            [shape((rows, 1024), BF16), shape((2, rows, 512), BF16), shape((1, VAL), F32), state_f32],
            [pltpu.VMEM((1, 512), F32)],
            1 << 29,
        )(info, d_mixed, core, proj_og, proj_og, proj_a, cum, seg, gain)

    (d_core, d_og, head_gain_grad, d_state), _ = in_flight([down], post_back, d_mixed)

    def mine_gate_up(normed_rows, d_pre, normed_a_rows, d_mix_cols, d_og, mixed, *got):
        mix_rows = owner_rows(d_mix_cols)
        halves = grad_mine(bits, [(normed_rows, d_pre)], got)
        return mix_rows, halves, grad_other(bits, (normed_a_rows, d_og), (mix_rows, mixed))

    (mix_rows, halves, sent), (d_state_in,) = in_flight(
        [down], mine_gate_up, normed_rows, d_pre, normed_a_rows, d_mix_cols, d_og, mixed, *got,
        also=[(d_state.astype(BF16), 0)],
    )
    gate_up = Halving(bits, *halves)
    d_state_in = jnp.where(place == 1, jnp.zeros_like(d_state_in), d_state_in)
    p_back, r_back, f_back, row_back, s_back = specs(blocks, True)

    def mixer_back(d_core, d_state_in, normed_a_rows):
        d_qk, d_v, d_rank, low_second_grad, bias_grad = call(
            back_kernel,
            blocks,
            [p_back(256, 0), p_back(256, 1), p_back(256, 2), p_back(256, 0),
             r_back(512), r_back(512), s_back, r_back(1024), r_back(1), row_back,
             f_back(HEADS, KEY, VAL), f_back(16, 512), r_back(16)],
            [p_back(512, 0), p_back(512, 0), r_back(16), f_back(16, 512), f_back(1, 512)],
            [shape((2, rows, 512), BF16), shape((2, rows, 512), BF16), shape((rows, 16), F32),
             shape((16, 512), F32), shape((1, 512), F32)],
            [pltpu.VMEM((HEADS, KEY, VAL), F32)],
            3 << 30,
        )(info, proj_a, proj_a, proj_a, proj_v, cum, sig, states, d_core, seg, seg_row,
          d_state_in, low_second, lowrank)
        late = grad_other(bits, (normed_a_rows, d_qk), (normed_a_rows, d_v))
        low_first_grad = tn(normed_a, d_rank.astype(BF16))
        return d_qk, d_v, d_rank, low_first_grad, low_second_grad, bias_grad, late

    (d_qk, d_v, d_rank, low_first_grad, low_second_grad, bias_grad, late), got = in_flight(
        [gate_up, down], mixer_back, d_core, d_state_in, normed_a_rows,
        also=[(array, 1) for array in sent],
    )
    own_down = down.finish()
    parts = (feed_gain_grad, low_first_grad, low_second_grad, bias_grad, head_gain_grad)
    small_sum = HopSum(jnp.concatenate([part.reshape(-1, 128) for part in parts]))

    def mine_pair(left_a, right_a, left_b, right_b, *got):
        return grad_mine(bits, [(left_a, right_a), (left_b, right_b)], got)

    halves, got = in_flight(
        [gate_up, small_sum], mine_pair, normed_a_rows, d_og, mix_rows, mixed, *got,
        also=[(array, 1) for array in late],
    )
    mix_early = Halving(bits, *halves)
    halves, _ = in_flight(
        [gate_up, mix_early, small_sum], mine_pair, normed_a_rows, d_qk, normed_a_rows, d_v, *got
    )
    mix_late = Halving(bits, *halves)

    def input_back(d_qk, d_v, d_og, w_a, w_b, d_rank, d_middle):
        return call(
            input_back_kernel,
            wides,
            [tile_pair(512, WIDE), tile_pair(512, WIDE), tile_pair(512, WIDE), keep(2, width, 768),
             keep(2, width, 768), tile(16, WIDE), keep(width, 16), tile(width, WIDE),
             tile(width, WIDE), keep(1, width)],
            [tile(width, WIDE), keep(1, width)],
            [shape((rows, width), BF16), shape((1, width), F32)],
            [],
            4 * rows * width * 1536,
            0,
        )(d_qk, d_v, d_og, w_a, w_b, d_rank, low_first, hidden_in, d_middle, gain_a)

    (input_grad, mixer_gain_grad), _ = in_flight(
        [mix_late, gate_up, mix_early, small_sum],
        input_back, d_qk, d_v, d_og, w_in_a, w_in_b, d_rank, d_middle,
    )
    gain_sum = HopSum(mixer_gain_grad.reshape(-1, 128))

    def feed_out(activ_a, activ_b, weight, middle):
        return call(
            feed_kernel,
            (2, wides),
            [part(cut), part(half - cut), part_weight(2), late_rows],
            late_rows,
            shape((rows, width), BF16),
            [pltpu.VMEM((wides, WIDE, width), F32)],
            4 * rows * width * half,
            0,
        )(activ_a, activ_b, weight, middle)

    block_out, _ = in_flight(
        [mix_late, gate_up, mix_early, small_sum, gain_sum], feed_out, activ_a, activ_b, w_rest, middle
    )
    while mix_late.out:
        in_flight([mix_late, gate_up, mix_early, small_sum, gain_sum], lambda: ())
    own_gate, own_up = gate_up.finish()
    own_og, own_out = mix_early.finish()
    own_qk, own_v = mix_late.finish()

    flat = small_sum.finish()
    small, spot = [gain_sum.finish().reshape(width)], 0
    for part, dims in zip(parts, ((width,), low_first.shape, low_second.shape, (512,), (VAL,))):
        size = part.size // 128
        small.append(flat[spot : spot + size].reshape(dims))
        spot += size
    return (
        block_out,
        input_grad,
        own_qk[:, :256],
        own_qk[:, 256:],
        own_v,
        own_og,
        own_out.T,
        own_gate,
        own_up,
        jnp.concatenate([part.T for part in own_down], axis=0),
        *small,
    )


def solution(mesh):
    tokens = P(("dp", "tensor"))
    split_in = P("dp", "tensor")
    split_out = P("tensor", "dp")
    weights = (split_in,) * 4 + (split_out,) + (split_in,) * 2 + (split_out,)
    in_specs = (tokens, P("dp", None), tokens) + weights + (P(),) * 6
    out_specs = (tokens, tokens) + weights + (P(),) * 6
    return jax.shard_map(local, mesh=mesh, in_specs=in_specs, out_specs=out_specs, check_vma=False)
```

```python
import functools

import jax
import jax.numpy as jnp
from jax import lax
from jax.experimental import pallas as pl
from jax.experimental.pallas import tpu as pltpu
from jax.sharding import PartitionSpec as P

HEADS = 4
KEY = 128
VAL = 256
CHUNK = 128
SCALE = KEY ** (-0.5)
F32 = jnp.float32
BF16 = jnp.bfloat16
HIGHEST = lax.Precision.HIGHEST
ALL = ("tensor", "dp")
VMEM_BYTES = 56 * 1024 * 1024
TILE = 256
WIDE = 512


def nn(a, b):
    return lax.dot_general(a, b, (((1,), (0,)), ((), ())), preferred_element_type=F32)


def nt(a, b):
    return lax.dot_general(a, b, (((1,), (1,)), ((), ())), preferred_element_type=F32)


def tn(a, b):
    return lax.dot_general(a, b, (((0,), (0,)), ((), ())), preferred_element_type=F32)


def triangle(lower):
    rows = lax.broadcasted_iota(jnp.int32, (CHUNK, CHUNK), 0)
    cols = lax.broadcasted_iota(jnp.int32, (CHUNK, CHUNK), 1)
    return rows >= cols if lower else rows <= cols


def split_sum(tri, x, terms):
    total = None
    for _ in range(terms):
        part = x.astype(BF16)
        x = x - part.astype(F32)
        term = nn(tri, part)
        total = term if total is None else total + term
    return total


def head_cols(h, width):
    return h // 2, slice((h % 2) * width, (h % 2 + 1) * width)


def head_pick(h, first, second):
    return (first if h % 2 == 0 else second)[h // 2]


def gate_kernel(info, low_ref, second_ref, bias_ref, k_ref, v0_ref, v1_ref, seg_ref, cum_ref, sig_ref, state_ref):
    c = pl.program_id(0)

    @pl.when(c == 0)
    def _():
        state_ref[...] = jnp.zeros_like(state_ref)

    logit = (
        jnp.dot(low_ref[...], second_ref[...], precision=HIGHEST, preferred_element_type=F32)
        + bias_ref[...]
    )
    e = jnp.exp(-jnp.abs(logit))
    decays = (jnp.minimum(logit, 0.0) - jnp.log1p(e)) * (1.0 / 16.0)
    sig_ref[...] = (jnp.where(logit >= 0, e, 1.0) / (1.0 + e)).astype(BF16)
    tri = triangle(True).astype(F32).astype(BF16)
    cum = split_sum(tri, decays, 3)
    cum_ref[...] = cum
    final = cum[CHUNK - 1 :, :]
    tail = (seg_ref[...] == info[1, c]).astype(F32)
    retain = (info[1, c] == info[0, c]).astype(F32)
    tail_decay = jnp.exp(final - cum) * tail
    keep = jnp.exp(final) * retain
    for h in range(HEADS):
        p, kc = head_cols(h, KEY)
        hk = slice(h * KEY, (h + 1) * KEY)
        kt = (k_ref[p, :, kc].astype(F32) * tail_decay[:, hk]).astype(BF16)
        state_ref[h] = state_ref[h] * keep[:, hk].reshape(KEY, 1) + tn(kt, head_pick(h, v0_ref, v1_ref))


def core_kernel(
    info, q_ref, k_ref, v0_ref, v1_ref, og0_ref, og1_ref, cum_ref, seg_ref, row_ref, first_ref, gain_ref,
    mixed_ref, core_ref, states_ref, state,
):
    c = pl.program_id(0)

    @pl.when(c == 0)
    def _():
        state[...] = first_ref[...].astype(F32)

    before, last = info[0, c], info[1, c]
    seg = seg_ref[...]
    mask = triangle(True) & (seg == row_ref[0])
    running = (seg == before).astype(F32)
    tail = (seg == last).astype(F32)
    retain = (last == before).astype(F32)
    cum = cum_ref[...]
    final = cum[CHUNK - 1 :, :]
    mid = cum[CHUNK // 2 - 1 : CHUNK // 2, :]
    up, down = jnp.exp(cum - mid), jnp.exp(mid - cum)
    whole = jnp.exp(cum) * running
    rest = jnp.exp(final - cum) * tail
    keep = jnp.exp(final) * retain
    for h in range(HEADS):
        p, kc = head_cols(h, KEY)
        hk = slice(h * KEY, (h + 1) * KEY)
        q = q_ref[p, :, kc].astype(F32) * SCALE
        k = k_ref[p, :, kc].astype(F32)
        v = head_pick(h, v0_ref, v1_ref)
        s = state[h]
        s_low = s.astype(BF16)
        states_ref[0, h] = s_low
        scores = nt((q * up[:, hk]).astype(BF16), (k * down[:, hk]).astype(BF16))
        scores = jnp.where(mask, scores, 0.0).astype(BF16)
        core = nn((q * whole[:, hk]).astype(BF16), s_low) + nn(scores, v)
        state[h] = s * keep[:, hk].reshape(KEY, 1) + tn((k * rest[:, hk]).astype(BF16), v)
        normed = core * lax.rsqrt(jnp.mean(core * core, axis=-1, keepdims=True) + 1.0)
        og = head_pick(h, og0_ref, og1_ref).astype(F32)
        hv = slice(h * VAL, (h + 1) * VAL)
        mixed = normed * gain_ref[...] * (og * jax.nn.sigmoid(og))
        mixed_ref[p, :, head_cols(h, VAL)[1]] = mixed.astype(BF16)
        core_ref[:, hv] = core.astype(BF16)


def post_kernel(
    info, dm_ref, core_ref, og0_ref, og1_ref, q_ref, cum_ref, seg_ref, gain_ref,
    dcore_ref, dog_ref, dgain_ref, dstate_ref, prefix,
):
    c = pl.program_id(0)

    @pl.when(c == 0)
    def _():
        prefix[...] = jnp.zeros_like(prefix)
        dgain_ref[...] = jnp.zeros_like(dgain_ref)
        dstate_ref[...] = jnp.zeros_like(dstate_ref)

    running = (seg_ref[...] == info[0, 0]).astype(F32)
    cum = cum_ref[...]
    decay = jnp.exp(cum + prefix[...]) * running * SCALE
    prefix[...] += cum[CHUNK - 1 :, :]
    gain = gain_ref[...]
    total = jnp.zeros((1, VAL), F32)
    for h in range(HEADS):
        p, kc = head_cols(h, KEY)
        hk = slice(h * KEY, (h + 1) * KEY)
        hv = slice(h * VAL, (h + 1) * VAL)
        core = core_ref[:, hv].astype(F32)
        scale = lax.rsqrt(jnp.mean(core * core, axis=-1, keepdims=True) + 1.0)
        normed = core * scale
        og = head_pick(h, og0_ref, og1_ref).astype(F32)
        sig = jax.nn.sigmoid(og)
        silu = og * sig
        dm = dm_ref[:, hv].astype(F32)
        both = dm * normed
        total += jnp.sum(both * silu, axis=0, keepdims=True)
        dog_ref[p, :, head_cols(h, VAL)[1]] = (both * gain * (sig * (1.0 + og * (1.0 - sig)))).astype(BF16)
        dn = dm * gain * silu
        dcore = scale * (dn - normed * jnp.mean(dn * normed, axis=-1, keepdims=True))
        dcore = dcore.astype(BF16)
        dcore_ref[:, hv] = dcore
        qa = (q_ref[p, :, kc].astype(F32) * decay[:, hk]).astype(BF16)
        dstate_ref[h] += tn(qa, dcore)
    dgain_ref[...] += total


def back_kernel(
    info, q_ref, k_ref, v0_ref, v1_ref, cum_ref, sig_ref, states_ref, dcore_ref, seg_ref, row_ref,
    first_ref, second_ref, low_ref, dqkv_ref, drank_ref, dsecond_ref, dbias_ref, dstate,
):
    i = pl.program_id(0)
    c = pl.num_programs(0) - 1 - i

    @pl.when(i == 0)
    def _():
        dstate[...] = first_ref[...].astype(F32)
        dsecond_ref[...] = jnp.zeros_like(dsecond_ref)
        dbias_ref[...] = jnp.zeros_like(dbias_ref)

    before, last = info[0, c], info[1, c]
    seg = seg_ref[...]
    mask = triangle(True) & (seg == row_ref[0])
    upper = triangle(False).astype(F32).astype(BF16)
    running = (seg == before).astype(F32)
    tail = (seg == last).astype(F32)
    retain = (last == before).astype(F32)
    cum = cum_ref[...]
    final = cum[CHUNK - 1 :, :]
    mid = cum[CHUNK // 2 - 1 : CHUNK // 2, :]
    up, down = jnp.exp(cum - mid), jnp.exp(mid - cum)
    whole = jnp.exp(cum) * running
    rest = jnp.exp(final - cum) * tail
    keep = jnp.exp(final) * retain
    logits = []
    for h in range(HEADS):
        p, kc = head_cols(h, KEY)
        hk = slice(h * KEY, (h + 1) * KEY)
        hv = slice(h * VAL, (h + 1) * VAL)
        q = q_ref[p, :, kc].astype(F32) * SCALE
        k = k_ref[p, :, kc].astype(F32)
        v = head_pick(h, v0_ref, v1_ref)
        do = dcore_ref[:, hv]
        s = states_ref[0, h]
        ds = dstate[h]
        ds_low = ds.astype(BF16)
        q_up = (q * up[:, hk]).astype(BF16)
        k_down = (k * down[:, hk]).astype(BF16)
        q_whole = (q * whole[:, hk]).astype(BF16)
        k_rest = (k * rest[:, hk]).astype(BF16)
        scores = jnp.where(mask, nt(q_up, k_down), 0.0).astype(BF16)
        dscores = jnp.where(mask, nt(do, v), 0.0).astype(BF16)
        dq_up = nn(dscores, k_down)
        dk_down = tn(dscores, q_up)
        dq_whole = nt(do, s)
        dk_rest = nt(v, ds_low)
        dv = tn(scores, do) + nn(k_rest, ds_low)
        dq = dq_up * up[:, hk] + dq_whole * whole[:, hk]
        dk = dk_down * down[:, hk] + dk_rest * rest[:, hk]
        from_rest = k_rest.astype(F32) * dk_rest
        dcum = (
            q_up.astype(F32) * dq_up
            - k_down.astype(F32) * dk_down
            + q_whole.astype(F32) * dq_whole
            - from_rest
        )
        kept = keep[:, hk].reshape(KEY, 1)
        through = jnp.sum(s.astype(F32) * ds, axis=1, keepdims=True) * kept
        dfinal = through.reshape(1, KEY) + jnp.sum(from_rest, axis=0, keepdims=True)
        ddecay = split_sum(upper, dcum, 2) + dfinal
        dstate[h] = ds * kept + tn(q_whole, do)
        logits.append(ddecay * (sig_ref[:, hk].astype(F32) * (1.0 / 16.0)))
        vc = head_cols(h, VAL)[1]
        dqkv_ref[p, :, kc] = (dq * SCALE).astype(BF16)
        dqkv_ref[p, :, slice(256 + kc.start, 256 + kc.stop)] = dk.astype(BF16)
        dqkv_ref[p, :, slice(512 + vc.start, 512 + vc.stop)] = dv.astype(BF16)
    dlogit = jnp.concatenate(logits, axis=1)
    dbias_ref[...] += jnp.sum(dlogit, axis=0, keepdims=True)
    low = dlogit.astype(BF16)
    dsecond_ref[...] += tn(low_ref[...].astype(BF16), low)
    drank_ref[...] = nt(low, second_ref[...].astype(BF16))


def rms_rows(x):
    scale = lax.rsqrt(jnp.mean(x * x, axis=-1, keepdims=True) + 1e-6)
    return x * scale, scale


def rms_rows_back(normed, scale, gain, grad):
    dn = grad * gain
    return scale * (dn - normed * jnp.mean(dn * normed, axis=-1, keepdims=True))


def output_rows(w_refs, p):
    return jnp.concatenate([ref[p] for ref in w_refs], axis=1)


def middle_kernel(mixed_ref, w0, w1, w2, w3, hidden_ref, gain_ref, middle_ref, normed_ref, cols_ref):
    middle = hidden_ref[...].astype(F32)
    for p in range(2):
        middle += nt(mixed_ref[p], output_rows((w0, w1, w2, w3), p))
    middle_ref[...] = middle
    normed = (rms_rows(middle)[0] * gain_ref[...]).astype(BF16)
    normed_ref[...] = normed
    cols_ref[...] = normed.T


def ff_kernel(normed_ref, dout_ref, wg_ref, wu_ref, wd_ref, first_ref, second_ref, dpre_ref):
    gate = nn(normed_ref[...], wg_ref[0])
    up = nn(normed_ref[...], wu_ref[0])
    sig = jax.nn.sigmoid(gate)
    silu = gate * sig
    activ = (silu * up).astype(BF16)
    cut = first_ref.shape[-1]
    first_ref[0] = activ[:, :cut]
    second_ref[0] = activ[:, cut:]
    d_activ = nn(dout_ref[...], wd_ref[0])
    dpre_ref[0, 0] = (d_activ * up * (sig * (1.0 + gate * (1.0 - sig)))).astype(BF16)
    dpre_ref[1, 0] = (d_activ * silu).astype(BF16)


def feed_kernel(first_ref, second_ref, wd_ref, middle_ref, out_ref, total):
    p, m = pl.program_id(0), pl.program_id(1)
    cut = first_ref.shape[-1]
    part = nt(first_ref[0], wd_ref[0, :, :cut]) + nt(second_ref[0], wd_ref[0, :, cut:])

    @pl.when(p == 0)
    def _():
        total[m] = part

    @pl.when(p == 1)
    def _():
        out_ref[...] = (middle_ref[...] + total[m] + part).astype(BF16)


def middle_back_kernel(
    dpre_ref, wg_ref, wu_ref, w0, w1, w2, w3, middle_ref, dout_ref, gain_ref,
    dmiddle_ref, dmix_ref, cols_ref, dmixed_ref, dgain_ref, total,
):
    p, m = pl.program_id(0), pl.program_id(1)
    part = nt(dpre_ref[0, 0], wg_ref[0]) + nt(dpre_ref[1, 0], wu_ref[0])

    @pl.when((p == 0) & (m == 0))
    def _():
        dgain_ref[...] = jnp.zeros_like(dgain_ref)

    @pl.when(p == 0)
    def _():
        total[m] = part

    @pl.when(p == 1)
    def _():
        grad = total[m] + part
        normed, scale = rms_rows(middle_ref[...])
        dgain_ref[...] += jnp.sum(grad * normed, axis=0, keepdims=True)
        dmiddle = dout_ref[...].astype(F32) + rms_rows_back(normed, scale, gain_ref[...], grad)
        dmiddle_ref[...] = dmiddle
        dmix = dmiddle.astype(BF16)
        dmix_ref[...] = dmix
        cols_ref[...] = dmix.T
        for q in range(2):
            dmixed_ref[:, q * 512 : (q + 1) * 512] = nn(
                dmix, output_rows((w0, w1, w2, w3), q)
            ).astype(BF16)


def input_back_kernel(
    dqkv_ref, dog_ref, wa_ref, wb_ref, drank_ref, first_ref, hidden_ref, dmiddle_ref, gain_ref,
    out_ref, dgain_ref,
):
    @pl.when(pl.program_id(0) == 0)
    def _():
        dgain_ref[...] = jnp.zeros_like(dgain_ref)

    grad = nt(drank_ref[...].astype(BF16), first_ref[...].astype(BF16))
    for p in range(2):
        grad += nt(dqkv_ref[p, :, :768], wa_ref[p])
        grad += nt(dqkv_ref[p, :, 768:], wb_ref[p, :, :256]) + nt(dog_ref[p], wb_ref[p, :, 256:])
    normed, scale = rms_rows(hidden_ref[...].astype(F32))
    dgain_ref[...] += jnp.sum(grad * normed, axis=0, keepdims=True)
    back = rms_rows_back(normed, scale, gain_ref[...], grad)
    out_ref[...] = (dmiddle_ref[...] + back).astype(BF16)


def products(refs, rows):
    at = 0
    for left, right in zip(refs[::2], refs[1::2]):
        cols = right.shape[-1]
        result = nn(left[0].reshape(rows, left.shape[-1]), right[...].reshape(-1, cols))
        yield result, slice(at, at + cols)
        at += cols


def grad_other_kernel(count, bits, *refs):
    operands, (out_a, out_b) = refs[:-2], refs[-2:]
    step = pl.program_id(0)
    rows = 2 * out_a.shape[2]
    for place, out in enumerate((out_a, out_b)):
        own = operands[count:] or operands if place else operands[:count]

        @pl.when(step // 2 == place)
        def _(own=own, out=out):
            for result, cols in products(own, rows):
                out[0, :, :, cols] = result.astype(BF16).reshape(2, rows // 2, -1)


def grad_mine_kernel(count, bits, *refs):
    operands, (got_a, got_b, send_a, keep_a, send_b, keep_b) = refs[:-6], refs[-6:]
    step, x = pl.program_id(0), bits[1]
    own = send_a.shape[1]

    def halves(operands, got):
        for both, cols in products(operands, 2 * own):
            low = (both[:own] + got[0, 0, :, cols].astype(F32)).astype(BF16)
            high = (both[own:] + got[0, 1, :, cols].astype(F32)).astype(BF16)
            yield low, high, cols

    @pl.when(step < 2)
    def _():
        for low, high, cols in halves(operands[:count], got_a):

            @pl.when(x == 0)
            def _(low=low, high=high, cols=cols):
                send_a[0, :, cols] = high
                keep_a[0, :, cols] = low

            @pl.when(x == 1)
            def _(low=low, high=high, cols=cols):
                send_a[0, :, cols] = low
                keep_a[0, :, cols] = high

    @pl.when(step >= 2)
    def _():
        for low, high, cols in halves(operands[count:] or operands, got_b):

            @pl.when(step == 2)
            def _(low=low, high=high, cols=cols):
                send_b[0, :, cols] = low
                send_b[1, :, cols] = high

            @pl.when(step == 3)
            def _(low=low, high=high, cols=cols):
                keep_b[0, :, cols] = low
                keep_b[1, :, cols] = high


def add(x, y):
    return (x.astype(F32) + y.astype(F32)).astype(BF16)


def fold_kernel(bits, ka, ga, kb, gb, sa, na, sb, nb):
    p, x = bits[2], bits[1]
    sa[...] = add(ka[1 - p], ga[1 - p])
    na[...] = add(ka[p], ga[p])
    sb[...] = add(kb[1 - x], gb[1 - x])
    nb[...] = add(kb[x], gb[x])


def join_kernel(bits, ka, ga, kb, gb, *outs):
    cut = ka.shape[-1]
    for i, out in enumerate(outs):
        z = bits[3] ^ i
        out[:, :cut] = add(ka[z], ga[z])
        out[:, cut:] = add(kb[z], gb[z])


def shape(dims, dtype):
    return jax.ShapeDtypeStruct(dims, dtype)


def call(kernel, grid, in_specs, out_specs, out_shape, scratch, cost, prefetch=1):
    grid = grid if isinstance(grid, tuple) else (grid,)
    return pl.pallas_call(
        kernel,
        grid_spec=pltpu.PrefetchScalarGridSpec(
            num_scalar_prefetch=prefetch,
            grid=grid,
            in_specs=in_specs,
            out_specs=out_specs,
            scratch_shapes=scratch,
        ),
        out_shape=out_shape,
        compiler_params=pltpu.CompilerParams(
            dimension_semantics=("arbitrary",) * len(grid), vmem_limit_bytes=VMEM_BYTES
        ),
        cost_estimate=pl.CostEstimate(flops=cost, bytes_accessed=16 << 20, transcendentals=1 << 20),
    )


def specs(blocks, backward=False):
    def at(c):
        return blocks - 1 - c if backward else c

    def proj(width, place):
        return pl.BlockSpec((2, CHUNK, width), lambda c, _: (0, at(c), place))

    def rows(width):
        return pl.BlockSpec((CHUNK, width), lambda c, _: (at(c), 0))

    def full(*dims):
        return pl.BlockSpec(dims, lambda c, _: (0,) * len(dims))

    row = pl.BlockSpec((1, 1, CHUNK), lambda c, _: (at(c), 0, 0))
    states = pl.BlockSpec((1, HEADS, KEY, VAL), lambda c, _: (at(c), 0, 0, 0))
    return proj, rows, full, row, states


def rms(x, eps):
    return x * lax.rsqrt(jnp.mean(x * x, axis=-1, keepdims=True) + eps)


def rms_back(x, gain, eps, grad):
    scale = lax.rsqrt(jnp.mean(x * x, axis=-1, keepdims=True) + eps)
    normed = x * scale
    dn = grad * gain
    back = scale * (dn - normed * jnp.mean(dn * normed, axis=-1, keepdims=True))
    return back, jnp.sum(grad * normed, axis=0)


def gather(shard):
    return lax.all_gather(shard, ALL, axis=0, tiled=True).reshape(2, -1, shard.shape[1])


def swap(x, stride):
    if isinstance(stride, tuple):
        places = 2 * lax.axis_size("dp")
        return lax.ppermute(x, ("dp", "tensor"), [(i, i ^ stride[1]) for i in range(places)])
    if stride == 0:
        return lax.ppermute(x, "tensor", [(0, 1), (1, 0)])
    return lax.ppermute(x, "dp", [(i, i ^ stride) for i in range(lax.axis_size("dp"))])


def own_bit(stride):
    return lax.axis_index("tensor") if stride == 0 else (lax.axis_index("dp") // stride) % 2


def long_strides():
    strides, stride = [], 4
    while stride < lax.axis_size("dp"):
        strides.append(stride)
        stride *= 2
    return strides


def in_place(x, mid):
    steps = len(x.shape) - 2
    x_at, t_at = (2, 1) if mid[0] == 2 else (1, 2)
    z_axes = list(range(3, steps))[::-1]
    order = [t_at] + z_axes + [x_at, 0, steps, steps + 1]
    return x.transpose(order).reshape(2, -1, x.shape[-1])


def owner_rows(cols):
    count, rows = cols.shape
    z = len(long_strides())
    own = count // lax.axis_size("dp")
    split = cols.reshape((2,) * (z + 2) + (own, rows))
    split = split.transpose([z + 1, z] + list(range(z))[::-1] + [z + 2, z + 3])
    return split.reshape(2, 2, -1, rows)


class HopSum:
    def __init__(self, x):
        self.x, self.hops = x, [[4, 1], [2]] + [[2 * stride] for stride in long_strides()]

    def sends(self):
        if not self.hops:
            return []
        hop = self.hops[0]
        return [(self.x, ("all", mask)) for mask in (hop if len(hop) == 1 else [*hop, sum(hop)])]

    def receive(self, got):
        if self.hops:
            self.x = self.x + sum(got)
            self.hops = self.hops[1:]

    def finish(self):
        while self.hops:
            in_flight([self], lambda: ())
        return self.x


class Growing:
    def __init__(self, x, strides):
        self.x, self.strides = x, list(strides)

    def sends(self):
        return [(self.x, self.strides[0])]

    def receive(self, got):
        bit, self.strides = own_bit(self.strides[0]), self.strides[1:]
        low, high = jnp.stack([self.x, got[0]]), jnp.stack([got[0], self.x])
        self.x = jnp.where(bit == 0, low, high)


def in_flight(movers, work, *inputs, also=()):
    sends = [mover.sends() for mover in movers]
    flat = [pair for group in sends for pair in group] + list(also)
    result, got = during(flat, work, *inputs)
    at = 0
    for mover, group in zip(movers, sends):
        mover.receive(got[at : at + len(group)])
        at += len(group)
    return result, got[at:]


def fence(*values):
    return lax.optimization_barrier(values)


def during(sends, work, *inputs):
    arrays, inputs = fence([array for array, _ in sends], inputs)
    got = [swap(array, stride) for array, (_, stride) in zip(arrays, sends)]
    return fence(work(*inputs), got)


def half_specs(halves, core, second_part):
    specs, operands = [], []
    for place, pairs in enumerate(halves):
        for left, right in pairs:
            own, rows = left.shape[2:]
            specs.append(pl.BlockSpec((1, 2, own, rows), lambda s, b: (core(b), 0, 0, 0)))
            cols = right.shape[-1]

            def part(s, b, place=place):
                return jnp.minimum(s, 1) if place == 0 else second_part(jnp.maximum(s - 2, 0), b)

            def at(s, b):
                return s // 2, jnp.where(s < 2, s, second_part(s - 2, b)), 0, 0

            if len(halves) == 1:
                specs.append(pl.BlockSpec((1, 1, rows, cols), at))
            else:
                specs.append(pl.BlockSpec((1, rows, cols), lambda s, b, part=part: (part(s, b), 0, 0)))
            operands += [left, right]
    widths = [sum(right.shape[-1] for _, right in halves[i]) for i in (0, -1)]
    return specs, operands, own, rows, widths


def grad_other(bits, *halves):
    in_specs, operands, own, rows, widths = half_specs(halves, lambda b: 1 - b[0], lambda s, b: s)
    dims = [(2, 2, own, cols) for cols in widths]
    return call(
        functools.partial(grad_other_kernel, 2 * len(halves[0])),
        4,
        in_specs,
        [
            pl.BlockSpec((1,) + dims[0][1:], lambda s, b: (jnp.minimum(s, 1), 0, 0, 0)),
            pl.BlockSpec((1,) + dims[1][1:], lambda s, b: (jnp.maximum(s - 2, 0), 0, 0, 0)),
        ],
        [shape(d, BF16) for d in dims],
        [],
        8 * own * rows * sum(widths),
    )(bits, *operands)


def grad_mine(bits, halves, got):
    def other_first(s, b):
        return b[2] ^ 1 ^ s

    in_specs, operands, own, rows, (cols_a, cols_b) = half_specs(halves, lambda b: b[0], other_first)
    in_specs.append(
        pl.BlockSpec((1, 2, own, cols_a), lambda s, b: (jnp.minimum(s, 1), 0, 0, 0))
    )
    in_specs.append(
        pl.BlockSpec(
            (1, 2, own, cols_b), lambda s, b: (other_first(jnp.maximum(s - 2, 0), b), 0, 0, 0)
        )
    )
    by_p = pl.BlockSpec((1, own, cols_a), lambda s, b: (jnp.minimum(s, 1), 0, 0))
    fixed = pl.BlockSpec((2, own, cols_b), lambda s, b: (0, 0, 0))
    send_a, keep_a, send_b, keep_b = call(
        functools.partial(grad_mine_kernel, 2 * len(halves[0])),
        4,
        in_specs,
        [by_p, by_p, fixed, fixed],
        [shape((2, own, cols_a), BF16)] * 2 + [shape((2, own, cols_b), BF16)] * 2,
        [],
        8 * own * rows * (cols_a + cols_b),
    )(bits, *operands, *got)
    return (send_a, keep_a), (send_b, keep_b)


def whole(kernel, bits, arrays, outs):
    def spec(dims):
        return pl.BlockSpec(dims, lambda i, b: (0,) * len(dims))

    return call(
        kernel, 1, [spec(a.shape) for a in arrays], [spec(dims) for dims in outs],
        [shape(dims, BF16) for dims in outs], [], 1 << 20,
    )(bits, *arrays)


class Halving:
    def __init__(self, bits, first, second):
        self.bits, self.stage = bits, 0
        (sa, ka), (sb, kb) = first, second
        self.keep, self.out, self.cut = [ka, kb], [(sa, 2), (sb, 0)], ka.shape[-1]
        strides = long_strides()
        self.groups = [strides[i : i + 2] for i in range(0, len(strides), 2)]

    def sends(self):
        return self.out

    def receive(self, got):
        if not self.out:
            return
        if self.stage == 0:
            (ka, kb), (ga, gb) = self.keep, got
            half_a, half_b = ka.shape[1:], kb.shape[1:]
            sa, na, sb, nb = whole(
                fold_kernel, self.bits, [ka, ga, kb, gb], [half_a, half_a, half_b, half_b]
            )
            self.keep, self.out = [na, nb], [(sa, 0), (sb, 2)]
        elif self.stage == 1:
            strides = self.groups.pop(0)
            arrays = [
                a.reshape(2 ** len(strides), -1, a.shape[-1])
                for a in (self.keep[0], got[0], self.keep[1], got[1])
            ]
            dims = (arrays[0].shape[1], arrays[0].shape[2] + arrays[2].shape[2])
            self.keep, *sends = whole(
                join_kernel, self.bits, arrays, [dims] * 2 ** len(strides)
            )
            self.out = [(send, self.mask(i + 1, strides)) for i, send in enumerate(sends)]
        else:
            total = self.keep + sum(got[1:], got[0])
            if self.groups:
                strides = self.groups.pop(0)
                total = total.reshape(2 ** len(strides), -1, total.shape[-1])
                at = sum(own_bit(stride) << i for i, stride in enumerate(strides[::-1]))
                parts = [
                    lax.dynamic_index_in_dim(total, at ^ i, 0, keepdims=False)
                    for i in range(2 ** len(strides))
                ]
                self.keep = parts[0]
                self.out = [(part, self.mask(i + 1, strides)) for i, part in enumerate(parts[1:])]
            else:
                self.keep, self.out = total.astype(F32), []
        self.stage += 1

    def mask(self, i, strides):
        return sum(((i >> place) & 1) * stride for place, stride in enumerate(strides[::-1]))

    def finish(self):
        while self.out:
            in_flight([self], lambda: ())
        return self.keep[:, : self.cut], self.keep[:, self.cut :]


def local(
    hidden_in, lengths, cotangent, query_weight, key_weight, value_weight, outgate_weight,
    output_weight, gate_weight, up_weight, down_weight, mixer_gain, feed_gain, low_first,
    low_second, decay_bias, head_gain,
):
    rows, width = hidden_in.shape
    blocks = rows // CHUNK
    place = lax.axis_index("tensor")
    half = gate_weight.shape[1]

    starts = jnp.cumsum(lengths[0]) - lengths[0]
    spots = place * rows + jnp.arange(-1, rows, dtype=jnp.int32)
    segments = jnp.sum((spots[:, None] >= starts[None, 1:]).astype(jnp.int32), axis=1)
    segments = jnp.where(spots < 0, -1, segments)
    seg = segments[1:].reshape(rows, 1)
    seg_row = segments[1:].reshape(blocks, 1, CHUNK)
    info = jnp.stack([segments[:-1].reshape(blocks, CHUNK)[:, 0], seg_row[:, 0, -1]])

    w_rest = gather(
        jnp.concatenate([gate_weight, up_weight, down_weight.T, output_weight.T], axis=1)
    )
    dp_at = lax.axis_index("dp")
    z_at = sum(own_bit(stride) << i for i, stride in enumerate(long_strides()[:2][::-1]))
    bits = jnp.stack([dp_at % 2, (dp_at // 2) % 2, place, z_at]).astype(jnp.int32)
    growing = Growing(
        jnp.concatenate([query_weight, key_weight, value_weight, outgate_weight], axis=1),
        long_strides()[::-1],
    )

    def norm(hidden_in):
        return (rms(hidden_in.astype(F32), 1e-6) * mixer_gain).astype(BF16)

    normed_a, _ = in_flight([growing], norm, hidden_in)
    while growing.strides:
        in_flight([growing], lambda: ())
    growing_a = Growing(growing.x[..., :768], (2, 0, 1))
    growing_b = Growing(growing.x[..., 768:], (0, 2, 1))

    def early(normed_a, cotangent):
        lowrank = jnp.dot(normed_a.astype(F32), low_first, precision=HIGHEST)
        return lowrank, owner_rows(cotangent.T), owner_rows(normed_a.T)

    (lowrank, dout_rows, normed_a_rows), _ = in_flight(
        [growing_a, growing_b], early, normed_a, cotangent
    )
    in_flight([growing_a, growing_b], lambda: ())
    in_flight([growing_a, growing_b], lambda: ())
    w_in_a, w_in_b = in_place(growing_a.x, (2, 0)), in_place(growing_b.x, (0, 2))

    proj_a = jnp.einsum("td,pdc->ptc", normed_a, w_in_a, preferred_element_type=F32).astype(BF16)
    proj_v = jnp.einsum(
        "td,pdc->ptc", normed_a, w_in_b[..., :256], preferred_element_type=F32
    ).astype(BF16)
    gain = head_gain.reshape(1, VAL)
    p_spec, r_spec, f_spec, row_spec, s_spec = specs(blocks)
    state_f32 = shape((HEADS, KEY, VAL), F32)
    cum, sig, final_state = call(
        gate_kernel,
        blocks,
        [r_spec(16), f_spec(16, 512), f_spec(1, 512), p_spec(256, 1), p_spec(256, 2),
         p_spec(256, 0), r_spec(1)],
        [r_spec(512), r_spec(512), f_spec(HEADS, KEY, VAL)],
        [shape((rows, 512), F32), shape((rows, 512), BF16), state_f32],
        [],
        1 << 29,
    )(info, lowrank, low_second, decay_bias.reshape(1, 512), proj_a, proj_a, proj_v, seg)
    def outgate_product(act, weight):
        return jnp.einsum("td,pdc->ptc", act, weight, preferred_element_type=F32).astype(BF16)

    proj_og, (state_in,) = during(
        [(final_state.astype(BF16), 0)], outgate_product, normed_a, w_in_b[..., 256:]
    )
    state_in = jnp.where(place == 0, jnp.zeros_like(state_in), state_in)
    mixed, core, states = call(
        core_kernel,
        blocks,
        [p_spec(256, 0), p_spec(256, 1), p_spec(256, 2), p_spec(256, 0), p_spec(256, 0), p_spec(256, 1),
         r_spec(512), r_spec(1), row_spec, f_spec(HEADS, KEY, VAL), f_spec(1, VAL)],
        [p_spec(512, 0), r_spec(1024), s_spec],
        [shape((2, rows, 512), BF16), shape((rows, 1024), BF16),
         shape((blocks, HEADS, KEY, VAL), BF16)],
        [pltpu.VMEM((HEADS, KEY, VAL), F32)],
        1 << 30,
    )(info, proj_a, proj_a, proj_a, proj_v, proj_og, proj_og, cum, seg, seg_row, state_in, gain)

    tiles, wides = rows // TILE, rows // WIDE
    cut = 768
    place_out = 3 * half // 128

    def tile(cols, size=TILE):
        return pl.BlockSpec((size, cols), lambda m: (m, 0))

    def tile_pair(cols, size=TILE):
        return pl.BlockSpec((2, size, cols), lambda m: (0, m, 0))

    def keep(*dims, at=None):
        return pl.BlockSpec(dims, lambda *_: at or (0,) * len(dims))

    def part(cols):
        return pl.BlockSpec((1, WIDE, cols), lambda p, m: (p, m, 0))

    def part_weight(at):
        return pl.BlockSpec((1, width, half), lambda p, m: (p, 0, at))

    part_pair = pl.BlockSpec((2, 1, WIDE, half), lambda p, m: (0, p, m, 0))
    part_rows = pl.BlockSpec((WIDE, width), lambda p, m: (m, 0))
    late_rows = pl.BlockSpec((WIDE, width), lambda p, m: (p * m, 0))
    late_cols = pl.BlockSpec((width, WIDE), lambda p, m: (0, p * m))
    w_out = [keep(2, width, 128, at=(0, 0, place_out + i)) for i in range(4)]
    gain_b, gain_a = feed_gain.reshape(1, width), mixer_gain.reshape(1, width)
    middle, normed_b, normed_b_cols = call(
        middle_kernel,
        tiles,
        [tile_pair(512), *w_out, tile(width), keep(1, width)],
        [tile(width), tile(width), pl.BlockSpec((width, TILE), lambda m: (0, m))],
        [shape((rows, width), F32), shape((rows, width), BF16), shape((width, rows), BF16)],
        [],
        2 * rows * width * 1024,
        0,
    )(mixed, w_rest, w_rest, w_rest, w_rest, hidden_in, gain_b)
    activ_a, activ_b, d_pre = call(
        ff_kernel,
        (2, wides),
        [part_rows, part_rows, part_weight(0), part_weight(1), part_weight(2)],
        [part(cut), part(half - cut), part_pair],
        [shape((2, rows, cut), BF16), shape((2, rows, half - cut), BF16),
         shape((2, 2, rows, half), BF16)],
        [],
        12 * rows * width * half,
        0,
    )(normed_b, cotangent, w_rest, w_rest, w_rest)

    down_pairs = [(dout_rows, activ_a)], [(dout_rows, activ_b)]
    sent = grad_other(bits, *down_pairs)

    def other_gate_up(normed_cols, d_pre):
        normed_rows = owner_rows(normed_cols)
        return normed_rows, grad_other(bits, [(normed_rows, d_pre)])

    (normed_rows, sent), got = in_flight(
        [], other_gate_up, normed_b_cols, d_pre, also=[(array, 1) for array in sent]
    )

    def middle_back(d_pre, weight, middle, dout):
        return call(
            middle_back_kernel,
            (2, wides),
            [part_pair, part_weight(0), part_weight(1), *w_out, late_rows, late_rows, keep(1, width)],
            [late_rows, late_rows, late_cols, late_rows, keep(1, width)],
            [shape((rows, width), F32), shape((rows, width), BF16), shape((width, rows), BF16),
             shape((rows, 1024), BF16), shape((1, width), F32)],
            [pltpu.VMEM((wides, WIDE, width), F32)],
            8 * rows * width * half,
            0,
        )(d_pre, weight, weight, weight, weight, weight, weight, middle, dout, gain_b)

    down = Halving(bits, *grad_mine(bits, down_pairs, got))
    (d_middle, d_mix, d_mix_cols, d_mixed, feed_gain_grad), got = in_flight(
        [down], middle_back, d_pre, w_rest, middle, cotangent, also=[(array, 1) for array in sent]
    )

    def post_back(d_mixed):
        return call(
            post_kernel,
            blocks,
            [r_spec(1024), r_spec(1024), p_spec(256, 0), p_spec(256, 1), p_spec(256, 0), r_spec(512),
             r_spec(1), f_spec(1, VAL)],
            [r_spec(1024), p_spec(512, 0), f_spec(1, VAL), f_spec(HEADS, KEY, VAL)],
            [shape((rows, 1024), BF16), shape((2, rows, 512), BF16), shape((1, VAL), F32), state_f32],
            [pltpu.VMEM((1, 512), F32)],
            1 << 29,
        )(info, d_mixed, core, proj_og, proj_og, proj_a, cum, seg, gain)

    (d_core, d_og, head_gain_grad, d_state), _ = in_flight([down], post_back, d_mixed)

    def mine_gate_up(normed_rows, d_pre, d_mix_cols, *got):
        return owner_rows(d_mix_cols), grad_mine(bits, [[(normed_rows, d_pre)]], got)

    (mix_rows, halves), (d_state_in,) = in_flight(
        [down], mine_gate_up, normed_rows, d_pre, d_mix_cols, *got,
        also=[(d_state.astype(BF16), 0)],
    )
    own_down = down.finish()
    gate_up = Halving(bits, *halves)
    d_state_in = jnp.where(place == 1, jnp.zeros_like(d_state_in), d_state_in)
    p_back, r_back, f_back, row_back, s_back = specs(blocks, True)

    def mixer_back(d_core, d_state_in, normed_a_rows, d_og, mix_rows, mixed):
        d_qkv, d_rank, low_second_grad, bias_grad = call(
            back_kernel,
            blocks,
            [p_back(256, 0), p_back(256, 1), p_back(256, 2), p_back(256, 0),
             r_back(512), r_back(512), s_back, r_back(1024), r_back(1), row_back,
             f_back(HEADS, KEY, VAL), f_back(16, 512), r_back(16)],
            [p_back(1024, 0), r_back(16), f_back(16, 512), f_back(1, 512)],
            [shape((2, rows, 1024), BF16), shape((rows, 16), F32), shape((16, 512), F32),
             shape((1, 512), F32)],
            [pltpu.VMEM((HEADS, KEY, VAL), F32)],
            3 << 30,
        )(info, proj_a, proj_a, proj_a, proj_v, cum, sig, states, d_core, seg, seg_row,
          d_state_in, low_second, lowrank)
        pairs = [(normed_a_rows, d_qkv)], [(normed_a_rows, d_og), (mix_rows, mixed)]
        low_first_grad = tn(normed_a, d_rank.astype(BF16))
        return d_qkv, d_rank, low_first_grad, low_second_grad, bias_grad, grad_other(bits, *pairs)

    (d_qkv, d_rank, low_first_grad, low_second_grad, bias_grad, sent), _ = in_flight(
        [gate_up], mixer_back, d_core, d_state_in, normed_a_rows, d_og, mix_rows, mixed
    )

    def input_back(d_qkv, d_og, w_a, w_b, d_rank, d_middle):
        return call(
            input_back_kernel,
            wides,
            [tile_pair(1024, WIDE), tile_pair(512, WIDE), keep(2, width, 768),
             keep(2, width, 768), tile(16, WIDE), keep(width, 16), tile(width, WIDE),
             tile(width, WIDE), keep(1, width)],
            [tile(width, WIDE), keep(1, width)],
            [shape((rows, width), BF16), shape((1, width), F32)],
            [],
            4 * rows * width * 1536,
            0,
        )(d_qkv, d_og, w_a, w_b, d_rank, low_first, hidden_in, d_middle, gain_a)

    (input_grad, mixer_gain_grad), got = in_flight(
        [gate_up], input_back, d_qkv, d_og, w_in_a, w_in_b, d_rank, d_middle,
        also=[(array, 1) for array in sent],
    )
    parts = (
        mixer_gain_grad, feed_gain_grad, low_first_grad, low_second_grad, bias_grad, head_gain_grad
    )
    small_sum = HopSum(jnp.concatenate([part.reshape(-1, 128) for part in parts]))

    def feed_out(activ_a, activ_b, weight, middle):
        return call(
            feed_kernel,
            (2, wides),
            [part(cut), part(half - cut), part_weight(2), late_rows],
            late_rows,
            shape((rows, width), BF16),
            [pltpu.VMEM((wides, WIDE, width), F32)],
            4 * rows * width * half,
            0,
        )(activ_a, activ_b, weight, middle)

    def last(normed_a_rows, d_qkv, d_og, mix_rows, mixed, *got):
        pairs = [(normed_a_rows, d_qkv)], [(normed_a_rows, d_og), (mix_rows, mixed)]
        halves, _ = in_flight([small_sum], lambda *got: grad_mine(bits, pairs, got), *got)
        mix = Halving(bits, *halves)
        block_out, _ = in_flight([mix, small_sum], feed_out, activ_a, activ_b, w_rest, middle)
        return mix, block_out

    sends = gate_up.sends()
    arrays, operands = fence(
        [array for array, _ in sends], (normed_a_rows, d_qkv, d_og, mix_rows, mixed, *got)
    )
    got = [swap(array, stride) for array, (_, stride) in zip(arrays, sends)]
    mix, block_out = last(*operands)
    got, block_out, mix.keep, out = fence(got, block_out, mix.keep, [send for send, _ in mix.out])
    mix.out = [(send, stride) for send, (_, stride) in zip(out, mix.out)]
    gate_up.receive(got)
    while mix.out:
        in_flight([mix, gate_up, small_sum], lambda: ())
    own_gate, own_up = gate_up.finish()
    own_qkv, own_rest = mix.finish()

    flat = small_sum.finish()
    small, spot = [], 0
    dims_of = ((width,), (width,), low_first.shape, low_second.shape, (512,), (VAL,))
    for part, dims in zip(parts, dims_of):
        size = part.size // 128
        small.append(flat[spot : spot + size].reshape(dims))
        spot += size
    return (
        block_out,
        input_grad,
        own_qkv[:, :256],
        own_qkv[:, 256:512],
        own_qkv[:, 512:],
        own_rest[:, :512],
        own_rest[:, 512:].T,
        own_gate,
        own_up,
        jnp.concatenate([part.T for part in own_down], axis=0),
        *small,
    )


def solution(mesh):
    tokens = P(("dp", "tensor"))
    split_in = P("dp", "tensor")
    split_out = P("tensor", "dp")
    weights = (split_in,) * 4 + (split_out,) + (split_in,) * 2 + (split_out,)
    in_specs = (tokens, P("dp", None), tokens) + weights + (P(),) * 6
    out_specs = (tokens, tokens) + weights + (P(),) * 6
    return jax.shard_map(local, mesh=mesh, in_specs=in_specs, out_specs=out_specs, check_vma=False)
```

```python
import functools
import math

import jax
import jax.numpy as jnp
from jax import lax
from jax.experimental import pallas as pl
from jax.experimental.pallas import tpu as pltpu
from jax.sharding import PartitionSpec as P

HEADS = 4
KEY = 128
VAL = 256
CHUNK = 128
SCALE = KEY ** (-0.5)
F32 = jnp.float32
BF16 = jnp.bfloat16
HIGHEST = lax.Precision.HIGHEST
ALL = ("tensor", "dp")
VMEM_BYTES = 56 * 1024 * 1024
TILE = 256
WIDE = 512


def nn(a, b):
    return lax.dot_general(a, b, (((1,), (0,)), ((), ())), preferred_element_type=F32)


def nt(a, b):
    return lax.dot_general(a, b, (((1,), (1,)), ((), ())), preferred_element_type=F32)


def tn(a, b):
    return lax.dot_general(a, b, (((0,), (0,)), ((), ())), preferred_element_type=F32)


def triangle(lower):
    rows = lax.broadcasted_iota(jnp.int32, (CHUNK, CHUNK), 0)
    cols = lax.broadcasted_iota(jnp.int32, (CHUNK, CHUNK), 1)
    return rows >= cols if lower else rows <= cols


def split_sum(tri, x, terms):
    total = None
    for _ in range(terms):
        part = x.astype(BF16)
        x = x - part.astype(F32)
        term = nn(tri, part)
        total = term if total is None else total + term
    return total


def head_cols(h, width):
    return h // 2, slice((h % 2) * width, (h % 2 + 1) * width)


def head_pick(h, first, second):
    return (first if h % 2 == 0 else second)[h // 2]


def gate_kernel(info, low_ref, second_ref, bias_ref, k_ref, v0_ref, v1_ref, seg_ref, cum_ref, sig_ref, state_ref):
    c = pl.program_id(0)

    @pl.when(c == 0)
    def _():
        state_ref[...] = jnp.zeros_like(state_ref)

    logit = (
        jnp.dot(low_ref[...], second_ref[...], precision=HIGHEST, preferred_element_type=F32)
        + bias_ref[...]
    )
    e = jnp.exp(-jnp.abs(logit))
    decays = (jnp.minimum(logit, 0.0) - jnp.log1p(e)) * (1.0 / 16.0)
    sig_ref[...] = (jnp.where(logit >= 0, e, 1.0) / (1.0 + e)).astype(BF16)
    tri = triangle(True).astype(F32).astype(BF16)
    cum = split_sum(tri, decays, 3)
    cum_ref[...] = cum
    final = cum[CHUNK - 1 :, :]
    tail = (seg_ref[...] == info[1, c]).astype(F32)
    retain = (info[1, c] == info[0, c]).astype(F32)
    tail_decay = jnp.exp(final - cum) * tail
    keep = jnp.exp(final) * retain
    for h in range(HEADS):
        p, kc = head_cols(h, KEY)
        hk = slice(h * KEY, (h + 1) * KEY)
        kt = (k_ref[p, :, kc].astype(F32) * tail_decay[:, hk]).astype(BF16)
        state_ref[h] = state_ref[h] * keep[:, hk].reshape(KEY, 1) + tn(kt, head_pick(h, v0_ref, v1_ref))


def core_kernel(
    info, q_ref, k_ref, v0_ref, v1_ref, og0_ref, og1_ref, cum_ref, seg_ref, row_ref, first_ref, gain_ref,
    mixed_ref, core_ref, states_ref, state,
):
    c = pl.program_id(0)

    @pl.when(c == 0)
    def _():
        state[...] = first_ref[...].astype(F32)

    before, last = info[0, c], info[1, c]
    seg = seg_ref[...]
    mask = triangle(True) & (seg == row_ref[0])
    running = (seg == before).astype(F32)
    tail = (seg == last).astype(F32)
    retain = (last == before).astype(F32)
    cum = cum_ref[...]
    final = cum[CHUNK - 1 :, :]
    mid = cum[CHUNK // 2 - 1 : CHUNK // 2, :]
    up, down = jnp.exp(cum - mid), jnp.exp(mid - cum)
    whole = jnp.exp(cum) * running
    rest = jnp.exp(final - cum) * tail
    keep = jnp.exp(final) * retain
    for h in range(HEADS):
        p, kc = head_cols(h, KEY)
        hk = slice(h * KEY, (h + 1) * KEY)
        q = q_ref[p, :, kc].astype(F32) * SCALE
        k = k_ref[p, :, kc].astype(F32)
        v = head_pick(h, v0_ref, v1_ref)
        s = state[h]
        s_low = s.astype(BF16)
        states_ref[0, h] = s_low
        scores = nt((q * up[:, hk]).astype(BF16), (k * down[:, hk]).astype(BF16))
        scores = jnp.where(mask, scores, 0.0).astype(BF16)
        core = nn((q * whole[:, hk]).astype(BF16), s_low) + nn(scores, v)
        state[h] = s * keep[:, hk].reshape(KEY, 1) + tn((k * rest[:, hk]).astype(BF16), v)
        normed = core * lax.rsqrt(jnp.mean(core * core, axis=-1, keepdims=True) + 1.0)
        og = head_pick(h, og0_ref, og1_ref).astype(F32)
        hv = slice(h * VAL, (h + 1) * VAL)
        mixed = normed * gain_ref[...] * (og * jax.nn.sigmoid(og))
        mixed_ref[p, :, head_cols(h, VAL)[1]] = mixed.astype(BF16)
        core_ref[:, hv] = core.astype(BF16)


def post_kernel(
    info, dm_ref, core_ref, og0_ref, og1_ref, q_ref, cum_ref, seg_ref, gain_ref,
    dcore_ref, dog_ref, dgain_ref, dstate_ref, prefix,
):
    c = pl.program_id(0)

    @pl.when(c == 0)
    def _():
        prefix[...] = jnp.zeros_like(prefix)
        dgain_ref[...] = jnp.zeros_like(dgain_ref)
        dstate_ref[...] = jnp.zeros_like(dstate_ref)

    running = (seg_ref[...] == info[0, 0]).astype(F32)
    cum = cum_ref[...]
    decay = jnp.exp(cum + prefix[...]) * running * SCALE
    prefix[...] += cum[CHUNK - 1 :, :]
    gain = gain_ref[...]
    total = jnp.zeros((1, VAL), F32)
    for h in range(HEADS):
        p, kc = head_cols(h, KEY)
        hk = slice(h * KEY, (h + 1) * KEY)
        hv = slice(h * VAL, (h + 1) * VAL)
        core = core_ref[:, hv].astype(F32)
        scale = lax.rsqrt(jnp.mean(core * core, axis=-1, keepdims=True) + 1.0)
        normed = core * scale
        og = head_pick(h, og0_ref, og1_ref).astype(F32)
        sig = jax.nn.sigmoid(og)
        silu = og * sig
        dm = dm_ref[:, hv].astype(F32)
        both = dm * normed
        total += jnp.sum(both * silu, axis=0, keepdims=True)
        dog_ref[p, :, head_cols(h, VAL)[1]] = (both * gain * (sig * (1.0 + og * (1.0 - sig)))).astype(BF16)
        dn = dm * gain * silu
        dcore = scale * (dn - normed * jnp.mean(dn * normed, axis=-1, keepdims=True))
        dcore = dcore.astype(BF16)
        dcore_ref[:, hv] = dcore
        qa = (q_ref[p, :, kc].astype(F32) * decay[:, hk]).astype(BF16)
        dstate_ref[h] += tn(qa, dcore)
    dgain_ref[...] += total


def back_kernel(
    info, q_ref, k_ref, v0_ref, v1_ref, cum_ref, sig_ref, states_ref, dcore_ref, seg_ref, row_ref,
    first_ref, second_ref, low_ref, dqkv_ref, drank_ref, dsecond_ref, dbias_ref, dstate,
):
    i = pl.program_id(0)
    c = pl.num_programs(0) - 1 - i

    @pl.when(i == 0)
    def _():
        dstate[...] = first_ref[...].astype(F32)
        dsecond_ref[...] = jnp.zeros_like(dsecond_ref)
        dbias_ref[...] = jnp.zeros_like(dbias_ref)

    before, last = info[0, c], info[1, c]
    seg = seg_ref[...]
    mask = triangle(True) & (seg == row_ref[0])
    upper = triangle(False).astype(F32).astype(BF16)
    running = (seg == before).astype(F32)
    tail = (seg == last).astype(F32)
    retain = (last == before).astype(F32)
    cum = cum_ref[...]
    final = cum[CHUNK - 1 :, :]
    mid = cum[CHUNK // 2 - 1 : CHUNK // 2, :]
    up, down = jnp.exp(cum - mid), jnp.exp(mid - cum)
    whole = jnp.exp(cum) * running
    rest = jnp.exp(final - cum) * tail
    keep = jnp.exp(final) * retain
    logits = []
    for h in range(HEADS):
        p, kc = head_cols(h, KEY)
        hk = slice(h * KEY, (h + 1) * KEY)
        hv = slice(h * VAL, (h + 1) * VAL)
        q = q_ref[p, :, kc].astype(F32) * SCALE
        k = k_ref[p, :, kc].astype(F32)
        v = head_pick(h, v0_ref, v1_ref)
        do = dcore_ref[:, hv]
        s = states_ref[0, h]
        ds = dstate[h]
        ds_low = ds.astype(BF16)
        q_up = (q * up[:, hk]).astype(BF16)
        k_down = (k * down[:, hk]).astype(BF16)
        q_whole = (q * whole[:, hk]).astype(BF16)
        k_rest = (k * rest[:, hk]).astype(BF16)
        scores = jnp.where(mask, nt(q_up, k_down), 0.0).astype(BF16)
        dscores = jnp.where(mask, nt(do, v), 0.0).astype(BF16)
        dq_up = nn(dscores, k_down)
        dk_down = tn(dscores, q_up)
        dq_whole = nt(do, s)
        dk_rest = nt(v, ds_low)
        dv = tn(scores, do) + nn(k_rest, ds_low)
        dq = dq_up * up[:, hk] + dq_whole * whole[:, hk]
        dk = dk_down * down[:, hk] + dk_rest * rest[:, hk]
        from_rest = k_rest.astype(F32) * dk_rest
        dcum = (
            q_up.astype(F32) * dq_up
            - k_down.astype(F32) * dk_down
            + q_whole.astype(F32) * dq_whole
            - from_rest
        )
        kept = keep[:, hk].reshape(KEY, 1)
        through = jnp.sum(s.astype(F32) * ds, axis=1, keepdims=True) * kept
        dfinal = through.reshape(1, KEY) + jnp.sum(from_rest, axis=0, keepdims=True)
        ddecay = split_sum(upper, dcum, 2) + dfinal
        dstate[h] = ds * kept + tn(q_whole, do)
        logits.append(ddecay * (sig_ref[:, hk].astype(F32) * (1.0 / 16.0)))
        vc = head_cols(h, VAL)[1]
        dqkv_ref[p, :, kc] = (dq * SCALE).astype(BF16)
        dqkv_ref[p, :, slice(256 + kc.start, 256 + kc.stop)] = dk.astype(BF16)
        dqkv_ref[p, :, slice(512 + vc.start, 512 + vc.stop)] = dv.astype(BF16)
    dlogit = jnp.concatenate(logits, axis=1)
    dbias_ref[...] += jnp.sum(dlogit, axis=0, keepdims=True)
    low = dlogit.astype(BF16)
    dsecond_ref[...] += tn(low_ref[...].astype(BF16), low)
    drank_ref[...] = nt(low, second_ref[...].astype(BF16))


def rms_rows(x):
    scale = lax.rsqrt(jnp.mean(x * x, axis=-1, keepdims=True) + 1e-6)
    return x * scale, scale


def rms_rows_back(normed, scale, gain, grad):
    dn = grad * gain
    return scale * (dn - normed * jnp.mean(dn * normed, axis=-1, keepdims=True))


def output_rows(w_refs, p):
    return jnp.concatenate([ref[p] for ref in w_refs], axis=1)


def middle_kernel(mixed_ref, w0, w1, w2, w3, hidden_ref, gain_ref, middle_ref, normed_ref, cols_ref):
    middle = hidden_ref[...].astype(F32)
    for p in range(2):
        middle += nt(mixed_ref[p], output_rows((w0, w1, w2, w3), p))
    middle_ref[...] = middle
    normed = (rms_rows(middle)[0] * gain_ref[...]).astype(BF16)
    normed_ref[...] = normed
    cols_ref[...] = normed.T


def ff_kernel(normed_ref, dout_ref, wg_ref, wu_ref, wd_ref, first_ref, second_ref, dpre_ref):
    gate = nn(normed_ref[...], wg_ref[0])
    up = nn(normed_ref[...], wu_ref[0])
    sig = jax.nn.sigmoid(gate)
    silu = gate * sig
    activ = (silu * up).astype(BF16)
    cut = first_ref.shape[-1]
    first_ref[0] = activ[:, :cut]
    second_ref[0] = activ[:, cut:]
    d_activ = nn(dout_ref[...], wd_ref[0])
    dpre_ref[0, 0] = (d_activ * up * (sig * (1.0 + gate * (1.0 - sig)))).astype(BF16)
    dpre_ref[1, 0] = (d_activ * silu).astype(BF16)


def feed_kernel(first_ref, second_ref, wd_ref, middle_ref, out_ref, total):
    p, m = pl.program_id(0), pl.program_id(1)
    cut = first_ref.shape[-1]
    part = nt(first_ref[0], wd_ref[0, :, :cut]) + nt(second_ref[0], wd_ref[0, :, cut:])

    @pl.when(p == 0)
    def _():
        total[m] = part

    @pl.when(p == 1)
    def _():
        out_ref[...] = (middle_ref[...] + total[m] + part).astype(BF16)


def middle_back_kernel(
    dpre_ref, wg_ref, wu_ref, w0, w1, w2, w3, middle_ref, dout_ref, gain_ref,
    dmiddle_ref, dmix_ref, cols_ref, dmixed_ref, dgain_ref, total,
):
    p, m = pl.program_id(0), pl.program_id(1)
    part = nt(dpre_ref[0, 0], wg_ref[0]) + nt(dpre_ref[1, 0], wu_ref[0])

    @pl.when((p == 0) & (m == 0))
    def _():
        dgain_ref[...] = jnp.zeros_like(dgain_ref)

    @pl.when(p == 0)
    def _():
        total[m] = part

    @pl.when(p == 1)
    def _():
        grad = total[m] + part
        normed, scale = rms_rows(middle_ref[...])
        dgain_ref[...] += jnp.sum(grad * normed, axis=0, keepdims=True)
        dmiddle = dout_ref[...].astype(F32) + rms_rows_back(normed, scale, gain_ref[...], grad)
        dmiddle_ref[...] = dmiddle
        dmix = dmiddle.astype(BF16)
        dmix_ref[...] = dmix
        cols_ref[...] = dmix.T
        for q in range(2):
            dmixed_ref[:, q * 512 : (q + 1) * 512] = nn(
                dmix, output_rows((w0, w1, w2, w3), q)
            ).astype(BF16)


def input_back_kernel(
    dqkv_ref, dog_ref, wa_ref, wb_ref, drank_ref, first_ref, hidden_ref, dmiddle_ref, gain_ref,
    out_ref, dgain_ref,
):
    @pl.when(pl.program_id(0) == 0)
    def _():
        dgain_ref[...] = jnp.zeros_like(dgain_ref)

    grad = nt(drank_ref[...].astype(BF16), first_ref[...].astype(BF16))
    for p in range(2):
        grad += nt(dqkv_ref[p, :, :768], wa_ref[p])
        grad += nt(dqkv_ref[p, :, 768:], wb_ref[p, :, :256]) + nt(dog_ref[p], wb_ref[p, :, 256:])
    normed, scale = rms_rows(hidden_ref[...].astype(F32))
    dgain_ref[...] += jnp.sum(grad * normed, axis=0, keepdims=True)
    back = rms_rows_back(normed, scale, gain_ref[...], grad)
    out_ref[...] = (dmiddle_ref[...] + back).astype(BF16)


def products(refs, rows):
    at = 0
    for left, right in zip(refs[::2], refs[1::2]):
        cols = right.shape[-1]
        result = nn(left[0].reshape(rows, left.shape[-1]), right[...].reshape(-1, cols))
        yield result, slice(at, at + cols)
        at += cols


def grad_other_kernel(bits, *refs):
    out = refs[-1]
    rows = 2 * out.shape[2]
    for result, cols in products(refs[:-1], rows):
        out[0, :, :, cols] = result.astype(BF16).reshape(2, rows // 2, -1)


def grad_mine_kernel(by_x, bits, *refs):
    got, send, keep = refs[-3:]
    own = send.shape[1]
    for both, cols in products(refs[:-3], 2 * own):
        low = (both[:own] + got[0, 0, :, cols].astype(F32)).astype(BF16)
        high = (both[own:] + got[0, 1, :, cols].astype(F32)).astype(BF16)
        if by_x:

            @pl.when(bits[1] == 0)
            def _(low=low, high=high, cols=cols):
                send[0, :, cols] = high
                keep[0, :, cols] = low

            @pl.when(bits[1] == 1)
            def _(low=low, high=high, cols=cols):
                send[0, :, cols] = low
                keep[0, :, cols] = high
        else:

            @pl.when(pl.program_id(0) == 0)
            def _(low=low, high=high, cols=cols):
                send[0, :, cols] = low
                send[1, :, cols] = high

            @pl.when(pl.program_id(0) == 1)
            def _(low=low, high=high, cols=cols):
                keep[0, :, cols] = low
                keep[1, :, cols] = high


def add(x, y):
    return (x.astype(F32) + y.astype(F32)).astype(BF16)


def fold_kernel(bits, ka, ga, kb, gb, sa, na, sb, nb):
    p, x = bits[2], bits[1]
    sa[...] = add(ka[1 - p], ga[1 - p])
    na[...] = add(ka[p], ga[p])
    sb[...] = add(kb[1 - x], gb[1 - x])
    nb[...] = add(kb[x], gb[x])


def join_kernel(bits, ka, ga, kb, gb, *outs):
    cut = ka.shape[-1]
    for i, out in enumerate(outs):
        z = bits[3] ^ i
        out[:, :cut] = add(ka[z], ga[z])
        out[:, cut:] = add(kb[z], gb[z])


def shape(dims, dtype):
    return jax.ShapeDtypeStruct(dims, dtype)


def call(kernel, grid, in_specs, out_specs, out_shape, scratch, cost, prefetch=1):
    grid = grid if isinstance(grid, tuple) else (grid,)
    return pl.pallas_call(
        kernel,
        grid_spec=pltpu.PrefetchScalarGridSpec(
            num_scalar_prefetch=prefetch,
            grid=grid,
            in_specs=in_specs,
            out_specs=out_specs,
            scratch_shapes=scratch,
        ),
        out_shape=out_shape,
        compiler_params=pltpu.CompilerParams(
            dimension_semantics=("arbitrary",) * len(grid), vmem_limit_bytes=VMEM_BYTES
        ),
        cost_estimate=pl.CostEstimate(flops=cost, bytes_accessed=16 << 20, transcendentals=1 << 20),
    )


def specs(blocks, backward=False):
    def at(c):
        return blocks - 1 - c if backward else c

    def proj(width, place):
        return pl.BlockSpec((2, CHUNK, width), lambda c, _: (0, at(c), place))

    def rows(width):
        return pl.BlockSpec((CHUNK, width), lambda c, _: (at(c), 0))

    def full(*dims):
        return pl.BlockSpec(dims, lambda c, _: (0,) * len(dims))

    row = pl.BlockSpec((1, 1, CHUNK), lambda c, _: (at(c), 0, 0))
    states = pl.BlockSpec((1, HEADS, KEY, VAL), lambda c, _: (at(c), 0, 0, 0))
    return proj, rows, full, row, states


def rms(x, eps):
    return x * lax.rsqrt(jnp.mean(x * x, axis=-1, keepdims=True) + eps)


def rms_back(x, gain, eps, grad):
    scale = lax.rsqrt(jnp.mean(x * x, axis=-1, keepdims=True) + eps)
    normed = x * scale
    dn = grad * gain
    back = scale * (dn - normed * jnp.mean(dn * normed, axis=-1, keepdims=True))
    return back, jnp.sum(grad * normed, axis=0)


def gather(shard):
    return lax.all_gather(shard, ALL, axis=0, tiled=True).reshape(2, -1, shard.shape[1])


def swap(x, stride):
    if isinstance(stride, tuple):
        places = 2 * lax.axis_size("dp")
        return lax.ppermute(x, ("dp", "tensor"), [(i, i ^ stride[1]) for i in range(places)])
    if stride == 0:
        return lax.ppermute(x, "tensor", [(0, 1), (1, 0)])
    return lax.ppermute(x, "dp", [(i, i ^ stride) for i in range(lax.axis_size("dp"))])


def own_bit(stride):
    return lax.axis_index("tensor") if stride == 0 else (lax.axis_index("dp") // stride) % 2


def long_strides():
    strides, stride = [], 4
    while stride < lax.axis_size("dp"):
        strides.append(stride)
        stride *= 2
    return strides


def in_place(x, mid):
    steps = len(x.shape) - 2
    x_at, t_at = (2, 1) if mid[0] == 2 else (1, 2)
    z_axes = list(range(3, steps))[::-1]
    order = [t_at] + z_axes + [x_at, 0, steps, steps + 1]
    return x.transpose(order).reshape(2, -1, x.shape[-1])


def owner_rows(cols):
    count, rows = cols.shape
    z = len(long_strides())
    own = count // lax.axis_size("dp")
    split = cols.reshape((2,) * (z + 2) + (own, rows))
    split = split.transpose([z + 1, z] + list(range(z))[::-1] + [z + 2, z + 3])
    return split.reshape(2, 2, -1, rows)


class HopSum:
    def __init__(self, x):
        far = [2 * stride for stride in long_strides()]
        self.x, self.hops = x, [[4, 1], [2]] + [far[i : i + 2] for i in range(0, len(far), 2)]

    def sends(self):
        if not self.hops:
            return []
        hop = self.hops[0]
        return [(self.x, ("all", mask)) for mask in (hop if len(hop) == 1 else [*hop, sum(hop)])]

    def receive(self, got):
        if self.hops:
            self.x = self.x + sum(got)
            self.hops = self.hops[1:]

    def finish(self):
        while self.hops:
            in_flight([self], lambda: ())
        return self.x


class Growing:
    def __init__(self, x, strides):
        self.x, self.strides = x, list(strides)

    def sends(self):
        return [(self.x, self.strides[0])]

    def receive(self, got):
        bit, self.strides = own_bit(self.strides[0]), self.strides[1:]
        low, high = jnp.stack([self.x, got[0]]), jnp.stack([got[0], self.x])
        self.x = jnp.where(bit == 0, low, high)


def in_flight(movers, work, *inputs, also=()):
    sends = [mover.sends() for mover in movers]
    flat = [pair for group in sends for pair in group] + list(also)
    result, got = during(flat, work, *inputs)
    at = 0
    for mover, group in zip(movers, sends):
        mover.receive(got[at : at + len(group)])
        at += len(group)
    return result, got[at:]


def fence(*values):
    return lax.optimization_barrier(values)


def during(sends, work, *inputs):
    arrays, inputs = fence([array for array, _ in sends], inputs)
    got = [swap(array, stride) for array, (_, stride) in zip(arrays, sends)]
    return fence(work(*inputs), got)


def grad_specs(pairs, core, part):
    specs, operands, total = [], [], 0
    for left, right, *lead in pairs:
        own, rows = left.shape[2:]
        cols = right.shape[-1]
        specs.append(pl.BlockSpec((1, 2, own, rows), lambda s, b: (core(b), 0, 0, 0)))
        if lead:
            at = lead[0]
            specs.append(pl.BlockSpec((1, 1, rows, cols), lambda s, b, at=at: (at, part(s, b), 0, 0)))
        else:
            specs.append(pl.BlockSpec((1, rows, cols), lambda s, b: (part(s, b), 0, 0)))
        operands += [left, right]
        total += cols
    return specs, operands, own, rows, total


def grad_other(bits, pairs):
    specs, operands, own, rows, cols = grad_specs(pairs, lambda b: 1 - b[0], lambda s, b: s)
    return call(
        grad_other_kernel,
        2,
        specs,
        pl.BlockSpec((1, 2, own, cols), lambda s, b: (s, 0, 0, 0)),
        shape((2, 2, own, cols), BF16),
        [],
        8 * own * rows * cols,
    )(bits, *operands)


def grad_mine(bits, pairs, got, by_x):
    def part(s, b):
        return s if by_x else b[2] ^ 1 ^ s

    specs, operands, own, rows, cols = grad_specs(pairs, lambda b: b[0], part)
    specs.append(pl.BlockSpec((1, 2, own, cols), lambda s, b: (part(s, b), 0, 0, 0)))
    if by_x:
        out = pl.BlockSpec((1, own, cols), lambda s, b: (s, 0, 0))
    else:
        out = pl.BlockSpec((2, own, cols), lambda s, b: (0, 0, 0))
    return call(
        functools.partial(grad_mine_kernel, by_x),
        2,
        specs,
        [out, out],
        [shape((2, own, cols), BF16)] * 2,
        [],
        8 * own * rows * cols,
    )(bits, *operands, got)


def whole(kernel, bits, arrays, outs):
    def spec(dims):
        return pl.BlockSpec(dims, lambda i, b: (0,) * len(dims))

    return call(
        kernel, 1, [spec(a.shape) for a in arrays], [spec(dims) for dims in outs],
        [shape(dims, BF16) for dims in outs], [], 1 << 20,
    )(bits, *arrays)


class Halving:
    def __init__(self, bits, first, second):
        self.bits, self.stage = bits, 0
        (sa, ka), (sb, kb) = first, second
        self.keep, self.out, self.cut = [ka, kb], [(sa, 2), (sb, 0)], ka.shape[-1]
        strides = long_strides()
        self.groups = [strides[i : i + 2] for i in range(0, len(strides), 2)]

    def sends(self):
        return self.out

    def receive(self, got):
        if not self.out:
            return
        if self.stage == 0:
            (ka, kb), (ga, gb) = self.keep, got
            half_a, half_b = ka.shape[1:], kb.shape[1:]
            sa, na, sb, nb = whole(
                fold_kernel, self.bits, [ka, ga, kb, gb], [half_a, half_a, half_b, half_b]
            )
            self.keep, self.out = [na, nb], [(sa, 0), (sb, 2)]
        elif self.stage == 1:
            strides = self.groups.pop(0)
            arrays = [
                a.reshape(2 ** len(strides), -1, a.shape[-1])
                for a in (self.keep[0], got[0], self.keep[1], got[1])
            ]
            dims = (arrays[0].shape[1], arrays[0].shape[2] + arrays[2].shape[2])
            self.keep, *sends = whole(
                join_kernel, self.bits, arrays, [dims] * 2 ** len(strides)
            )
            self.out = [(send, self.mask(i + 1, strides)) for i, send in enumerate(sends)]
        else:
            total = self.keep + sum(got[1:], got[0])
            if self.groups:
                strides = self.groups.pop(0)
                total = total.reshape(2 ** len(strides), -1, total.shape[-1])
                at = sum(own_bit(stride) << i for i, stride in enumerate(strides[::-1]))
                parts = [
                    lax.dynamic_index_in_dim(total, at ^ i, 0, keepdims=False)
                    for i in range(2 ** len(strides))
                ]
                self.keep = parts[0]
                self.out = [(part, self.mask(i + 1, strides)) for i, part in enumerate(parts[1:])]
            else:
                self.keep, self.out = total.astype(F32), []
        self.stage += 1

    def mask(self, i, strides):
        return sum(((i >> place) & 1) * stride for place, stride in enumerate(strides[::-1]))

    def finish(self):
        while self.out:
            in_flight([self], lambda: ())
        return self.keep[:, : self.cut], self.keep[:, self.cut :]


def local(
    hidden_in, lengths, cotangent, query_weight, key_weight, value_weight, outgate_weight,
    output_weight, gate_weight, up_weight, down_weight, mixer_gain, feed_gain, low_first,
    low_second, decay_bias, head_gain,
):
    rows, width = hidden_in.shape
    blocks = rows // CHUNK
    place = lax.axis_index("tensor")
    half = gate_weight.shape[1]

    starts = jnp.cumsum(lengths[0]) - lengths[0]
    spots = place * rows + jnp.arange(-1, rows, dtype=jnp.int32)
    segments = jnp.sum((spots[:, None] >= starts[None, 1:]).astype(jnp.int32), axis=1)
    segments = jnp.where(spots < 0, -1, segments)
    seg = segments[1:].reshape(rows, 1)
    seg_row = segments[1:].reshape(blocks, 1, CHUNK)
    info = jnp.stack([segments[:-1].reshape(blocks, CHUNK)[:, 0], seg_row[:, 0, -1]])

    w_rest = gather(
        jnp.concatenate([gate_weight, up_weight, down_weight.T, output_weight.T], axis=1)
    )
    dp_at = lax.axis_index("dp")
    z_at = sum(own_bit(stride) << i for i, stride in enumerate(long_strides()[:2][::-1]))
    bits = jnp.stack([dp_at % 2, (dp_at // 2) % 2, place, z_at]).astype(jnp.int32)
    growing = Growing(
        jnp.concatenate([query_weight, key_weight, value_weight, outgate_weight], axis=1),
        long_strides()[::-1],
    )

    def norm(hidden_in):
        return (rms(hidden_in.astype(F32), 1e-6) * mixer_gain).astype(BF16)

    normed_a, _ = in_flight([growing], norm, hidden_in)
    while growing.strides:
        in_flight([growing], lambda: ())
    growing_a = Growing(growing.x[..., :768], (2, 0, 1))
    growing_b = Growing(growing.x[..., 768:], (0, 2, 1))

    def early(normed_a, cotangent):
        lowrank = jnp.dot(normed_a.astype(F32), low_first, precision=HIGHEST)
        return lowrank, owner_rows(cotangent.T), owner_rows(normed_a.T)

    (lowrank, dout_rows, normed_a_rows), _ = in_flight(
        [growing_a, growing_b], early, normed_a, cotangent
    )
    in_flight([growing_a, growing_b], lambda: ())
    in_flight([growing_a, growing_b], lambda: ())
    w_in_a, w_in_b = in_place(growing_a.x, (2, 0)), in_place(growing_b.x, (0, 2))

    proj_a = jnp.einsum("td,pdc->ptc", normed_a, w_in_a, preferred_element_type=F32).astype(BF16)
    proj_v = jnp.einsum(
        "td,pdc->ptc", normed_a, w_in_b[..., :256], preferred_element_type=F32
    ).astype(BF16)
    gain = head_gain.reshape(1, VAL)
    p_spec, r_spec, f_spec, row_spec, s_spec = specs(blocks)
    state_f32 = shape((HEADS, KEY, VAL), F32)
    cum, sig, final_state = call(
        gate_kernel,
        blocks,
        [r_spec(16), f_spec(16, 512), f_spec(1, 512), p_spec(256, 1), p_spec(256, 2),
         p_spec(256, 0), r_spec(1)],
        [r_spec(512), r_spec(512), f_spec(HEADS, KEY, VAL)],
        [shape((rows, 512), F32), shape((rows, 512), BF16), state_f32],
        [],
        1 << 29,
    )(info, lowrank, low_second, decay_bias.reshape(1, 512), proj_a, proj_a, proj_v, seg)
    def outgate_product(act, weight):
        return jnp.einsum("td,pdc->ptc", act, weight, preferred_element_type=F32).astype(BF16)

    proj_og, (state_in,) = during(
        [(final_state.astype(BF16), 0)], outgate_product, normed_a, w_in_b[..., 256:]
    )
    state_in = jnp.where(place == 0, jnp.zeros_like(state_in), state_in)
    mixed, core, states = call(
        core_kernel,
        blocks,
        [p_spec(256, 0), p_spec(256, 1), p_spec(256, 2), p_spec(256, 0), p_spec(256, 0), p_spec(256, 1),
         r_spec(512), r_spec(1), row_spec, f_spec(HEADS, KEY, VAL), f_spec(1, VAL)],
        [p_spec(512, 0), r_spec(1024), s_spec],
        [shape((2, rows, 512), BF16), shape((rows, 1024), BF16),
         shape((blocks, HEADS, KEY, VAL), BF16)],
        [pltpu.VMEM((HEADS, KEY, VAL), F32)],
        1 << 30,
    )(info, proj_a, proj_a, proj_a, proj_v, proj_og, proj_og, cum, seg, seg_row, state_in, gain)

    tiles, wides = rows // TILE, rows // WIDE
    cut = 768
    place_out = 3 * half // 128

    def tile(cols, size=TILE):
        return pl.BlockSpec((size, cols), lambda m: (m, 0))

    def tile_pair(cols, size=TILE):
        return pl.BlockSpec((2, size, cols), lambda m: (0, m, 0))

    def keep(*dims, at=None):
        return pl.BlockSpec(dims, lambda *_: at or (0,) * len(dims))

    def part(cols):
        return pl.BlockSpec((1, WIDE, cols), lambda p, m: (p, m, 0))

    def part_weight(at):
        return pl.BlockSpec((1, width, half), lambda p, m: (p, 0, at))

    part_pair = pl.BlockSpec((2, 1, WIDE, half), lambda p, m: (0, p, m, 0))
    part_rows = pl.BlockSpec((WIDE, width), lambda p, m: (m, 0))
    late_rows = pl.BlockSpec((WIDE, width), lambda p, m: (p * m, 0))
    late_cols = pl.BlockSpec((width, WIDE), lambda p, m: (0, p * m))
    w_out = [keep(2, width, 128, at=(0, 0, place_out + i)) for i in range(4)]
    gain_b, gain_a = feed_gain.reshape(1, width), mixer_gain.reshape(1, width)
    middle, normed_b, normed_b_cols = call(
        middle_kernel,
        tiles,
        [tile_pair(512), *w_out, tile(width), keep(1, width)],
        [tile(width), tile(width), pl.BlockSpec((width, TILE), lambda m: (0, m))],
        [shape((rows, width), F32), shape((rows, width), BF16), shape((width, rows), BF16)],
        [],
        2 * rows * width * 1024,
        0,
    )(mixed, w_rest, w_rest, w_rest, w_rest, hidden_in, gain_b)
    activ_a, activ_b, d_pre = call(
        ff_kernel,
        (2, wides),
        [part_rows, part_rows, part_weight(0), part_weight(1), part_weight(2)],
        [part(cut), part(half - cut), part_pair],
        [shape((2, rows, cut), BF16), shape((2, rows, half - cut), BF16),
         shape((2, 2, rows, half), BF16)],
        [],
        12 * rows * width * half,
        0,
    )(normed_b, cotangent, w_rest, w_rest, w_rest)

    def two_halves(first, second):
        sent = grad_other(bits, first)
        sent_b, (got_a,) = in_flight([], lambda: grad_other(bits, second), also=[(sent, 1)])
        mine_a, (got_b,) = in_flight(
            [], lambda got: grad_mine(bits, first, got, True), got_a, also=[(sent_b, 1)]
        )
        return mine_a, grad_mine(bits, second, got_b, False)

    normed_rows = owner_rows(normed_b_cols)
    gate_up = Halving(bits, *two_halves([(normed_rows, d_pre, 0)], [(normed_rows, d_pre, 1)]))
    down_a, down_b = [(dout_rows, activ_a)], [(dout_rows, activ_b)]

    def middle_back(d_pre, weight, middle, dout):
        results = call(
            middle_back_kernel,
            (2, wides),
            [part_pair, part_weight(0), part_weight(1), *w_out, late_rows, late_rows, keep(1, width)],
            [late_rows, late_rows, late_cols, late_rows, keep(1, width)],
            [shape((rows, width), F32), shape((rows, width), BF16), shape((width, rows), BF16),
             shape((rows, 1024), BF16), shape((1, width), F32)],
            [pltpu.VMEM((wides, WIDE, width), F32)],
            8 * rows * width * half,
            0,
        )(d_pre, weight, weight, weight, weight, weight, weight, middle, dout, gain_b)
        return results, [grad_other(bits, down_a), grad_other(bits, down_b)]

    (results, sent_down), _ = in_flight([gate_up], middle_back, d_pre, w_rest, middle, cotangent)
    d_middle, d_mix, d_mix_cols, d_mixed, feed_gain_grad = results

    def post_back(d_mixed, d_mix_cols):
        results = call(
            post_kernel,
            blocks,
            [r_spec(1024), r_spec(1024), p_spec(256, 0), p_spec(256, 1), p_spec(256, 0), r_spec(512),
             r_spec(1), f_spec(1, VAL)],
            [r_spec(1024), p_spec(512, 0), f_spec(1, VAL), f_spec(HEADS, KEY, VAL)],
            [shape((rows, 1024), BF16), shape((2, rows, 512), BF16), shape((1, VAL), F32), state_f32],
            [pltpu.VMEM((1, 512), F32)],
            1 << 29,
        )(info, d_mixed, core, proj_og, proj_og, proj_a, cum, seg, gain)
        return results, owner_rows(d_mix_cols)

    (results, mix_rows), got_down = in_flight(
        [gate_up], post_back, d_mixed, d_mix_cols, also=[(array, 1) for array in sent_down]
    )
    d_core, d_og, head_gain_grad, d_state = results
    mix_b = [(normed_a_rows, d_og), (mix_rows, mixed)]
    p_back, r_back, f_back, row_back, s_back = specs(blocks, True)

    def beside_state(*got_down):
        kept = grad_mine(bits, down_a, got_down[0], True), grad_mine(bits, down_b, got_down[1], False)
        return kept, grad_other(bits, mix_b)

    def core_back(d_core, d_state_in):
        d_qkv, d_rank, low_second_grad, bias_grad = call(
            back_kernel,
            blocks,
            [p_back(256, 0), p_back(256, 1), p_back(256, 2), p_back(256, 0),
             r_back(512), r_back(512), s_back, r_back(1024), r_back(1), row_back,
             f_back(HEADS, KEY, VAL), f_back(16, 512), r_back(16)],
            [p_back(1024, 0), r_back(16), f_back(16, 512), f_back(1, 512)],
            [shape((2, rows, 1024), BF16), shape((rows, 16), F32), shape((16, 512), F32),
             shape((1, 512), F32)],
            [pltpu.VMEM((HEADS, KEY, VAL), F32)],
            3 << 30,
        )(info, proj_a, proj_a, proj_a, proj_v, cum, sig, states, d_core, seg, seg_row,
          d_state_in, low_second, lowrank)
        return d_qkv, d_rank, low_second_grad, bias_grad, grad_other(bits, [(normed_a_rows, d_qkv)])

    class Sent:
        pass

    sent = Sent()

    def through_core(d_core, d_state, *got_down):
        (kept, sent_b), (d_state_in,) = in_flight(
            [], beside_state, *got_down, also=[(d_state.astype(BF16), 0)]
        )
        sent.down = Halving(bits, *kept)
        d_state_in = jnp.where(place == 1, jnp.zeros_like(d_state_in), d_state_in)
        return in_flight([sent.down], core_back, d_core, d_state_in, also=[(sent_b, 1)])

    (results, (got_b,)), _ = in_flight([gate_up], through_core, d_core, d_state, *got_down)
    d_qkv, d_rank, low_second_grad, bias_grad, sent_a = results
    down = sent.down
    own_gate, own_up = gate_up.finish()

    def mine_rest(d_rank, got_b):
        return tn(normed_a, d_rank.astype(BF16)), grad_mine(bits, mix_b, got_b, False)

    (low_first_grad, half_b), (got_a,) = in_flight(
        [down], mine_rest, d_rank, got_b, also=[(sent_a, 1)]
    )
    mix = Halving(bits, grad_mine(bits, [(normed_a_rows, d_qkv)], got_a, True), half_b)

    def last(d_qkv, d_og, w_a, w_b, d_rank, d_middle):
        input_grad, mixer_gain_grad = call(
            input_back_kernel,
            wides,
            [tile_pair(1024, WIDE), tile_pair(512, WIDE), keep(2, width, 768),
             keep(2, width, 768), tile(16, WIDE), keep(width, 16), tile(width, WIDE),
             tile(width, WIDE), keep(1, width)],
            [tile(width, WIDE), keep(1, width)],
            [shape((rows, width), BF16), shape((1, width), F32)],
            [],
            4 * rows * width * 1536,
            0,
        )(d_qkv, d_og, w_a, w_b, d_rank, low_first, hidden_in, d_middle, gain_a)
        parts = (
            mixer_gain_grad, feed_gain_grad, low_first_grad, low_second_grad, bias_grad,
            head_gain_grad,
        )
        sent.small = HopSum(jnp.concatenate([grad.reshape(-1, 128) for grad in parts]))

        def feed_out(activ_a, activ_b, weight, middle):
            return call(
                feed_kernel,
                (2, wides),
                [part(cut), part(half - cut), part_weight(2), late_rows],
                late_rows,
                shape((rows, width), BF16),
                [pltpu.VMEM((wides, WIDE, width), F32)],
                4 * rows * width * half,
                0,
            )(activ_a, activ_b, weight, middle)

        block_out, _ = in_flight([sent.small], feed_out, activ_a, activ_b, w_rest, middle)
        return input_grad, block_out

    (input_grad, block_out), _ = in_flight(
        [mix, down], last, d_qkv, d_og, w_in_a, w_in_b, d_rank, d_middle
    )
    small_sum = sent.small
    while mix.out:
        in_flight([mix, down, small_sum], lambda: ())
    own_down = down.finish()
    own_qkv, own_rest = mix.finish()

    flat = small_sum.finish()
    small, spot = [], 0
    dims_of = ((width,), (width,), low_first.shape, low_second.shape, (512,), (VAL,))
    for dims in dims_of:
        size = math.prod(dims) // 128
        small.append(flat[spot : spot + size].reshape(dims))
        spot += size
    return (
        block_out,
        input_grad,
        own_qkv[:, :256],
        own_qkv[:, 256:512],
        own_qkv[:, 512:],
        own_rest[:, :512],
        own_rest[:, 512:].T,
        own_gate,
        own_up,
        jnp.concatenate([part.T for part in own_down], axis=0),
        *small,
    )


def solution(mesh):
    tokens = P(("dp", "tensor"))
    split_in = P("dp", "tensor")
    split_out = P("tensor", "dp")
    weights = (split_in,) * 4 + (split_out,) + (split_in,) * 2 + (split_out,)
    in_specs = (tokens, P("dp", None), tokens) + weights + (P(),) * 6
    out_specs = (tokens, tokens) + weights + (P(),) * 6
    return jax.shard_map(local, mesh=mesh, in_specs=in_specs, out_specs=out_specs, check_vma=False)
```

```python
import functools

import jax
import jax.numpy as jnp
from jax import lax
from jax.experimental import pallas as pl
from jax.experimental.pallas import tpu as pltpu
from jax.sharding import PartitionSpec as P

HEADS = 4
KEY = 128
VAL = 256
CHUNK = 128
SCALE = KEY ** (-0.5)
F32 = jnp.float32
BF16 = jnp.bfloat16
HIGHEST = lax.Precision.HIGHEST
ALL = ("tensor", "dp")
VMEM_BYTES = 56 * 1024 * 1024
TILE = 256
WIDE = 512


def nn(a, b):
    return lax.dot_general(a, b, (((1,), (0,)), ((), ())), preferred_element_type=F32)


def nt(a, b):
    return lax.dot_general(a, b, (((1,), (1,)), ((), ())), preferred_element_type=F32)


def tn(a, b):
    return lax.dot_general(a, b, (((0,), (0,)), ((), ())), preferred_element_type=F32)


def triangle(lower):
    rows = lax.broadcasted_iota(jnp.int32, (CHUNK, CHUNK), 0)
    cols = lax.broadcasted_iota(jnp.int32, (CHUNK, CHUNK), 1)
    return rows >= cols if lower else rows <= cols


def split_sum(tri, x, terms):
    total = None
    for _ in range(terms):
        part = x.astype(BF16)
        x = x - part.astype(F32)
        term = nn(tri, part)
        total = term if total is None else total + term
    return total


def head_cols(h, width):
    return h // 2, slice((h % 2) * width, (h % 2 + 1) * width)


def head_pick(h, first, second):
    return (first if h % 2 == 0 else second)[h // 2]


def gate_kernel(info, low_ref, second_ref, bias_ref, k_ref, v0_ref, v1_ref, seg_ref, cum_ref, sig_ref, state_ref):
    c = pl.program_id(0)

    @pl.when(c == 0)
    def _():
        state_ref[...] = jnp.zeros_like(state_ref)

    logit = (
        jnp.dot(low_ref[...], second_ref[...], precision=HIGHEST, preferred_element_type=F32)
        + bias_ref[...]
    )
    e = jnp.exp(-jnp.abs(logit))
    decays = (jnp.minimum(logit, 0.0) - jnp.log1p(e)) * (1.0 / 16.0)
    sig_ref[...] = (jnp.where(logit >= 0, e, 1.0) / (1.0 + e)).astype(BF16)
    tri = triangle(True).astype(F32).astype(BF16)
    cum = split_sum(tri, decays, 3)
    cum_ref[...] = cum
    final = cum[CHUNK - 1 :, :]
    tail = (seg_ref[...] == info[1, c]).astype(F32)
    retain = (info[1, c] == info[0, c]).astype(F32)
    tail_decay = jnp.exp(final - cum) * tail
    keep = jnp.exp(final) * retain
    for h in range(HEADS):
        p, kc = head_cols(h, KEY)
        hk = slice(h * KEY, (h + 1) * KEY)
        kt = (k_ref[p, :, kc].astype(F32) * tail_decay[:, hk]).astype(BF16)
        state_ref[h] = state_ref[h] * keep[:, hk].reshape(KEY, 1) + tn(kt, head_pick(h, v0_ref, v1_ref))


def core_kernel(
    info, q_ref, k_ref, v0_ref, v1_ref, og0_ref, og1_ref, cum_ref, seg_ref, row_ref, first_ref, gain_ref,
    mixed_ref, core_ref, states_ref, state,
):
    c = pl.program_id(0)

    @pl.when(c == 0)
    def _():
        state[...] = first_ref[...].astype(F32)

    before, last = info[0, c], info[1, c]
    seg = seg_ref[...]
    mask = triangle(True) & (seg == row_ref[0])
    running = (seg == before).astype(F32)
    tail = (seg == last).astype(F32)
    retain = (last == before).astype(F32)
    cum = cum_ref[...]
    final = cum[CHUNK - 1 :, :]
    mid = cum[CHUNK // 2 - 1 : CHUNK // 2, :]
    up, down = jnp.exp(cum - mid), jnp.exp(mid - cum)
    whole = jnp.exp(cum) * running
    rest = jnp.exp(final - cum) * tail
    keep = jnp.exp(final) * retain
    for h in range(HEADS):
        p, kc = head_cols(h, KEY)
        hk = slice(h * KEY, (h + 1) * KEY)
        q = q_ref[p, :, kc].astype(F32) * SCALE
        k = k_ref[p, :, kc].astype(F32)
        v = head_pick(h, v0_ref, v1_ref)
        s = state[h]
        s_low = s.astype(BF16)
        states_ref[0, h] = s_low
        scores = nt((q * up[:, hk]).astype(BF16), (k * down[:, hk]).astype(BF16))
        scores = jnp.where(mask, scores, 0.0).astype(BF16)
        core = nn((q * whole[:, hk]).astype(BF16), s_low) + nn(scores, v)
        state[h] = s * keep[:, hk].reshape(KEY, 1) + tn((k * rest[:, hk]).astype(BF16), v)
        normed = core * lax.rsqrt(jnp.mean(core * core, axis=-1, keepdims=True) + 1.0)
        og = head_pick(h, og0_ref, og1_ref).astype(F32)
        hv = slice(h * VAL, (h + 1) * VAL)
        mixed = normed * gain_ref[...] * (og * jax.nn.sigmoid(og))
        mixed_ref[p, :, head_cols(h, VAL)[1]] = mixed.astype(BF16)
        core_ref[:, hv] = core.astype(BF16)


def post_kernel(
    info, dm_ref, core_ref, og0_ref, og1_ref, q_ref, cum_ref, seg_ref, gain_ref,
    dcore_ref, dog_ref, dgain_ref, dstate_ref, prefix,
):
    c = pl.program_id(0)

    @pl.when(c == 0)
    def _():
        prefix[...] = jnp.zeros_like(prefix)
        dgain_ref[...] = jnp.zeros_like(dgain_ref)
        dstate_ref[...] = jnp.zeros_like(dstate_ref)

    running = (seg_ref[...] == info[0, 0]).astype(F32)
    cum = cum_ref[...]
    decay = jnp.exp(cum + prefix[...]) * running * SCALE
    prefix[...] += cum[CHUNK - 1 :, :]
    gain = gain_ref[...]
    total = jnp.zeros((1, VAL), F32)
    for h in range(HEADS):
        p, kc = head_cols(h, KEY)
        hk = slice(h * KEY, (h + 1) * KEY)
        hv = slice(h * VAL, (h + 1) * VAL)
        core = core_ref[:, hv].astype(F32)
        scale = lax.rsqrt(jnp.mean(core * core, axis=-1, keepdims=True) + 1.0)
        normed = core * scale
        og = head_pick(h, og0_ref, og1_ref).astype(F32)
        sig = jax.nn.sigmoid(og)
        silu = og * sig
        dm = dm_ref[:, hv].astype(F32)
        both = dm * normed
        total += jnp.sum(both * silu, axis=0, keepdims=True)
        dog_ref[p, :, head_cols(h, VAL)[1]] = (both * gain * (sig * (1.0 + og * (1.0 - sig)))).astype(BF16)
        dn = dm * gain * silu
        dcore = scale * (dn - normed * jnp.mean(dn * normed, axis=-1, keepdims=True))
        dcore = dcore.astype(BF16)
        dcore_ref[:, hv] = dcore
        qa = (q_ref[p, :, kc].astype(F32) * decay[:, hk]).astype(BF16)
        dstate_ref[h] += tn(qa, dcore)
    dgain_ref[...] += total


def back_kernel(
    info, q_ref, k_ref, v0_ref, v1_ref, cum_ref, sig_ref, states_ref, dcore_ref, seg_ref, row_ref,
    first_ref, second_ref, low_ref, dqkv_ref, drank_ref, dsecond_ref, dbias_ref, dstate,
):
    i = pl.program_id(0)
    c = pl.num_programs(0) - 1 - i

    @pl.when(i == 0)
    def _():
        dstate[...] = first_ref[...].astype(F32)
        dsecond_ref[...] = jnp.zeros_like(dsecond_ref)
        dbias_ref[...] = jnp.zeros_like(dbias_ref)

    before, last = info[0, c], info[1, c]
    seg = seg_ref[...]
    mask = triangle(True) & (seg == row_ref[0])
    upper = triangle(False).astype(F32).astype(BF16)
    running = (seg == before).astype(F32)
    tail = (seg == last).astype(F32)
    retain = (last == before).astype(F32)
    cum = cum_ref[...]
    final = cum[CHUNK - 1 :, :]
    mid = cum[CHUNK // 2 - 1 : CHUNK // 2, :]
    up, down = jnp.exp(cum - mid), jnp.exp(mid - cum)
    whole = jnp.exp(cum) * running
    rest = jnp.exp(final - cum) * tail
    keep = jnp.exp(final) * retain
    logits = []
    for h in range(HEADS):
        p, kc = head_cols(h, KEY)
        hk = slice(h * KEY, (h + 1) * KEY)
        hv = slice(h * VAL, (h + 1) * VAL)
        q = q_ref[p, :, kc].astype(F32) * SCALE
        k = k_ref[p, :, kc].astype(F32)
        v = head_pick(h, v0_ref, v1_ref)
        do = dcore_ref[:, hv]
        s = states_ref[0, h]
        ds = dstate[h]
        ds_low = ds.astype(BF16)
        q_up = (q * up[:, hk]).astype(BF16)
        k_down = (k * down[:, hk]).astype(BF16)
        q_whole = (q * whole[:, hk]).astype(BF16)
        k_rest = (k * rest[:, hk]).astype(BF16)
        scores = jnp.where(mask, nt(q_up, k_down), 0.0).astype(BF16)
        dscores = jnp.where(mask, nt(do, v), 0.0).astype(BF16)
        dq_up = nn(dscores, k_down)
        dk_down = tn(dscores, q_up)
        dq_whole = nt(do, s)
        dk_rest = nt(v, ds_low)
        dv = tn(scores, do) + nn(k_rest, ds_low)
        dq = dq_up * up[:, hk] + dq_whole * whole[:, hk]
        dk = dk_down * down[:, hk] + dk_rest * rest[:, hk]
        from_rest = k_rest.astype(F32) * dk_rest
        dcum = (
            q_up.astype(F32) * dq_up
            - k_down.astype(F32) * dk_down
            + q_whole.astype(F32) * dq_whole
            - from_rest
        )
        kept = keep[:, hk].reshape(KEY, 1)
        through = jnp.sum(s.astype(F32) * ds, axis=1, keepdims=True) * kept
        dfinal = through.reshape(1, KEY) + jnp.sum(from_rest, axis=0, keepdims=True)
        ddecay = split_sum(upper, dcum, 2) + dfinal
        dstate[h] = ds * kept + tn(q_whole, do)
        logits.append(ddecay * (sig_ref[:, hk].astype(F32) * (1.0 / 16.0)))
        vc = head_cols(h, VAL)[1]
        dqkv_ref[p, :, kc] = (dq * SCALE).astype(BF16)
        dqkv_ref[p, :, slice(256 + kc.start, 256 + kc.stop)] = dk.astype(BF16)
        dqkv_ref[p, :, slice(512 + vc.start, 512 + vc.stop)] = dv.astype(BF16)
    dlogit = jnp.concatenate(logits, axis=1)
    dbias_ref[...] += jnp.sum(dlogit, axis=0, keepdims=True)
    low = dlogit.astype(BF16)
    dsecond_ref[...] += tn(low_ref[...].astype(BF16), low)
    drank_ref[...] = nt(low, second_ref[...].astype(BF16))


def rms_rows(x):
    scale = lax.rsqrt(jnp.mean(x * x, axis=-1, keepdims=True) + 1e-6)
    return x * scale, scale


def rms_rows_back(normed, scale, gain, grad):
    dn = grad * gain
    return scale * (dn - normed * jnp.mean(dn * normed, axis=-1, keepdims=True))


def output_rows(w_refs, p):
    return jnp.concatenate([ref[p] for ref in w_refs], axis=1)


def middle_kernel(mixed_ref, w0, w1, w2, w3, hidden_ref, gain_ref, middle_ref, normed_ref, cols_ref):
    middle = hidden_ref[...].astype(F32)
    for p in range(2):
        middle += nt(mixed_ref[p], output_rows((w0, w1, w2, w3), p))
    middle_ref[...] = middle
    normed = (rms_rows(middle)[0] * gain_ref[...]).astype(BF16)
    normed_ref[...] = normed
    cols_ref[...] = normed.T


def ff_kernel(normed_ref, dout_ref, wg_ref, wu_ref, wd_ref, first_ref, second_ref, dpre_ref):
    gate = nn(normed_ref[...], wg_ref[0])
    up = nn(normed_ref[...], wu_ref[0])
    sig = jax.nn.sigmoid(gate)
    silu = gate * sig
    activ = (silu * up).astype(BF16)
    cut = first_ref.shape[-1]
    first_ref[0] = activ[:, :cut]
    second_ref[0] = activ[:, cut:]
    d_activ = nn(dout_ref[...], wd_ref[0])
    dpre_ref[0, 0] = (d_activ * up * (sig * (1.0 + gate * (1.0 - sig)))).astype(BF16)
    dpre_ref[1, 0] = (d_activ * silu).astype(BF16)


def feed_kernel(first_ref, second_ref, wd_ref, middle_ref, out_ref, total):
    p, m = pl.program_id(0), pl.program_id(1)
    cut = first_ref.shape[-1]
    part = nt(first_ref[0], wd_ref[0, :, :cut]) + nt(second_ref[0], wd_ref[0, :, cut:])

    @pl.when(p == 0)
    def _():
        total[m] = part

    @pl.when(p == 1)
    def _():
        out_ref[...] = (middle_ref[...] + total[m] + part).astype(BF16)


def middle_back_kernel(
    dpre_ref, wg_ref, wu_ref, w0, w1, w2, w3, middle_ref, dout_ref, gain_ref,
    dmiddle_ref, dmix_ref, cols_ref, dmixed_ref, dgain_ref, total,
):
    p, m = pl.program_id(0), pl.program_id(1)
    part = nt(dpre_ref[0, 0], wg_ref[0]) + nt(dpre_ref[1, 0], wu_ref[0])

    @pl.when((p == 0) & (m == 0))
    def _():
        dgain_ref[...] = jnp.zeros_like(dgain_ref)

    @pl.when(p == 0)
    def _():
        total[m] = part

    @pl.when(p == 1)
    def _():
        grad = total[m] + part
        normed, scale = rms_rows(middle_ref[...])
        dgain_ref[...] += jnp.sum(grad * normed, axis=0, keepdims=True)
        dmiddle = dout_ref[...].astype(F32) + rms_rows_back(normed, scale, gain_ref[...], grad)
        dmiddle_ref[...] = dmiddle
        dmix = dmiddle.astype(BF16)
        dmix_ref[...] = dmix
        cols_ref[...] = dmix.T
        for q in range(2):
            dmixed_ref[:, q * 512 : (q + 1) * 512] = nn(
                dmix, output_rows((w0, w1, w2, w3), q)
            ).astype(BF16)


def input_back_kernel(
    dqkv_ref, dog_ref, wa_ref, wb_ref, drank_ref, first_ref, hidden_ref, dmiddle_ref, gain_ref,
    out_ref, dgain_ref,
):
    @pl.when(pl.program_id(0) == 0)
    def _():
        dgain_ref[...] = jnp.zeros_like(dgain_ref)

    grad = nt(drank_ref[...].astype(BF16), first_ref[...].astype(BF16))
    for p in range(2):
        grad += nt(dqkv_ref[p, :, :768], wa_ref[p])
        grad += nt(dqkv_ref[p, :, 768:], wb_ref[p, :, :256]) + nt(dog_ref[p], wb_ref[p, :, 256:])
    normed, scale = rms_rows(hidden_ref[...].astype(F32))
    dgain_ref[...] += jnp.sum(grad * normed, axis=0, keepdims=True)
    back = rms_rows_back(normed, scale, gain_ref[...], grad)
    out_ref[...] = (dmiddle_ref[...] + back).astype(BF16)


def products(refs, rows):
    at = 0
    for left, right in zip(refs[::2], refs[1::2]):
        cols = right.shape[-1]
        result = nn(left[0].reshape(rows, left.shape[-1]), right[...].reshape(-1, cols))
        yield result, slice(at, at + cols)
        at += cols


def grad_other_kernel(count, bits, *refs):
    operands, (out_a, out_b) = refs[:-2], refs[-2:]
    step = pl.program_id(0)
    rows = 2 * out_a.shape[2]
    for place, out in enumerate((out_a, out_b)):
        own = operands[count:] or operands if place else operands[:count]

        @pl.when(step // 2 == place)
        def _(own=own, out=out):
            for result, cols in products(own, rows):
                out[0, :, :, cols] = result.astype(BF16).reshape(2, rows // 2, -1)


def grad_mine_kernel(count, bits, *refs):
    operands, (got_a, got_b, send_a, keep_a, send_b, keep_b) = refs[:-6], refs[-6:]
    step, x = pl.program_id(0), bits[1]
    own = send_a.shape[1]

    def halves(operands, got):
        for both, cols in products(operands, 2 * own):
            low = (both[:own] + got[0, 0, :, cols].astype(F32)).astype(BF16)
            high = (both[own:] + got[0, 1, :, cols].astype(F32)).astype(BF16)
            yield low, high, cols

    @pl.when(step < 2)
    def _():
        for low, high, cols in halves(operands[:count], got_a):

            @pl.when(x == 0)
            def _(low=low, high=high, cols=cols):
                send_a[0, :, cols] = high
                keep_a[0, :, cols] = low

            @pl.when(x == 1)
            def _(low=low, high=high, cols=cols):
                send_a[0, :, cols] = low
                keep_a[0, :, cols] = high

    @pl.when(step >= 2)
    def _():
        for low, high, cols in halves(operands[count:] or operands, got_b):

            @pl.when(step == 2)
            def _(low=low, high=high, cols=cols):
                send_b[0, :, cols] = low
                send_b[1, :, cols] = high

            @pl.when(step == 3)
            def _(low=low, high=high, cols=cols):
                keep_b[0, :, cols] = low
                keep_b[1, :, cols] = high


def half_other_kernel(bits, *refs):
    out = refs[-1]
    rows = 2 * out.shape[2]
    for result, cols in products(refs[:-1], rows):
        out[0, :, :, cols] = result.astype(BF16).reshape(2, rows // 2, -1)


def half_mine_kernel(by_x, bits, *refs):
    got, send, keep = refs[-3:]
    own = send.shape[1]
    for both, cols in products(refs[:-3], 2 * own):
        low = (both[:own] + got[0, 0, :, cols].astype(F32)).astype(BF16)
        high = (both[own:] + got[0, 1, :, cols].astype(F32)).astype(BF16)
        if by_x:

            @pl.when(bits[1] == 0)
            def _(low=low, high=high, cols=cols):
                send[0, :, cols] = high
                keep[0, :, cols] = low

            @pl.when(bits[1] == 1)
            def _(low=low, high=high, cols=cols):
                send[0, :, cols] = low
                keep[0, :, cols] = high
        else:

            @pl.when(pl.program_id(0) == 0)
            def _(low=low, high=high, cols=cols):
                send[0, :, cols] = low
                send[1, :, cols] = high

            @pl.when(pl.program_id(0) == 1)
            def _(low=low, high=high, cols=cols):
                keep[0, :, cols] = low
                keep[1, :, cols] = high


def add(x, y):
    return (x.astype(F32) + y.astype(F32)).astype(BF16)


def fold_kernel(bits, ka, ga, kb, gb, sa, na, sb, nb):
    p, x = bits[2], bits[1]
    sa[...] = add(ka[1 - p], ga[1 - p])
    na[...] = add(ka[p], ga[p])
    sb[...] = add(kb[1 - x], gb[1 - x])
    nb[...] = add(kb[x], gb[x])


def join_kernel(bits, ka, ga, kb, gb, *outs):
    cut = ka.shape[-1]
    for i, out in enumerate(outs):
        z = bits[3] ^ i
        out[:, :cut] = add(ka[z], ga[z])
        out[:, cut:] = add(kb[z], gb[z])


def shape(dims, dtype):
    return jax.ShapeDtypeStruct(dims, dtype)


def call(kernel, grid, in_specs, out_specs, out_shape, scratch, cost, prefetch=1):
    grid = grid if isinstance(grid, tuple) else (grid,)
    return pl.pallas_call(
        kernel,
        grid_spec=pltpu.PrefetchScalarGridSpec(
            num_scalar_prefetch=prefetch,
            grid=grid,
            in_specs=in_specs,
            out_specs=out_specs,
            scratch_shapes=scratch,
        ),
        out_shape=out_shape,
        compiler_params=pltpu.CompilerParams(
            dimension_semantics=("arbitrary",) * len(grid), vmem_limit_bytes=VMEM_BYTES
        ),
        cost_estimate=pl.CostEstimate(flops=cost, bytes_accessed=16 << 20, transcendentals=1 << 20),
    )


def specs(blocks, backward=False):
    def at(c):
        return blocks - 1 - c if backward else c

    def proj(width, place):
        return pl.BlockSpec((2, CHUNK, width), lambda c, _: (0, at(c), place))

    def rows(width):
        return pl.BlockSpec((CHUNK, width), lambda c, _: (at(c), 0))

    def full(*dims):
        return pl.BlockSpec(dims, lambda c, _: (0,) * len(dims))

    row = pl.BlockSpec((1, 1, CHUNK), lambda c, _: (at(c), 0, 0))
    states = pl.BlockSpec((1, HEADS, KEY, VAL), lambda c, _: (at(c), 0, 0, 0))
    return proj, rows, full, row, states


def rms(x, eps):
    return x * lax.rsqrt(jnp.mean(x * x, axis=-1, keepdims=True) + eps)


def rms_back(x, gain, eps, grad):
    scale = lax.rsqrt(jnp.mean(x * x, axis=-1, keepdims=True) + eps)
    normed = x * scale
    dn = grad * gain
    back = scale * (dn - normed * jnp.mean(dn * normed, axis=-1, keepdims=True))
    return back, jnp.sum(grad * normed, axis=0)


def gather(shard):
    return lax.all_gather(shard, ALL, axis=0, tiled=True).reshape(2, -1, shard.shape[1])


def swap(x, stride):
    if isinstance(stride, tuple):
        places = 2 * lax.axis_size("dp")
        return lax.ppermute(x, ("dp", "tensor"), [(i, i ^ stride[1]) for i in range(places)])
    if stride == 0:
        return lax.ppermute(x, "tensor", [(0, 1), (1, 0)])
    return lax.ppermute(x, "dp", [(i, i ^ stride) for i in range(lax.axis_size("dp"))])


def own_bit(stride):
    return lax.axis_index("tensor") if stride == 0 else (lax.axis_index("dp") // stride) % 2


def long_strides():
    strides, stride = [], 4
    while stride < lax.axis_size("dp"):
        strides.append(stride)
        stride *= 2
    return strides


def in_place(x, mid):
    steps = len(x.shape) - 2
    x_at, t_at = (2, 1) if mid[0] == 2 else (1, 2)
    z_axes = list(range(3, steps))[::-1]
    order = [t_at] + z_axes + [x_at, 0, steps, steps + 1]
    return x.transpose(order).reshape(2, -1, x.shape[-1])


def owner_rows(cols):
    count, rows = cols.shape
    z = len(long_strides())
    own = count // lax.axis_size("dp")
    split = cols.reshape((2,) * (z + 2) + (own, rows))
    split = split.transpose([z + 1, z] + list(range(z))[::-1] + [z + 2, z + 3])
    return split.reshape(2, 2, -1, rows)


class HopSum:
    def __init__(self, x):
        far = [2 * stride for stride in long_strides()]
        self.x, self.hops = x, [far[i : i + 2] for i in range(0, len(far), 2)] + [[4], [1], [2]]

    def sends(self):
        if not self.hops:
            return []
        hop = self.hops[0]
        return [(self.x, ("all", mask)) for mask in (hop if len(hop) == 1 else [*hop, sum(hop)])]

    def receive(self, got):
        if self.hops:
            self.x = self.x + sum(got)
            self.hops = self.hops[1:]

    def finish(self):
        while self.hops:
            in_flight([self], lambda: ())
        return self.x


class Growing:
    def __init__(self, x, strides):
        self.x, self.strides = x, list(strides)

    def sends(self):
        return [(self.x, self.strides[0])]

    def receive(self, got):
        bit, self.strides = own_bit(self.strides[0]), self.strides[1:]
        low, high = jnp.stack([self.x, got[0]]), jnp.stack([got[0], self.x])
        self.x = jnp.where(bit == 0, low, high)


def in_flight(movers, work, *inputs, also=()):
    sends = [mover.sends() for mover in movers]
    flat = [pair for group in sends for pair in group] + list(also)
    result, got = during(flat, work, *inputs)
    at = 0
    for mover, group in zip(movers, sends):
        mover.receive(got[at : at + len(group)])
        at += len(group)
    return result, got[at:]


def fence(*values):
    return lax.optimization_barrier(values)


def during(sends, work, *inputs):
    arrays, inputs = fence([array for array, _ in sends], inputs)
    got = [swap(array, stride) for array, (_, stride) in zip(arrays, sends)]
    return fence(work(*inputs), got)


def half_specs(halves, core, second_part):
    specs, operands = [], []
    for place, pairs in enumerate(halves):
        for left, right in pairs:
            own, rows = left.shape[2:]
            specs.append(pl.BlockSpec((1, 2, own, rows), lambda s, b: (core(b), 0, 0, 0)))
            cols = right.shape[-1]

            def part(s, b, place=place):
                return jnp.minimum(s, 1) if place == 0 else second_part(jnp.maximum(s - 2, 0), b)

            def at(s, b):
                return s // 2, jnp.where(s < 2, s, second_part(s - 2, b)), 0, 0

            if len(halves) == 1:
                specs.append(pl.BlockSpec((1, 1, rows, cols), at))
            else:
                specs.append(pl.BlockSpec((1, rows, cols), lambda s, b, part=part: (part(s, b), 0, 0)))
            operands += [left, right]
    widths = [sum(right.shape[-1] for _, right in halves[i]) for i in (0, -1)]
    return specs, operands, own, rows, widths


def grad_other(bits, *halves):
    in_specs, operands, own, rows, widths = half_specs(halves, lambda b: 1 - b[0], lambda s, b: s)
    dims = [(2, 2, own, cols) for cols in widths]
    return call(
        functools.partial(grad_other_kernel, 2 * len(halves[0])),
        4,
        in_specs,
        [
            pl.BlockSpec((1,) + dims[0][1:], lambda s, b: (jnp.minimum(s, 1), 0, 0, 0)),
            pl.BlockSpec((1,) + dims[1][1:], lambda s, b: (jnp.maximum(s - 2, 0), 0, 0, 0)),
        ],
        [shape(d, BF16) for d in dims],
        [],
        8 * own * rows * sum(widths),
    )(bits, *operands)


def grad_mine(bits, halves, got):
    def other_first(s, b):
        return b[2] ^ 1 ^ s

    in_specs, operands, own, rows, (cols_a, cols_b) = half_specs(halves, lambda b: b[0], other_first)
    in_specs.append(
        pl.BlockSpec((1, 2, own, cols_a), lambda s, b: (jnp.minimum(s, 1), 0, 0, 0))
    )
    in_specs.append(
        pl.BlockSpec(
            (1, 2, own, cols_b), lambda s, b: (other_first(jnp.maximum(s - 2, 0), b), 0, 0, 0)
        )
    )
    by_p = pl.BlockSpec((1, own, cols_a), lambda s, b: (jnp.minimum(s, 1), 0, 0))
    fixed = pl.BlockSpec((2, own, cols_b), lambda s, b: (0, 0, 0))
    send_a, keep_a, send_b, keep_b = call(
        functools.partial(grad_mine_kernel, 2 * len(halves[0])),
        4,
        in_specs,
        [by_p, by_p, fixed, fixed],
        [shape((2, own, cols_a), BF16)] * 2 + [shape((2, own, cols_b), BF16)] * 2,
        [],
        8 * own * rows * (cols_a + cols_b),
    )(bits, *operands, *got)
    return (send_a, keep_a), (send_b, keep_b)


def grad_specs(pairs, core, part):
    specs, operands, total = [], [], 0
    for left, right in pairs:
        own, rows = left.shape[2:]
        cols = right.shape[-1]
        specs.append(pl.BlockSpec((1, 2, own, rows), lambda s, b: (core(b), 0, 0, 0)))
        specs.append(pl.BlockSpec((1, rows, cols), lambda s, b: (part(s, b), 0, 0)))
        operands += [left, right]
        total += cols
    return specs, operands, own, rows, total


def half_other(bits, pairs):
    specs, operands, own, rows, cols = grad_specs(pairs, lambda b: 1 - b[0], lambda s, b: s)
    return call(
        half_other_kernel,
        2,
        specs,
        pl.BlockSpec((1, 2, own, cols), lambda s, b: (s, 0, 0, 0)),
        shape((2, 2, own, cols), BF16),
        [],
        8 * own * rows * cols,
    )(bits, *operands)


def half_mine(bits, pairs, got, by_x):
    def part(s, b):
        return s if by_x else b[2] ^ 1 ^ s

    specs, operands, own, rows, cols = grad_specs(pairs, lambda b: b[0], part)
    specs.append(pl.BlockSpec((1, 2, own, cols), lambda s, b: (part(s, b), 0, 0, 0)))
    if by_x:
        out = pl.BlockSpec((1, own, cols), lambda s, b: (s, 0, 0))
    else:
        out = pl.BlockSpec((2, own, cols), lambda s, b: (0, 0, 0))
    return call(
        functools.partial(half_mine_kernel, by_x),
        2,
        specs,
        [out, out],
        [shape((2, own, cols), BF16)] * 2,
        [],
        8 * own * rows * cols,
    )(bits, *operands, got)


def whole(kernel, bits, arrays, outs):
    def spec(dims):
        return pl.BlockSpec(dims, lambda i, b: (0,) * len(dims))

    return call(
        kernel, 1, [spec(a.shape) for a in arrays], [spec(dims) for dims in outs],
        [shape(dims, BF16) for dims in outs], [], 1 << 20,
    )(bits, *arrays)


class Halving:
    def __init__(self, bits, first, second):
        self.bits, self.stage = bits, 0
        (sa, ka), (sb, kb) = first, second
        self.keep, self.out, self.cut = [ka, kb], [(sa, 2), (sb, 0)], ka.shape[-1]
        strides = long_strides()
        self.groups = [strides[i : i + 2] for i in range(0, len(strides), 2)]

    def sends(self):
        return self.out

    def receive(self, got):
        if not self.out:
            return
        if self.stage == 0:
            (ka, kb), (ga, gb) = self.keep, got
            half_a, half_b = ka.shape[1:], kb.shape[1:]
            sa, na, sb, nb = whole(
                fold_kernel, self.bits, [ka, ga, kb, gb], [half_a, half_a, half_b, half_b]
            )
            self.keep, self.out = [na, nb], [(sa, 0), (sb, 2)]
        elif self.stage == 1:
            strides = self.groups.pop(0)
            arrays = [
                a.reshape(2 ** len(strides), -1, a.shape[-1])
                for a in (self.keep[0], got[0], self.keep[1], got[1])
            ]
            dims = (arrays[0].shape[1], arrays[0].shape[2] + arrays[2].shape[2])
            self.keep, *sends = whole(
                join_kernel, self.bits, arrays, [dims] * 2 ** len(strides)
            )
            self.out = [(send, self.mask(i + 1, strides)) for i, send in enumerate(sends)]
        else:
            total = self.keep + sum(got[1:], got[0])
            if self.groups:
                strides = self.groups.pop(0)
                total = total.reshape(2 ** len(strides), -1, total.shape[-1])
                at = sum(own_bit(stride) << i for i, stride in enumerate(strides[::-1]))
                parts = [
                    lax.dynamic_index_in_dim(total, at ^ i, 0, keepdims=False)
                    for i in range(2 ** len(strides))
                ]
                self.keep = parts[0]
                self.out = [(part, self.mask(i + 1, strides)) for i, part in enumerate(parts[1:])]
            else:
                self.keep, self.out = total.astype(F32), []
        self.stage += 1

    def mask(self, i, strides):
        return sum(((i >> place) & 1) * stride for place, stride in enumerate(strides[::-1]))

    def finish(self):
        while self.out:
            in_flight([self], lambda: ())
        return self.keep[:, : self.cut], self.keep[:, self.cut :]


def local(
    hidden_in, lengths, cotangent, query_weight, key_weight, value_weight, outgate_weight,
    output_weight, gate_weight, up_weight, down_weight, mixer_gain, feed_gain, low_first,
    low_second, decay_bias, head_gain,
):
    rows, width = hidden_in.shape
    blocks = rows // CHUNK
    place = lax.axis_index("tensor")
    half = gate_weight.shape[1]

    starts = jnp.cumsum(lengths[0]) - lengths[0]
    spots = place * rows + jnp.arange(-1, rows, dtype=jnp.int32)
    segments = jnp.sum((spots[:, None] >= starts[None, 1:]).astype(jnp.int32), axis=1)
    segments = jnp.where(spots < 0, -1, segments)
    seg = segments[1:].reshape(rows, 1)
    seg_row = segments[1:].reshape(blocks, 1, CHUNK)
    info = jnp.stack([segments[:-1].reshape(blocks, CHUNK)[:, 0], seg_row[:, 0, -1]])

    w_rest = gather(
        jnp.concatenate([gate_weight, up_weight, down_weight.T, output_weight.T], axis=1)
    )
    dp_at = lax.axis_index("dp")
    z_at = sum(own_bit(stride) << i for i, stride in enumerate(long_strides()[:2][::-1]))
    bits = jnp.stack([dp_at % 2, (dp_at // 2) % 2, place, z_at]).astype(jnp.int32)
    growing = Growing(
        jnp.concatenate([query_weight, key_weight, value_weight, outgate_weight], axis=1),
        long_strides()[::-1],
    )

    def norm(hidden_in):
        return (rms(hidden_in.astype(F32), 1e-6) * mixer_gain).astype(BF16)

    normed_a, _ = in_flight([growing], norm, hidden_in)
    while growing.strides:
        in_flight([growing], lambda: ())
    growing_a = Growing(growing.x[..., :768], (2, 0, 1))
    growing_b = Growing(growing.x[..., 768:], (0, 2, 1))

    def early(normed_a, cotangent):
        lowrank = jnp.dot(normed_a.astype(F32), low_first, precision=HIGHEST)
        return lowrank, owner_rows(cotangent.T), owner_rows(normed_a.T)

    (lowrank, dout_rows, normed_a_rows), _ = in_flight(
        [growing_a, growing_b], early, normed_a, cotangent
    )
    in_flight([growing_a, growing_b], lambda: ())
    in_flight([growing_a, growing_b], lambda: ())
    w_in_a, w_in_b = in_place(growing_a.x, (2, 0)), in_place(growing_b.x, (0, 2))

    proj_a = jnp.einsum("td,pdc->ptc", normed_a, w_in_a, preferred_element_type=F32).astype(BF16)
    proj_v = jnp.einsum(
        "td,pdc->ptc", normed_a, w_in_b[..., :256], preferred_element_type=F32
    ).astype(BF16)
    gain = head_gain.reshape(1, VAL)
    p_spec, r_spec, f_spec, row_spec, s_spec = specs(blocks)
    state_f32 = shape((HEADS, KEY, VAL), F32)
    cum, sig, final_state = call(
        gate_kernel,
        blocks,
        [r_spec(16), f_spec(16, 512), f_spec(1, 512), p_spec(256, 1), p_spec(256, 2),
         p_spec(256, 0), r_spec(1)],
        [r_spec(512), r_spec(512), f_spec(HEADS, KEY, VAL)],
        [shape((rows, 512), F32), shape((rows, 512), BF16), state_f32],
        [],
        1 << 29,
    )(info, lowrank, low_second, decay_bias.reshape(1, 512), proj_a, proj_a, proj_v, seg)
    def outgate_product(act, weight):
        return jnp.einsum("td,pdc->ptc", act, weight, preferred_element_type=F32).astype(BF16)

    proj_og, (state_in,) = during(
        [(final_state.astype(BF16), 0)], outgate_product, normed_a, w_in_b[..., 256:]
    )
    state_in = jnp.where(place == 0, jnp.zeros_like(state_in), state_in)
    mixed, core, states = call(
        core_kernel,
        blocks,
        [p_spec(256, 0), p_spec(256, 1), p_spec(256, 2), p_spec(256, 0), p_spec(256, 0), p_spec(256, 1),
         r_spec(512), r_spec(1), row_spec, f_spec(HEADS, KEY, VAL), f_spec(1, VAL)],
        [p_spec(512, 0), r_spec(1024), s_spec],
        [shape((2, rows, 512), BF16), shape((rows, 1024), BF16),
         shape((blocks, HEADS, KEY, VAL), BF16)],
        [pltpu.VMEM((HEADS, KEY, VAL), F32)],
        1 << 30,
    )(info, proj_a, proj_a, proj_a, proj_v, proj_og, proj_og, cum, seg, seg_row, state_in, gain)

    tiles, wides = rows // TILE, rows // WIDE
    cut = 768
    place_out = 3 * half // 128

    def tile(cols, size=TILE):
        return pl.BlockSpec((size, cols), lambda m: (m, 0))

    def tile_pair(cols, size=TILE):
        return pl.BlockSpec((2, size, cols), lambda m: (0, m, 0))

    def keep(*dims, at=None):
        return pl.BlockSpec(dims, lambda *_: at or (0,) * len(dims))

    def part(cols):
        return pl.BlockSpec((1, WIDE, cols), lambda p, m: (p, m, 0))

    def part_weight(at):
        return pl.BlockSpec((1, width, half), lambda p, m: (p, 0, at))

    part_pair = pl.BlockSpec((2, 1, WIDE, half), lambda p, m: (0, p, m, 0))
    part_rows = pl.BlockSpec((WIDE, width), lambda p, m: (m, 0))
    late_rows = pl.BlockSpec((WIDE, width), lambda p, m: (p * m, 0))
    late_cols = pl.BlockSpec((width, WIDE), lambda p, m: (0, p * m))
    w_out = [keep(2, width, 128, at=(0, 0, place_out + i)) for i in range(4)]
    gain_b, gain_a = feed_gain.reshape(1, width), mixer_gain.reshape(1, width)
    middle, normed_b, normed_b_cols = call(
        middle_kernel,
        tiles,
        [tile_pair(512), *w_out, tile(width), keep(1, width)],
        [tile(width), tile(width), pl.BlockSpec((width, TILE), lambda m: (0, m))],
        [shape((rows, width), F32), shape((rows, width), BF16), shape((width, rows), BF16)],
        [],
        2 * rows * width * 1024,
        0,
    )(mixed, w_rest, w_rest, w_rest, w_rest, hidden_in, gain_b)
    activ_a, activ_b, d_pre = call(
        ff_kernel,
        (2, wides),
        [part_rows, part_rows, part_weight(0), part_weight(1), part_weight(2)],
        [part(cut), part(half - cut), part_pair],
        [shape((2, rows, cut), BF16), shape((2, rows, half - cut), BF16),
         shape((2, 2, rows, half), BF16)],
        [],
        12 * rows * width * half,
        0,
    )(normed_b, cotangent, w_rest, w_rest, w_rest)

    down_pairs = [(dout_rows, activ_a)], [(dout_rows, activ_b)]
    sent = grad_other(bits, *down_pairs)

    def other_gate_up(normed_cols, d_pre):
        normed_rows = owner_rows(normed_cols)
        return normed_rows, grad_other(bits, [(normed_rows, d_pre)])

    (normed_rows, sent), got = in_flight(
        [], other_gate_up, normed_b_cols, d_pre, also=[(array, 1) for array in sent]
    )

    def middle_back(d_pre, weight, middle, dout):
        return call(
            middle_back_kernel,
            (2, wides),
            [part_pair, part_weight(0), part_weight(1), *w_out, late_rows, late_rows, keep(1, width)],
            [late_rows, late_rows, late_cols, late_rows, keep(1, width)],
            [shape((rows, width), F32), shape((rows, width), BF16), shape((width, rows), BF16),
             shape((rows, 1024), BF16), shape((1, width), F32)],
            [pltpu.VMEM((wides, WIDE, width), F32)],
            8 * rows * width * half,
            0,
        )(d_pre, weight, weight, weight, weight, weight, weight, middle, dout, gain_b)

    down = Halving(bits, *grad_mine(bits, down_pairs, got))
    (d_middle, d_mix, d_mix_cols, d_mixed, feed_gain_grad), got = in_flight(
        [down], middle_back, d_pre, w_rest, middle, cotangent, also=[(array, 1) for array in sent]
    )

    def post_back(d_mixed):
        return call(
            post_kernel,
            blocks,
            [r_spec(1024), r_spec(1024), p_spec(256, 0), p_spec(256, 1), p_spec(256, 0), r_spec(512),
             r_spec(1), f_spec(1, VAL)],
            [r_spec(1024), p_spec(512, 0), f_spec(1, VAL), f_spec(HEADS, KEY, VAL)],
            [shape((rows, 1024), BF16), shape((2, rows, 512), BF16), shape((1, VAL), F32), state_f32],
            [pltpu.VMEM((1, 512), F32)],
            1 << 29,
        )(info, d_mixed, core, proj_og, proj_og, proj_a, cum, seg, gain)

    (d_core, d_og, head_gain_grad, d_state), _ = in_flight([down], post_back, d_mixed)

    def mine_gate_up(normed_rows, d_pre, d_mix_cols, d_og, mixed, normed_a_rows, *got):
        mix_rows = owner_rows(d_mix_cols)
        halves = grad_mine(bits, [[(normed_rows, d_pre)]], got)
        return mix_rows, halves, half_other(bits, [(normed_a_rows, d_og), (mix_rows, mixed)])

    (mix_rows, halves, sent_b), (d_state_in,) = in_flight(
        [down], mine_gate_up, normed_rows, d_pre, d_mix_cols, d_og, mixed, normed_a_rows, *got,
        also=[(d_state.astype(BF16), 0)],
    )
    own_down = down.finish()
    gate_up = Halving(bits, *halves)
    d_state_in = jnp.where(place == 1, jnp.zeros_like(d_state_in), d_state_in)
    p_back, r_back, f_back, row_back, s_back = specs(blocks, True)

    def mixer_back(d_core, d_state_in, normed_a_rows):
        d_qkv, d_rank, low_second_grad, bias_grad = call(
            back_kernel,
            blocks,
            [p_back(256, 0), p_back(256, 1), p_back(256, 2), p_back(256, 0),
             r_back(512), r_back(512), s_back, r_back(1024), r_back(1), row_back,
             f_back(HEADS, KEY, VAL), f_back(16, 512), r_back(16)],
            [p_back(1024, 0), r_back(16), f_back(16, 512), f_back(1, 512)],
            [shape((2, rows, 1024), BF16), shape((rows, 16), F32), shape((16, 512), F32),
             shape((1, 512), F32)],
            [pltpu.VMEM((HEADS, KEY, VAL), F32)],
            3 << 30,
        )(info, proj_a, proj_a, proj_a, proj_v, cum, sig, states, d_core, seg, seg_row,
          d_state_in, low_second, lowrank)
        low_first_grad = tn(normed_a, d_rank.astype(BF16))
        sent_a = half_other(bits, [(normed_a_rows, d_qkv)])
        return d_qkv, d_rank, low_first_grad, low_second_grad, bias_grad, sent_a

    (d_qkv, d_rank, low_first_grad, low_second_grad, bias_grad, sent_a), (got_b,) = in_flight(
        [gate_up], mixer_back, d_core, d_state_in, normed_a_rows, also=[(sent_b, 1)]
    )

    def mine_mix(normed_a_rows, d_qkv, d_og, mix_rows, mixed, got_b, sent_a):
        half_b, (got_a,) = in_flight(
            [],
            lambda left, og, mix_left, mix_right, got: half_mine(
                bits, [(left, og), (mix_left, mix_right)], got, False
            ),
            normed_a_rows, d_og, mix_rows, mixed, got_b,
            also=[(sent_a, 1)],
        )
        return half_mine(bits, [(normed_a_rows, d_qkv)], got_a, True), half_b

    halves, _ = in_flight(
        [gate_up], mine_mix, normed_a_rows, d_qkv, d_og, mix_rows, mixed, got_b, sent_a
    )
    mix = Halving(bits, *halves)

    def last(d_qkv, d_og, w_a, w_b, d_rank, d_middle):
        input_grad, mixer_gain_grad = call(
            input_back_kernel,
            wides,
            [tile_pair(1024, WIDE), tile_pair(512, WIDE), keep(2, width, 768),
             keep(2, width, 768), tile(16, WIDE), keep(width, 16), tile(width, WIDE),
             tile(width, WIDE), keep(1, width)],
            [tile(width, WIDE), keep(1, width)],
            [shape((rows, width), BF16), shape((1, width), F32)],
            [],
            4 * rows * width * 1536,
            0,
        )(d_qkv, d_og, w_a, w_b, d_rank, low_first, hidden_in, d_middle, gain_a)
        block_out = call(
            feed_kernel,
            (2, wides),
            [part(cut), part(half - cut), part_weight(2), late_rows],
            late_rows,
            shape((rows, width), BF16),
            [pltpu.VMEM((wides, WIDE, width), F32)],
            4 * rows * width * half,
            0,
        )(activ_a, activ_b, w_rest, middle)
        return input_grad, mixer_gain_grad, block_out

    (input_grad, mixer_gain_grad, block_out), _ = in_flight(
        [mix, gate_up], last, d_qkv, d_og, w_in_a, w_in_b, d_rank, d_middle
    )
    own_gate, own_up = gate_up.finish()
    parts = (
        mixer_gain_grad, feed_gain_grad, low_first_grad, low_second_grad, bias_grad, head_gain_grad
    )
    small_sum = HopSum(jnp.concatenate([grad.reshape(-1, 128) for grad in parts]))
    in_flight([mix, small_sum], lambda: ())
    flat, _ = in_flight([mix], small_sum.finish)
    own_qkv, own_rest = mix.finish()

    small, spot = [], 0
    dims_of = ((width,), (width,), low_first.shape, low_second.shape, (512,), (VAL,))
    for part, dims in zip(parts, dims_of):
        size = part.size // 128
        small.append(flat[spot : spot + size].reshape(dims))
        spot += size
    return (
        block_out,
        input_grad,
        own_qkv[:, :256],
        own_qkv[:, 256:512],
        own_qkv[:, 512:],
        own_rest[:, :512],
        own_rest[:, 512:].T,
        own_gate,
        own_up,
        jnp.concatenate([part.T for part in own_down], axis=0),
        *small,
    )


def solution(mesh):
    tokens = P(("dp", "tensor"))
    split_in = P("dp", "tensor")
    split_out = P("tensor", "dp")
    weights = (split_in,) * 4 + (split_out,) + (split_in,) * 2 + (split_out,)
    in_specs = (tokens, P("dp", None), tokens) + weights + (P(),) * 6
    out_specs = (tokens, tokens) + weights + (P(),) * 6
    return jax.shard_map(local, mesh=mesh, in_specs=in_specs, out_specs=out_specs, check_vma=False)
```
